128 devices in a mesh: section: 4 (over y), chain: 8 (over z, x_lo), tp: 4 (over x_hi, core).
Axes of the slice: x: 4 (x_hi: 2, x_lo: 2; x = x_hi * 2 + x_lo), y: 4, z: 4, core: 2. Of those that a mesh axis runs over, the one named last changes fastest.
Arguments:
- block_input: bfloat16 [8, 64, 8192], P('chain', None, 'tp'), may hold values from -6 to 6
- norm_gain: bfloat16 [8192], replicated, may hold values from 0.099609375 to 1.8984375
- w_query: bfloat16 [8192, 4096], P(('section', 'chain'), 'tp'), may hold values from -0.0625 to 0.0625
- w_kv: bfloat16 [8192, 2048], P(('section', 'chain'), 'tp'), may hold values from -0.0625 to 0.0625
- w_out: bfloat16 [4096, 8192], P('tp', ('section', 'chain')), may hold values from -0.09375 to 0.09375
- kv_cache: bfloat16 [4, 8, 256, 16, 2048], P('section', 'chain', None, None, 'tp'), may hold values from -6 to 6
- page_table: int32 [8, 256], P('chain'), may hold values from 0 to 255, each once within a row
- prefix_len: int32 [8], P('chain'), may hold values from 1024 to 4096, as said below
- page_owner: int32 [8, 16, 1], P('chain', 'section'), may hold values from 0 to 3; in each aligned block of 4 rows (0 to 3, 4 to 7, ..., all dimensions but the last counted through in order) at most 2 rows name the same one
Outputs:
- block_output: bfloat16 [4, 8, 64, 8192], P('section', 'chain', None, 'tp')
- decode_pool: bfloat16 [4, 8, 8, 16, 2048], P('section', 'chain', None, None, 'tp')
The draws below stay inside these ranges and needn't reach their ends.
Inputs may be any that keep to these rules, and one draw needn't show every extreme that they name: `page_table`: each chain's table names every physical page once. `prefix_len`: some chain has a prefix of 4096 tokens. `page_owner`: among the 4 pages of one device, one owner is named at most 2 times.
All inputs are finite; a program needn't handle non-finite values.
Results may differ from the reference program's by a relative error of at most 0.02.
Values may be sent and summed in bfloat16 or wider, within the bound.
A program may use at most 128 MiB of HBM per device.

```python
import math
import jax
import jax.numpy as jnp
import numpy as np
from jax import lax

D = 8192
QH = 32
KVH = 8
HD = 128
SPAN = 32
PAGE = 16
SPANS = 2
PREFIX = 4096
NEW = 64
PREFIX_PAGES = 256
NEW_PAGES = 4
MOST = 2
N_SECTION = 4
N_CHAIN = 8
N_TP = 4


def draw_prefix_len(key, part):
    key = jax.random.fold_in(key, 7)
    first_key, second_key = jax.random.split(key)
    lengths = jax.random.randint(first_key, (N_CHAIN,), PREFIX // 4, PREFIX + 1)
    longest = jax.random.randint(second_key, (), 0, N_CHAIN)
    return lengths.at[longest].set(PREFIX).astype(jnp.int32)


def block_levels(rng, dims, shards, low, high):
    gain, own = 1.0, jax.random.fold_in(rng, 6)
    for dim, shards_of in shards:
        draws = jnp.exp(jax.random.uniform(jax.random.fold_in(own, dim), (shards_of,), jnp.float32, low / len(shards), high / len(shards)))
        gain = gain * jnp.repeat(draws, dims[dim] // shards_of).reshape([-1 if axis == dim else 1 for axis in range(len(dims))])
    return gain


def shared_out(own_key, own, number, rows, count, top, most, lean):
    ranking = jax.random.permutation(own_key, count)
    crowded, ordinary = portions_of(count, rows * top, most, lean, True), portions_of(count, rows * top, most, lean, False)
    places = jnp.arange(count)

    def named(sizes, rotation):
        used = int((sizes > 0).sum())
        fixed = max(1, used // 4)
        passed = fixed + (places - fixed + rotation * (used - fixed)) % max(1, count - fixed)
        return jnp.zeros((count,), jnp.int32).at[ranking[jnp.where(places < fixed, places, passed)]].set(jnp.asarray(sizes, jnp.int32))

    sizes = jnp.where(number % 4 == 0, named(crowded, number // 4), named(ordinary, number - number // 4 - 1))
    mixed = jax.random.permutation(jax.random.fold_in(own, 3), count)
    giver, sink = mixed[0:count // 2 * 2:2], mixed[1:count // 2 * 2:2]
    slack = jnp.minimum(sizes[giver] - 1, most - sizes[sink]) // 2
    slack = jnp.where((giver == ranking[0]) | (sink == ranking[0]) | (sizes[sink] == 0), 0, jnp.maximum(slack, 0))
    passed = jax.random.randint(jax.random.fold_in(own, 4), (count // 2,), 0, 1 << 20) % (slack + 1)
    sizes = sizes.at[giver].add(-passed).at[sink].add(passed)
    items = jnp.searchsorted(jnp.cumsum(sizes), jnp.arange(rows * top), side="right").astype(jnp.int32)
    grid = items.reshape(top, rows).T
    grid = grid[jax.random.permutation(jax.random.fold_in(own, 1), rows)]
    rotation = jax.random.randint(jax.random.fold_in(own, 2), (rows, 1), 0, top)
    return jnp.take_along_axis(grid, (jnp.arange(top)[None, :] + rotation) % top, axis=1)


def portions_of(amount, total, reach, slope, full):
    loads = [(1 << 20) // math.isqrt(rank ** slope) + 1 for rank in range(1, amount + 1)]
    largest = reach if full else min(reach, max(-(-total // amount), total * loads[0] // sum(loads)))
    least = 1 if total - largest >= amount - 1 else 0
    holding, surplus = [largest] + [least] * (amount - 1), total - largest - least * (amount - 1)
    while surplus > 0:
        movable = [i for i in range(1, amount) if holding[i] < largest] or [i for i in range(1, amount) if holding[i] < reach]
        pool, left = sum([loads[i] for i in movable]), surplus
        for i in movable:
            addition = min(reach - holding[i], max(1, left * loads[i] // pool), surplus)
            holding[i] = holding[i] + addition
            surplus = surplus - addition
    return np.array(holding)


def noise(own_key, shape, scale, limit, cuts=(), kind=jnp.bfloat16):
    drawn = scale * jax.random.normal(own_key, shape, jnp.float32)
    if cuts:
        drawn = drawn * block_levels(own_key, shape, cuts, -0.22, 0.18)
    return jnp.clip(drawn, -limit, limit).astype(kind)


def setup_inputs(seed: int = 0) -> dict:
    splits = jax.random.split(jax.random.key(seed), 10)
    block_input = noise(splits[0], (N_CHAIN, NEW, D), 1.0, 6.0, ((0, 8), (2, 4)))
    norm_gain = jnp.clip(1.0 + 0.18 * jax.random.normal(splits[1], (D,), jnp.float32), 0.099609375, 1.8984375).astype(jnp.bfloat16)
    w_query = noise(splits[2], (D, QH * HD), D ** -0.5, 0.0625, ((0, 32), (1, 4)))
    w_kv = noise(splits[3], (D, 2 * KVH * HD), D ** -0.5, 0.0625, ((0, 32), (1, 4)))
    w_out = noise(splits[4], (QH * HD, D), (QH * HD) ** -0.5, 0.09375, ((0, 4), (1, 32)))
    kv_cache = noise(splits[5], (N_SECTION, N_CHAIN, PREFIX_PAGES, PAGE, 2 * KVH * HD), 1.0, 6.0, ((0, 4), (1, 8), (4, 4)))
    page_table = jax.vmap(lambda own: jax.random.permutation(own, PREFIX_PAGES))(jax.random.split(splits[6], N_CHAIN)).reshape((N_CHAIN, PREFIX_PAGES)).astype(jnp.int32)
    prefix_len = draw_prefix_len(jax.random.fold_in(splits[9], 71), 0)
    page_owner_keys = jax.random.split(jax.random.fold_in(splits[8], 1), N_CHAIN * (N_SECTION * NEW_PAGES) // NEW_PAGES)
    page_owner_turns = jax.random.permutation(jax.random.fold_in(splits[8], 3), N_CHAIN * (N_SECTION * NEW_PAGES) // NEW_PAGES)
    page_owner = jax.vmap(lambda own, number: shared_out(jax.random.fold_in(splits[8], 2), own, number, NEW_PAGES, N_SECTION, 1, MOST, 2))(page_owner_keys, page_owner_turns).reshape((N_CHAIN, N_SECTION * NEW_PAGES, 1))
    return dict(block_input=block_input, norm_gain=norm_gain, w_query=w_query, w_kv=w_kv, w_out=w_out, kv_cache=kv_cache, page_table=page_table, prefix_len=prefix_len, page_owner=page_owner)


def rotate(values, positions):
    half_width = values.shape[-1] // 2
    inverse = 500000.0 ** (-(jnp.arange(half_width, dtype=jnp.float32) * 2.0 / values.shape[-1]))
    angles = positions[:, None] * inverse[None, :]
    cosine = jnp.cos(angles)[:, None, :]
    sine_of = jnp.sin(angles)[:, None, :]
    leading = values[..., :half_width]
    trailing = values[..., half_width:]
    return jnp.concatenate([leading * cosine - trailing * sine_of, trailing * cosine + leading * sine_of], axis=-1)

def normalize(hidden, norm_gain):
    widened = hidden.astype(jnp.float32)
    scaled = widened * lax.rsqrt(lax.optimization_barrier(jnp.mean(widened * widened, axis=-1, keepdims=True)) + 1e-05)
    return (scaled * norm_gain.astype(jnp.float32)).astype(jnp.bfloat16)

def attend(queries, keys_all, values_all, allowed, scale_factor):
    scores = jnp.einsum('rhgd,khd->hgrk', queries.astype(jnp.float32), keys_all.astype(jnp.float32)) * scale_factor
    scores = jnp.where(allowed[None, None], scores, -1e+30)
    row_peak = lax.optimization_barrier(jnp.max(scores, axis=-1, keepdims=True))
    raised = jnp.exp(scores - row_peak)
    row_total = lax.optimization_barrier(jnp.sum(raised, axis=-1, keepdims=True))
    weights = (raised / row_total).astype(jnp.bfloat16)
    mixed_rows = jnp.einsum('hgrk,khd->rhgd', weights.astype(jnp.float32), values_all.astype(jnp.float32))
    return mixed_rows.astype(jnp.bfloat16)

def reference(block_input, norm_gain, w_query, w_kv, w_out, kv_cache, page_table, prefix_len, page_owner):
    group_size = QH // KVH
    scale_factor = 1.0 / math.sqrt(HD)
    new_rows = SPANS * SPAN
    page_count = new_rows // PAGE
    most_pages = max(2, (page_count + N_SECTION - 1) // N_SECTION)
    kv_width = KVH * 2 * HD
    head_cols = QH * HD // N_TP
    row_ids = jnp.arange(new_rows)
    key_ids = jnp.arange(PREFIX + new_rows)
    page_ids = jnp.arange(page_count)
    slot_range = jnp.arange(N_SECTION * most_pages)
    section_rows = [[None] * N_CHAIN for section_id in range(N_SECTION)]
    outgoing = [[None] * N_CHAIN for section_id in range(N_SECTION)]
    for chain_id in range(N_CHAIN):
        hidden = block_input[chain_id]
        length = prefix_len[chain_id]
        positions = (length + row_ids).astype(jnp.float32)
        allowed = jnp.where(key_ids[None, :] < PREFIX, key_ids[None, :] < length, key_ids[None, :] - PREFIX <= row_ids[:, None])
        for section_id in range(N_SECTION):
            cached = kv_cache[section_id, chain_id][page_table[chain_id]].reshape(PREFIX, KVH, 2, HD)
            normed = normalize(hidden, norm_gain)
            queries = jnp.dot(normed, w_query, preferred_element_type=jnp.float32).reshape(new_rows, QH, HD)
            queries = rotate(queries, positions).astype(jnp.bfloat16).reshape(new_rows, KVH, group_size, HD)
            projected = jnp.dot(normed, w_kv, preferred_element_type=jnp.float32).reshape(new_rows, KVH, 2, HD)
            fresh_keys = rotate(projected[:, :, 0], positions).astype(jnp.bfloat16)
            fresh_values = projected[:, :, 1].astype(jnp.bfloat16)
            keys_all = jnp.concatenate([cached[:, :, 0], fresh_keys], axis=0)
            values_all = jnp.concatenate([cached[:, :, 1], fresh_values], axis=0)
            mixed_rows = attend(queries, keys_all, values_all, allowed, scale_factor).reshape(new_rows, QH * HD)
            summed = jnp.zeros((new_rows, D), jnp.float32)
            for tp_id in range(N_TP):
                piece = jnp.dot(mixed_rows[:, tp_id * head_cols:(tp_id + 1) * head_cols], w_out[tp_id * head_cols:(tp_id + 1) * head_cols], preferred_element_type=jnp.float32)
                summed = summed + lax.optimization_barrier(piece.astype(jnp.bfloat16)).astype(jnp.float32)
            hidden = (hidden.astype(jnp.float32) + summed).astype(jnp.bfloat16)
            section_rows[section_id][chain_id] = hidden
            fresh_rows = jnp.stack([fresh_keys, fresh_values], axis=2).reshape(page_count, PAGE * kv_width)
            owners = page_owner[chain_id, section_id * page_count:(section_id + 1) * page_count, 0]
            earlier = (owners[:, None] == owners[None, :]) & (page_ids[None, :] < page_ids[:, None])
            page_ranks = lax.optimization_barrier(jnp.sum(earlier.astype(jnp.int32), axis=1)).astype(jnp.int32)
            slot_ids = owners * most_pages + page_ranks
            selection = (slot_ids[None, :] == slot_range[:, None]).astype(jnp.bfloat16)
            placed = jnp.dot(selection, fresh_rows, preferred_element_type=jnp.float32).astype(jnp.bfloat16)
            outgoing[section_id][chain_id] = placed.reshape(N_SECTION, most_pages, PAGE, kv_width)
    block_output = jnp.stack([jnp.stack(section_rows[section_id]) for section_id in range(N_SECTION)])
    decode_pool = jnp.stack([jnp.stack([jnp.concatenate([outgoing[section_id][chain_id][owner_id] for section_id in range(N_SECTION)], axis=0) for chain_id in range(N_CHAIN)]) for owner_id in range(N_SECTION)])
    return (block_output, decode_pool)
```

```python
import math

import jax
import jax.numpy as jnp
from jax import lax
from jax.experimental import pallas as pl
from jax.experimental.pallas import tpu as pltpu
from jax.sharding import PartitionSpec as P

HD = 128
PAGE = 16
PREFIX = 4096
NEW = 64
WIDTH = 8192
NSEC = 4
NCH = 8
NTP = 4
QC = 256
PC = 384
CH = 512
NCHUNK = PREFIX // CH
STREAMS = ((0, 32), (32, 32))
NS = len(STREAMS)
R = STREAMS[0][1]
MESH = pl.DeviceIdType.MESH
BF = jnp.bfloat16
F32 = jnp.float32


def kernel(
    hin, wsend, wo, cache, bias, cosd, sind, sel,
    bout, pool,
    cachev, wq_l, wo_l, h0, hA, part1, rbuf, ssend, srecv, sbuf2, qbuf, kvnew, S, msend, mixb, osend, ob, placed, obuf, pbuf,
    csem, h0s, h0r, h2s, h2r, wqs, wqr, wos, wor,
    s1, r1, ss_s, ss_r, s2, r2, s3, r3, s4, r4, s5, r5, s6, r6, s7, r7, s7f, r7f, so, ro, ps, pr,
):
    y = lax.axis_index("section")
    c = lax.axis_index("chain")
    t = lax.axis_index("tp")
    u = t // 2
    k = t % 2
    own = 2 * y + u
    twin = (y, c, 2 * u + 1 - k)

    def remote(src, dst, ssem, rsem, dev):
        return pltpu.make_async_remote_copy(
            src_ref=src, dst_ref=dst, send_sem=ssem, recv_sem=rsem, device_id=dev, device_id_type=MESH
        )

    def got(dst, rsem):
        pltpu.make_async_copy(dst, dst, rsem).wait()

    barrier = pltpu.get_barrier_semaphore()
    for d in range(1, NCH):
        pl.semaphore_signal(barrier, inc=1, device_id=(y, (c + d) % NCH, t), device_id_type=MESH)
    for dy in range(NSEC):
        for dt in range(NTP):
            if dy or dt:
                pl.semaphore_signal(
                    barrier, inc=1, device_id=((y + dy) % NSEC, c, (t + dt) % NTP), device_id_type=MESH
                )
    pl.semaphore_wait(barrier, NCH - 1 + NSEC * NTP - 1)

    def first_hop(d):
        peer = (c + d) % NCH
        src = hin.at[:, pl.ds(pl.multiple_of(peer * QC, QC), QC)]
        return lambda: remote(src, h0.at[c % 2], h0s.at[d], h0r.at[c % 2], (y, peer, t)), src

    @pl.when(c // 2 == y)
    def _():
        for d in range(1, NCH):
            first_hop(d)[0]().start()
        pltpu.make_async_copy(first_hop(0)[1], h0.at[c % 2], h0r.at[c % 2]).start()

    def wq_copy(d):
        peer = (y + d) % NSEC
        return remote(wsend.at[peer], wq_l.at[y], wqs.at[d], wqr.at[y], (peer, c, t))

    for d in range(1, NSEC):
        wq_copy(d).start()
    pltpu.make_async_copy(wsend.at[y], wq_l.at[y], wqr.at[y]).start()

    def wo_copy(d):
        peer = (y + d) % NSEC
        src = wo.at[pl.ds(pl.multiple_of(peer * QC, QC), QC), :]
        return lambda: remote(src, wo_l.at[k, y % 2], wos.at[d], wor.at[k, y % 2], (peer, c, 2 * u + y // 2)), src

    cache_copy = pltpu.make_async_copy(cache, cachev, csem)

    def second_hop(j, st):
        r0 = STREAMS[st][0]
        src = h0.at[j, pl.ds(r0, R), :]
        dst = hA.at[st, t // 2, 2 * y + j, :, pl.ds(pl.multiple_of((t % 2) * QC, QC), QC)]
        rsem = h2r.at[st, t % 2]
        return lambda: remote(src, dst, h2s.at[st, j], rsem, (y, c, 2 * j + t // 2)), src, dst, rsem

    for j in range(2):
        got(h0.at[j], h0r.at[j])
    for st in range(NS):
        for j in range(2):
            mine = (j == u) & (k == t // 2)

            @pl.when(mine)
            def _():
                _, src, dst, rsem = second_hop(j, st)
                pltpu.make_async_copy(src, dst, rsem).start()

            @pl.when(jnp.logical_not(mine))
            def _():
                second_hop(j, st)[0]().start()

    def ag_copy(st, e):
        g = (own + e) % 8
        piece = hA.at[st, k, own]
        return remote(piece, piece, s7.at[st, e], r7.at[st, own], (g // 2, c, 2 * (g % 2) + k))

    def twin_copy(st, e):
        g = (own + 8 - e) % 8
        piece = hA.at[st, k, g]
        return remote(piece, piece, s7f.at[st, e], r7f.at[st, g], twin)

    def ag_send(st):
        for e in range(1, 8):
            ag_copy(st, e).start()
        twin_copy(st, 0).start()

    def ag_forward(st):
        for e in range(1, 8):
            g = (own + 8 - e) % 8
            got(hA.at[st, k, g], r7.at[st, g])
            twin_copy(st, e).start()

    def ag_wait(st):
        for e in range(8):
            g = (own + 8 - e) % 8
            got(hA.at[st, 1 - k, g], r7f.at[st, g])

    def ag_sent(st):
        for e in range(1, 8):
            ag_copy(st, e).wait_send()
        for e in range(8):
            twin_copy(st, e).wait_send()

    for st in range(NS):
        for a in range(2):
            got(hA.at[st, k, own, :, pl.ds(a * QC, QC)], h2r.at[st, a])
        ag_send(st)

    for d in range(NSEC):
        if d:
            wo_copy(d)[0]().start()
        else:
            @pl.when(k == y // 2)
            def _():
                pltpu.make_async_copy(wo_copy(0)[1], wo_l.at[k, y % 2], wor.at[k, y % 2]).start()

            @pl.when(k != y // 2)
            def _():
                wo_copy(0)[0]().start()
    cache_copy.start()

    @pl.when(c // 2 == y)
    def _():
        for d in range(1, NCH):
            first_hop(d)[0]().wait_send()

    for st in range(NS):
        for j in range(2):
            mine = (j == u) & (k == t // 2)

            @pl.when(jnp.logical_not(mine))
            def _():
                second_hop(j, st)[0]().wait_send()

    for st in range(NS):
        ag_forward(st)
    for d in range(NSEC):
        got(wq_l.at[d], wqr.at[d])
    for d in range(1, NSEC):
        wq_copy(d).wait_send()
    for st in range(NS):
        ag_wait(st)
    for a in range(2):
        for b in range(2):
            got(wo_l.at[a, b], wor.at[a, b])
    for d in range(NSEC):
        if d:
            wo_copy(d)[0]().wait_send()
        else:
            @pl.when(k != y // 2)
            def _():
                wo_copy(0)[0]().wait_send()
    cache_copy.wait()

    def p1_copy(st, d):
        peer = (c + d) % NCH
        return remote(part1.at[st, peer], rbuf.at[st, c], s1.at[st, d], r1.at[st, c], (y, peer, t))

    def ss_copy(st, d):
        peer = (c + d) % NCH
        return remote(ssend.at[st, peer], srecv.at[st, c], ss_s.at[st, d], ss_r.at[st, c], (y, peer, t))

    def project(st):
        total = None
        for half in range(2):
            x = hA[st, half].reshape(NCH * R, 512)
            w = wq_l[pl.ds(2 * half, 2)].reshape(512, PC)
            term = jnp.dot(x, w, preferred_element_type=F32)
            total = term if total is None else total + term
        part1[st] = total.astype(BF).reshape(NCH, R, PC)
        for d in range(1, NCH):
            p1_copy(st, d).start()
        ones = jnp.ones((8, 128), BF)
        for g in range(NCH):
            acc = None
            for half in range(2):
                wide = hA[st, half, g].astype(F32)
                square = wide * wide
                for a in range(4):
                    piece = square[:, a * 128:(a + 1) * 128]
                    acc = piece if acc is None else acc + piece
            high = acc.astype(BF)
            low = (acc - high.astype(F32)).astype(BF)
            dims = (((1,), (1,)), ((), ()))
            row = lax.dot_general(ones, high, dims, preferred_element_type=F32)
            row = row + lax.dot_general(ones, low, dims, preferred_element_type=F32)
            ssend[st, g] = jnp.concatenate([row, jnp.zeros((8, 128 - R), F32)], axis=1)
        for d in range(1, NCH):
            ss_copy(st, d).start()
        rbuf[st, c] = part1[st, c]
        srecv[st, c] = ssend[st, c]

    def p2_copy(st, s):
        return remote(sbuf2.at[st], qbuf.at[st, y], s2.at[st], r2.at[st, y], (s, c, t))

    def finish_projection(st, s):
        r0 = STREAMS[st][0]
        for d in range(1, NCH):
            g = (c + NCH - d) % NCH
            got(rbuf.at[st, g], r1.at[st, g])
            got(srecv.at[st, g], ss_r.at[st, g])
        total = rbuf[st, 0].astype(F32)
        squares = srecv[st, 0]
        for g in range(1, NCH):
            total = total + rbuf[st, g].astype(F32)
            squares = squares + srecv[st, g]
        inv = lax.rsqrt(squares * (1.0 / WIDTH) + 1e-05)[0:1, :R]
        eye = lax.broadcasted_iota(jnp.int32, (R, R), 0) == lax.broadcasted_iota(jnp.int32, (R, R), 1)
        scale = jnp.sum(jnp.where(eye, inv, 0.0), axis=1, keepdims=True)
        total = total * scale
        cs = cosd[r0:r0 + R, :]
        sn = sind[r0:r0 + R, :]
        to_score = math.log2(math.e) / math.sqrt(HD)

        def rope(v):
            return v * cs + pltpu.roll(v, 64, 1) * sn

        q0 = rope(total[:, 0:128]) * to_score
        q1 = rope(total[:, 128:256]) * to_score
        kv = total[:, 256:384]
        even = (y % 2 == 0).astype(F32)
        kv = rope(kv) * even + kv * (1.0 - even)
        sbuf2[st] = jnp.concatenate([q0, q1, kv], axis=1).astype(BF)

        @pl.when(y == s)
        def _():
            qbuf[st, y] = sbuf2[st]

        @pl.when(y != s)
        def _():
            p2_copy(st, s).start()

        for d in range(1, NCH):
            p1_copy(st, d).wait_send()
            ss_copy(st, d).wait_send()
        ag_sent(st)

        @pl.when((s > 0) & (y == s - 1))
        def _():
            bout_sent(st)

    def p3_copy(st, d):
        peer = (y + d) % NSEC
        return remote(msend.at[st, peer], mixb.at[st, k, c], s3.at[st, d], r3.at[st], (peer, c, t))

    def pool_copy(d):
        peer = (y + d) % NSEC
        return remote(placed.at[peer], pbuf.at[y], ps.at[d], pr.at[y], (peer, c, t))

    def attend(st):
        r0 = STREAMS[st][0]
        seen = r0 + R
        for d in range(1, NSEC):
            g = (y + d) % NSEC
            got(qbuf.at[st, g], r2.at[st, g])
        for g in range(NSEC):
            kvnew[r0:r0 + R, g * 128:(g + 1) * 128] = qbuf[st, g, :, QC:PC]
        dims = (((1,), (1,)), ((), ()))
        for j in range(2):
            q = jnp.concatenate(
                [qbuf[st, 2 * j + hh // 2, :, (hh % 2) * 128:(hh % 2 + 1) * 128] for hh in range(4)], axis=0
            )
            kcol = j * 256
            vcol = j * 256 + 128
            sf = lax.dot_general(q, kvnew[0:seen, kcol:kcol + 128], dims, preferred_element_type=F32)
            row = lax.broadcasted_iota(jnp.int32, (4, R, seen), 1).reshape(4 * R, seen) + r0
            col = lax.broadcasted_iota(jnp.int32, (4 * R, seen), 1)
            sf = jnp.where(col <= row, sf, -1e30)

            def scores(i, peak):
                keys = cachev[pl.ds(pl.multiple_of(i * CH, CH), CH), kcol:kcol + 128]
                sc = lax.dot_general(q, keys, dims, preferred_element_type=F32) + bias[pl.ds(i, 1), :]
                S[i] = sc
                for a in range(CH // 128):
                    peak = jnp.maximum(peak, sc[:, a * 128:(a + 1) * 128])
                return peak

            peak = lax.fori_loop(0, NCHUNK, scores, jnp.full((4 * R, 128), -1e30, F32))
            top = jnp.maximum(jnp.max(peak, axis=1, keepdims=True), jnp.max(sf, axis=1, keepdims=True))

            pf = jnp.exp2(sf - top)
            acc0 = jnp.dot(pf.astype(BF), kvnew[0:seen, vcol:vcol + 128], preferred_element_type=F32)

            def weigh(i, carry):
                acc, den = carry
                p = jnp.exp2(S[i] - top)
                for a in range(CH // 128):
                    den = den + p[:, a * 128:(a + 1) * 128]
                values = cachev[pl.ds(pl.multiple_of(i * CH, CH), CH), vcol:vcol + 128]
                return acc + jnp.dot(p.astype(BF), values, preferred_element_type=F32), den

            acc, den = lax.fori_loop(0, NCHUNK, weigh, (acc0, jnp.zeros((4 * R, 128), F32)))
            den = jnp.sum(den, axis=1, keepdims=True) + jnp.sum(pf, axis=1, keepdims=True)
            mixed = (acc / den).astype(BF)
            for hh in range(4):
                msend[st, 2 * j + hh // 2, :, (hh % 2) * 128:(hh % 2 + 1) * 128] = mixed[hh * R:(hh + 1) * R]
        for d in range(1, NSEC):
            p3_copy(st, d).start()
        mixb[st, k, c] = msend[st, y]

    def place_pages():
        for slot in range(2 * NSEC):
            acc = None
            for q in range(NEW // PAGE):
                term = kvnew[q * PAGE:(q + 1) * PAGE, :].astype(F32) * sel[slot, q]
                acc = term if acc is None else acc + term
            placed[slot // 2, (slot % 2) * PAGE:(slot % 2 + 1) * PAGE, :] = acc.astype(BF)
        for d in range(1, NSEC):
            pool_copy(d).start()
        pbuf[y] = placed[y]

    def mix(st, s):
        @pl.when(y == s)
        def _():
            attend(st)
            if st == NS - 1:
                place_pages()

        @pl.when(y != s)
        def _():
            p2_copy(st, s).wait_send()

    def p4_copy(st, d):
        peer = (c + d) % NCH
        piece = mixb.at[st, k, c]
        return remote(piece, piece, s4.at[st, d], r4.at[st, c], (y, peer, t))

    def p5_copy(st, d):
        g = (c + NCH - d) % NCH
        piece = mixb.at[st, k, g]
        return remote(piece, piece, s5.at[st, d], r5.at[st, g], twin)

    def spread(st, s):
        @pl.when(y != s)
        def _():
            got(mixb.at[st, k, c], r3.at[st])

        for d in range(1, NCH):
            p4_copy(st, d).start()
        p5_copy(st, 0).start()

    def spread_twin(st):
        for d in range(1, NCH):
            g = (c + NCH - d) % NCH
            got(mixb.at[st, k, g], r4.at[st, g])
            p5_copy(st, d).start()

    def p6_copy(st, e):
        g = (own + e) % 8
        return remote(osend.at[st, g], ob.at[st, own], s6.at[st, e], r6.at[st, own], (g // 2, c, 2 * (g % 2) + k))

    def bout_copy(st, d):
        r0 = STREAMS[st][0]
        peer = (c + d) % NCH
        src = hA.at[st, t // 2, peer, :, pl.ds(pl.multiple_of((t % 2) * QC, QC), QC)]
        dst = obuf.at[c, pl.ds(r0, R), :]
        return lambda: remote(src, dst, so.at[st, d], ro.at[st, c], (y, peer, t)), src, dst

    def bout_sent(st):
        for d in range(1, NCH):
            bout_copy(st, d)[0]().wait_send()
        got(bout_copy(st, 0)[2], so.at[st, 0])

    def output_projection(st, s):
        for d in range(NCH):
            g = (c + NCH - d) % NCH
            got(mixb.at[st, 1 - k, g], r5.at[st, g])
        for b in range(2):
            total = None
            for a in range(2):
                x = mixb[st, a].reshape(NCH * R, QC)
                term = jnp.dot(x, wo_l[a, b], preferred_element_type=F32)
                total = term if total is None else total + term
            osend[st, :, :, b * QC:(b + 1) * QC] = total.astype(BF).reshape(NCH, R, QC)

        for d in range(1, NCH):
            p4_copy(st, d).wait_send()
        for d in range(NCH):
            p5_copy(st, d).wait_send()

        @pl.when(y == s)
        def _():
            for d in range(1, NSEC):
                p3_copy(st, d).wait_send()

        for e in range(1, 8):
            p6_copy(st, e).start()
        ob[st, own] = osend[st, own]

    def residual(st):
        for e in range(1, 8):
            g = (own + 8 - e) % 8
            got(ob.at[st, g], r6.at[st, g])
        total = ob[st, 0].astype(F32)
        for g in range(1, 8):
            total = total + ob[st, g].astype(F32)
        hA[st, k, own] = (hA[st, k, own].astype(F32) + total).astype(BF)
        ag_send(st)
        for e in range(1, 8):
            p6_copy(st, e).wait_send()

    def put_out(st, s):
        @pl.when(y == s)
        def _():
            for d in range(1, NCH):
                bout_copy(st, d)[0]().start()
            _, src, dst = bout_copy(st, 0)
            pltpu.make_async_copy(src, dst, so.at[st, 0]).start()

    def section_step(s, carry):
        for st in range(NS):
            project(st)
        for st in range(NS):
            finish_projection(st, s)
        for st in range(NS):
            mix(st, s)
            spread(st, s)
        for st in range(NS):
            spread_twin(st)
        for st in range(NS):
            output_projection(st, s)
        for st in range(NS):
            residual(st)
        for st in range(NS):
            ag_forward(st)
        for st in range(NS):
            ag_wait(st)
            put_out(st, s)
        return carry

    lax.fori_loop(0, NSEC, section_step, 0)

    for st in range(NS):
        ag_sent(st)

        @pl.when(y == NSEC - 1)
        def _():
            bout_sent(st)

        for d in range(1, NCH):
            g = (c + NCH - d) % NCH
            got(obuf.at[g, pl.ds(STREAMS[st][0], R), :], ro.at[st, g])
    for d in range(1, NSEC):
        g = (y + NSEC - d) % NSEC
        got(pbuf.at[g], pr.at[g])
        pool_copy(d).wait_send()
    for g in range(NCH):
        bout[:, g * QC:(g + 1) * QC] = obuf[g]
    for g in range(NSEC):
        pool[g] = pbuf[g]


def local(block_input, norm_gain, w_query, w_kv, w_out, kv_cache, page_table, prefix_len, page_owner):
    y = lax.axis_index("section")
    c = lax.axis_index("chain")
    length = prefix_len[0]
    rows = w_query.shape[0]
    gain = lax.dynamic_slice_in_dim(norm_gain, (y * NCH + c) * rows, rows, 0).astype(F32)[:, None]
    wq = (w_query.astype(F32) * gain).astype(BF).reshape(rows, NSEC, QC)
    wkv = (w_kv.astype(F32) * gain).astype(BF).reshape(rows, NSEC, PC - QC)
    wsend = jnp.concatenate([wq, wkv], axis=-1).transpose(1, 0, 2)

    pages = PREFIX // PAGE
    ids = jnp.arange(pages, dtype=jnp.int32)
    logical = jnp.sum(jnp.where(page_table[0][None, :] == ids[:, None], ids[None, :], 0), axis=1)
    place = logical[:, None] * PAGE + jnp.arange(PAGE, dtype=jnp.int32)[None, :]
    bias = jnp.where(place < length, 0.0, -1e30).astype(F32).reshape(NCHUNK, CH)

    inverse = 500000.0 ** (-(jnp.arange(HD // 2, dtype=F32) * 2.0 / HD))
    angles = (length + jnp.arange(NEW)).astype(F32)[:, None] * inverse[None, :]
    cosine, sine = jnp.cos(angles), jnp.sin(angles)
    cosd = jnp.concatenate([cosine, cosine], axis=1)
    sind = jnp.concatenate([-sine, sine], axis=1)

    owners = page_owner[0, :, 0]
    q = jnp.arange(NEW // PAGE)
    earlier = (owners[:, None] == owners[None, :]) & (q[None, :] < q[:, None])
    slots = owners * 2 + jnp.sum(earlier.astype(jnp.int32), axis=1)
    sel = (slots[None, :] == jnp.arange(2 * NSEC)[:, None]).astype(F32)

    vm = pl.BlockSpec(memory_space=pltpu.VMEM)
    dma = pltpu.SemaphoreType.DMA
    V = pltpu.VMEM
    bout, pool = pl.pallas_call(
        kernel,
        out_shape=(
            jax.ShapeDtypeStruct((NEW, WIDTH // NTP), BF),
            jax.ShapeDtypeStruct((NSEC, 2 * PAGE, 512), BF),
        ),
        in_specs=[vm, vm, vm, pl.BlockSpec(memory_space=pl.ANY), vm, vm, vm, pl.BlockSpec(memory_space=pltpu.SMEM)],
        out_specs=(vm, vm),
        scratch_shapes=[
            V((PREFIX, 512), BF),
            V((NSEC, 256, PC), BF),
            V((2, 2, 256, 256), BF),
            V((2, NEW, QC), BF),
            V((NS, 2, NCH, R, 512), BF),
            V((NS, NCH, R, PC), BF),
            V((NS, NCH, R, PC), BF),
            V((NS, NCH, 8, 128), F32),
            V((NS, NCH, 8, 128), F32),
            V((NS, R, PC), BF),
            V((NS, NSEC, R, PC), BF),
            V((NEW, 512), BF),
            V((NCHUNK, 4 * R, CH), F32),
            V((NS, NSEC, R, QC), BF),
            V((NS, 2, NCH, R, QC), BF),
            V((NS, NCH, R, 512), BF),
            V((NS, NCH, R, 512), BF),
            V((NSEC, 2 * PAGE, 512), BF),
            V((NCH, NEW, QC), BF),
            V((NSEC, 2 * PAGE, 512), BF),
            dma(()),
            dma((NCH,)), dma((2,)),
            dma((NS, 2)), dma((NS, 2)),
            dma((NSEC,)), dma((NSEC,)),
            dma((NSEC,)), dma((2, 2)),
            dma((NS, NCH)), dma((NS, NCH)),
            dma((NS, NCH)), dma((NS, NCH)),
            dma((NS,)), dma((NS, NSEC)),
            dma((NS, NSEC)), dma((NS,)),
            dma((NS, NCH)), dma((NS, NCH)),
            dma((NS, NCH)), dma((NS, NCH)),
            dma((NS, 8)), dma((NS, 8)),
            dma((NS, 8)), dma((NS, 8)),
            dma((NS, 8)), dma((NS, 8)),
            dma((NS, NCH)), dma((NS, NCH)),
            dma((NSEC,)), dma((NSEC,)),
        ],
        compiler_params=pltpu.CompilerParams(
            collective_id=0, has_side_effects=True, vmem_limit_bytes=48 * 1024 * 1024
        ),
    )(block_input[0], wsend, w_out, kv_cache.reshape(PREFIX, 512), bias, cosd, sind, sel)
    return bout[None, None], pool.reshape(1, 1, 2 * NSEC, PAGE, 512)


def solution(mesh):
    in_specs = (
        P("chain", None, "tp"),
        P(),
        P(("section", "chain"), "tp"),
        P(("section", "chain"), "tp"),
        P("tp", ("section", "chain")),
        P("section", "chain", None, None, "tp"),
        P("chain", None),
        P("chain"),
        P("chain", "section", None),
    )
    out_specs = (P("section", "chain", None, "tp"), P("section", "chain", None, None, "tp"))
    return jax.shard_map(local, mesh=mesh, in_specs=in_specs, out_specs=out_specs, check_vma=False)
```

```python
import math

import jax
import jax.numpy as jnp
from jax import lax
from jax.experimental import pallas as pl
from jax.experimental.pallas import tpu as pltpu
from jax.sharding import PartitionSpec as P

HD = 128
PAGE = 16
PREFIX = 4096
NEW = 64
WIDTH = 8192
NSEC = 4
NCH = 8
NTP = 4
QC = 256
PC = 384
CH = 512
NCHUNK = PREFIX // CH
STREAMS = ((0, 32), (32, 32))
NS = len(STREAMS)
SKEW = 0
R = STREAMS[0][1]
MESH = pl.DeviceIdType.MESH
BF = jnp.bfloat16
F32 = jnp.float32


def kernel(
    hin, wq, wkv, wo, gain, cache, bias, table, sel,
    bout, pool,
    cachev, wq_l, wo_l, hA, part1, rbuf, ssend, srecv, sbuf2, qbuf, kvnew, S, msend, mixb, osend, ob, placed, obuf, pbuf,
    csem, h0s, h0r, h2s, h2r, wqs, wqr, wks, wkr, wos, wor,
    s1, r1, ss_s, ss_r, s2, r2, s3, r3, s4, r4, s5, r5, s6, r6, s7, r7, s7f, r7f, so, ro, ps, pr,
):
    y = lax.axis_index("section")
    c = lax.axis_index("chain")
    t = lax.axis_index("tp")
    u = t // 2
    k = t % 2
    own = 2 * y + u
    twin = (y, c, 2 * u + 1 - k)

    def remote(src, dst, ssem, rsem, dev):
        return pltpu.make_async_remote_copy(
            src_ref=src, dst_ref=dst, send_sem=ssem, recv_sem=rsem, device_id=dev, device_id_type=MESH
        )

    def got(dst, rsem):
        pltpu.make_async_copy(dst, dst, rsem).wait()

    barrier = pltpu.get_barrier_semaphore()
    for d in range(1, NCH):
        pl.semaphore_signal(barrier, inc=1, device_id=(y, (c + d) % NCH, t), device_id_type=MESH)
    for dy in range(NSEC):
        for dt in range(NTP):
            if dy or dt:
                pl.semaphore_signal(
                    barrier, inc=1, device_id=((y + dy) % NSEC, c, (t + dt) % NTP), device_id_type=MESH
                )
    for g in range(NCH):
        mine = (y == c // 2) & (c == g) & (t == 2 * (c % 2) + t // 2)

        @pl.when(jnp.logical_not(mine))
        def _():
            pl.semaphore_signal(
                barrier, inc=1, device_id=(c // 2, g, 2 * (c % 2) + t // 2), device_id_type=MESH
            )

    own_dest = (c == own) & (k == u)
    pl.semaphore_wait(barrier, NCH - 1 + NSEC * NTP - 1 + 8 - own_dest.astype(jnp.int32))

    def wq_copy(d):
        peer = (y + d) % NSEC
        src = wq.at[:, pl.ds(pl.multiple_of(peer * QC, QC), QC)]
        dst = wq_l.at[y, :, pl.ds(0, QC)]
        return lambda: remote(src, dst, wqs.at[d], wqr.at[y], (peer, c, t)), src, dst

    def wkv_copy(d):
        peer = (y + d) % NSEC
        src = wkv.at[:, pl.ds(pl.multiple_of(peer * HD, HD), HD)]
        dst = wq_l.at[y, :, pl.ds(QC, HD)]
        return lambda: remote(src, dst, wks.at[d], wkr.at[y], (peer, c, t)), src, dst

    def wo_copy(d):
        peer = (y + d) % NSEC
        src = wo.at[pl.ds(pl.multiple_of(peer * QC, QC), QC), :]
        return lambda: remote(src, wo_l.at[k, y % 2], wos.at[d], wor.at[k, y % 2], (peer, c, 2 * u + y // 2)), src

    def first_hop(st, d):
        r0 = STREAMS[st][0]
        peer = (c + d) % NCH
        src = hin.at[pl.ds(r0, R), pl.ds(pl.multiple_of(peer * QC, QC), QC)]
        dst = hA.at[st, t // 2, c, :, pl.ds(pl.multiple_of((t % 2) * QC, QC), QC)]
        return lambda: remote(src, dst, h0s.at[st, d], h0r.at[st, c], (y, peer, t)), src, dst

    def columns(st, tt):
        return hA.at[st, tt // 2, :, :, pl.ds(pl.multiple_of((tt % 2) * QC, QC), QC)]

    across = 2 * (1 - u) + k
    across_twin = 2 * (1 - u) + 1 - k

    def second_hop(st, which):
        if which == 0:
            return remote(columns(st, t), columns(st, t), h2s.at[st, 0], h2r.at[st, 0], (y, c, across))
        if which == 1:
            return remote(columns(st, t), columns(st, t), h2s.at[st, 1], h2r.at[st, 1], twin)
        return remote(columns(st, across), columns(st, across), h2s.at[st, 2], h2r.at[st, 2], twin)

    for st in range(NS):
        for d in range(1, NCH):
            first_hop(st, d)[0]().start()
        _, src, dst = first_hop(st, 0)
        pltpu.make_async_copy(src, dst, h0r.at[st, c]).start()
    for d in range(1, NSEC):
        wq_copy(d)[0]().start()
        wkv_copy(d)[0]().start()
    _, src, dst = wq_copy(0)
    pltpu.make_async_copy(src, dst, wqr.at[y]).start()
    _, src, dst = wkv_copy(0)
    pltpu.make_async_copy(src, dst, wkr.at[y]).start()
    cache_copy = pltpu.make_async_copy(cache, cachev, csem)
    cache_copy.start()

    for st in range(NS):
        for d in range(NCH):
            g = (c + NCH - d) % NCH
            got(hA.at[st, t // 2, g, :, pl.ds(pl.multiple_of((t % 2) * QC, QC), QC)], h0r.at[st, g])
        second_hop(st, 0).start()
        second_hop(st, 1).start()

    for d in range(NSEC):
        g = (y + NSEC - d) % NSEC
        got(wq_l.at[g, :, pl.ds(0, QC)], wqr.at[g])
        got(wq_l.at[g, :, pl.ds(QC, HD)], wkr.at[g])
    for d in range(NSEC):
        if d:
            wo_copy(d)[0]().start()
        else:
            @pl.when(k == y // 2)
            def _():
                pltpu.make_async_copy(wo_copy(0)[1], wo_l.at[k, y % 2], wor.at[k, y % 2]).start()

            @pl.when(k != y // 2)
            def _():
                wo_copy(0)[0]().start()
    for d in range(1, NSEC):
        wq_copy(d)[0]().wait_send()
        wkv_copy(d)[0]().wait_send()
    for g in range(NSEC):
        row = gain[pl.ds(g * NCH + c, 1), :]
        column = jnp.transpose(jnp.broadcast_to(row, (128, QC)))
        for a in range(PC // 128):
            part = wq_l[g, :, a * 128:(a + 1) * 128].astype(F32) * column
            wq_l[g, :, a * 128:(a + 1) * 128] = part.astype(BF)
    for st in range(NS):
        got(columns(st, across), h2r.at[st, 0])
        second_hop(st, 2).start()
    for st in range(NS):
        got(columns(st, 2 * u + 1 - k), h2r.at[st, 1])
        got(columns(st, across_twin), h2r.at[st, 2])
        for d in range(1, NCH):
            first_hop(st, d)[0]().wait_send()
        for which in range(3):
            second_hop(st, which).wait_send()
    cache_copy.wait()

    def ag_copy(st, e):
        g = (own + e) % 8
        piece = hA.at[st, k, own]
        return remote(piece, piece, s7.at[st, e], r7.at[st, own], (g // 2, c, 2 * (g % 2) + k))

    def twin_copy(st, e):
        g = (own + 8 - e) % 8
        piece = hA.at[st, k, g]
        return remote(piece, piece, s7f.at[st, e], r7f.at[st, g], twin)

    def ag_send(st):
        for e in range(1, 8):
            ag_copy(st, e).start()
        twin_copy(st, 0).start()

    def ag_forward(st, s):
        @pl.when(s < NSEC - 1)
        def _():
            for e in range(1, 8):
                g = (own + 8 - e) % 8
                got(hA.at[st, k, g], r7.at[st, g])
                twin_copy(st, e).start()

    def ag_wait(st, s):
        @pl.when(s < NSEC - 1)
        def _():
            for e in range(8):
                g = (own + 8 - e) % 8
                got(hA.at[st, 1 - k, g], r7f.at[st, g])

    def ag_sent(st):
        for e in range(1, 8):
            ag_copy(st, e).wait_send()
        for e in range(8):
            twin_copy(st, e).wait_send()

    def p1_copy(st, d):
        peer = (c + d) % NCH
        return remote(part1.at[st, peer], rbuf.at[st, c], s1.at[st, d], r1.at[st, c], (y, peer, t))

    def ss_copy(st, d):
        peer = (c + d) % NCH
        return remote(ssend.at[st, peer], srecv.at[st, c], ss_s.at[st, d], ss_r.at[st, c], (y, peer, t))

    def project(st):
        total = None
        for half in range(2):
            x = hA[st, half].reshape(NCH * R, 512)
            w = wq_l[pl.ds(2 * half, 2)].reshape(512, PC)
            term = jnp.dot(x, w, preferred_element_type=F32)
            total = term if total is None else total + term
        part1[st] = total.astype(BF).reshape(NCH, R, PC)
        for d in range(1, NCH):
            p1_copy(st, d).start()
        ones = jnp.ones((8, 128), BF)
        for g in range(NCH):
            acc = None
            for half in range(2):
                wide = hA[st, half, g].astype(F32)
                square = wide * wide
                for a in range(4):
                    piece = square[:, a * 128:(a + 1) * 128]
                    acc = piece if acc is None else acc + piece
            high = acc.astype(BF)
            low = (acc - high.astype(F32)).astype(BF)
            dims = (((1,), (1,)), ((), ()))
            row = lax.dot_general(ones, high, dims, preferred_element_type=F32)
            row = row + lax.dot_general(ones, low, dims, preferred_element_type=F32)
            ssend[st, g] = jnp.concatenate([row, jnp.zeros((8, 128 - R), F32)], axis=1)
        for d in range(1, NCH):
            ss_copy(st, d).start()
        rbuf[st, c] = part1[st, c]
        srecv[st, c] = ssend[st, c]

    def p2_copy(st, s):
        return remote(sbuf2.at[st], qbuf.at[st, y], s2.at[st], r2.at[st, y], (s, c, t))

    def finish_projection(st, s):
        r0 = STREAMS[st][0]
        for d in range(1, NCH):
            g = (c + NCH - d) % NCH
            got(rbuf.at[st, g], r1.at[st, g])
            got(srecv.at[st, g], ss_r.at[st, g])
        total = rbuf[st, 0].astype(F32)
        squares = srecv[st, 0]
        for g in range(1, NCH):
            total = total + rbuf[st, g].astype(F32)
            squares = squares + srecv[st, g]
        inv = lax.rsqrt(squares * (1.0 / WIDTH) + 1e-05)[0:1, :R]
        eye = lax.broadcasted_iota(jnp.int32, (R, R), 0) == lax.broadcasted_iota(jnp.int32, (R, R), 1)
        scale = jnp.sum(jnp.where(eye, inv, 0.0), axis=1, keepdims=True)
        total = total * scale
        cs = table[0, r0:r0 + R, :]
        sn = table[1, r0:r0 + R, :]
        to_score = math.log2(math.e) / math.sqrt(HD)

        def rope(v):
            return v * cs + pltpu.roll(v, 64, 1) * sn

        q0 = rope(total[:, 0:128]) * to_score
        q1 = rope(total[:, 128:256]) * to_score
        kv = total[:, 256:384]
        even = (y % 2 == 0).astype(F32)
        kv = rope(kv) * even + kv * (1.0 - even)
        sbuf2[st] = jnp.concatenate([q0, q1, kv], axis=1).astype(BF)

        @pl.when(y == s)
        def _():
            qbuf[st, y] = sbuf2[st]

        @pl.when(y != s)
        def _():
            p2_copy(st, s).start()

        for d in range(1, NCH):
            p1_copy(st, d).wait_send()
            ss_copy(st, d).wait_send()

        @pl.when(s > 0)
        def _():
            ag_sent(st)
            bout_sent(st, s - 1)

    def p3_copy(st, peer):
        return remote(msend.at[st, peer], mixb.at[st, k, c], s3.at[st, peer], r3.at[st], (peer, c, t))

    def pool_copy(d):
        peer = (y + d) % NSEC
        return remote(placed.at[peer], pbuf.at[y], ps.at[d], pr.at[y], (peer, c, t))

    def attend(st):
        r0 = STREAMS[st][0]
        seen = r0 + R
        dims = (((1,), (1,)), ((), ()))
        for j in range(2):
            for g in (2 * j, 2 * j + 1):
                @pl.when(y != g)
                def _():
                    got(qbuf.at[st, g], r2.at[st, g])

                kvnew[r0:r0 + R, g * 128:(g + 1) * 128] = qbuf[st, g, :, QC:PC]
            q = jnp.concatenate(
                [qbuf[st, 2 * j + hh // 2, :, (hh % 2) * 128:(hh % 2 + 1) * 128] for hh in range(4)], axis=0
            )
            kcol = j * 256
            vcol = j * 256 + 128
            sf = lax.dot_general(q, kvnew[0:seen, kcol:kcol + 128], dims, preferred_element_type=F32)
            row = lax.broadcasted_iota(jnp.int32, (4, R, seen), 1).reshape(4 * R, seen) + r0
            col = lax.broadcasted_iota(jnp.int32, (4 * R, seen), 1)
            sf = jnp.where(col <= row, sf, -1e30)
            peak = jnp.full((4 * R, 128), -1e30, F32)
            for i in range(NCHUNK):
                keys = cachev[i * CH:(i + 1) * CH, kcol:kcol + 128]
                sc = lax.dot_general(q, keys, dims, preferred_element_type=F32) + bias[i:i + 1, :]
                S[i] = sc
                for a in range(CH // 128):
                    peak = jnp.maximum(peak, sc[:, a * 128:(a + 1) * 128])
            top = jnp.maximum(jnp.max(peak, axis=1, keepdims=True), jnp.max(sf, axis=1, keepdims=True))
            pf = jnp.exp2(sf - top)
            acc = jnp.dot(pf.astype(BF), kvnew[0:seen, vcol:vcol + 128], preferred_element_type=F32)
            den = jnp.zeros((4 * R, 128), F32)
            for i in range(NCHUNK):
                p = jnp.exp2(S[i] - top)
                for a in range(CH // 128):
                    den = den + p[:, a * 128:(a + 1) * 128]
                values = cachev[i * CH:(i + 1) * CH, vcol:vcol + 128]
                acc = acc + jnp.dot(p.astype(BF), values, preferred_element_type=F32)
            den = jnp.sum(den, axis=1, keepdims=True) + jnp.sum(pf, axis=1, keepdims=True)
            mixed = (acc / den).astype(BF)
            for hh in range(4):
                msend[st, 2 * j + hh // 2, :, (hh % 2) * 128:(hh % 2 + 1) * 128] = mixed[hh * R:(hh + 1) * R]
            for g in (2 * j, 2 * j + 1):
                @pl.when(y != g)
                def _():
                    p3_copy(st, g).start()

                @pl.when(y == g)
                def _():
                    mixb[st, k, c] = msend[st, g]

    def place_pages():
        for slot in range(2 * NSEC):
            acc = None
            for q in range(NEW // PAGE):
                term = kvnew[q * PAGE:(q + 1) * PAGE, :].astype(F32) * sel[slot, q]
                acc = term if acc is None else acc + term
            placed[slot // 2, (slot % 2) * PAGE:(slot % 2 + 1) * PAGE, :] = acc.astype(BF)
        for d in range(1, NSEC):
            pool_copy(d).start()
        pbuf[y] = placed[y]

    def mix(st, s):
        @pl.when(y == s)
        def _():
            attend(st)

        @pl.when(y != s)
        def _():
            p2_copy(st, s).wait_send()

    def p4_copy(st, d):
        peer = (c + d) % NCH
        piece = mixb.at[st, k, c]
        return remote(piece, piece, s4.at[st, d], r4.at[st, c], (y, peer, t))

    def p5_copy(st, d):
        g = (c + NCH - d) % NCH
        piece = mixb.at[st, k, g]
        return remote(piece, piece, s5.at[st, d], r5.at[st, g], twin)

    def spread(st, s):
        @pl.when(y != s)
        def _():
            got(mixb.at[st, k, c], r3.at[st])

        for d in range(1, NCH):
            p4_copy(st, d).start()
        p5_copy(st, 0).start()
        if st == NS - 1:
            @pl.when(y == s)
            def _():
                place_pages()

    def spread_twin(st):
        for d in range(1, NCH):
            g = (c + NCH - d) % NCH
            got(mixb.at[st, k, g], r4.at[st, g])
            p5_copy(st, d).start()

    def p6_copy(st, e):
        g = (own + e) % 8
        return remote(osend.at[st, g], ob.at[st, own], s6.at[st, e], r6.at[st, own], (g // 2, c, 2 * (g % 2) + k))

    def bout_copy(st, s, a):
        src = hA.at[st, k, own, :, pl.ds(a * QC, QC)]
        dst = obuf.at[c, pl.ds(STREAMS[st][0], R), :]
        return lambda: remote(src, dst, so.at[st, a], ro.at[st, c], (s, own, 2 * k + a)), src, dst

    def bout_mine(s, a):
        return (y == s) & (c == own) & (t == 2 * k + a)

    def bout_send(st, s):
        for a in range(2):
            @pl.when(bout_mine(s, a))
            def _():
                _, src, dst = bout_copy(st, s, a)
                pltpu.make_async_copy(src, dst, so.at[st, a]).start()

            @pl.when(jnp.logical_not(bout_mine(s, a)))
            def _():
                bout_copy(st, s, a)[0]().start()

    def bout_sent(st, s):
        for a in range(2):
            @pl.when(bout_mine(s, a))
            def _():
                got(bout_copy(st, s, a)[2], so.at[st, a])

            @pl.when(jnp.logical_not(bout_mine(s, a)))
            def _():
                bout_copy(st, s, a)[0]().wait_send()

    def wo_wait():
        for a in range(2):
            for b in range(2):
                got(wo_l.at[a, b], wor.at[a, b])
        for d in range(NSEC):
            if d:
                wo_copy(d)[0]().wait_send()
            else:
                @pl.when(k != y // 2)
                def _():
                    wo_copy(0)[0]().wait_send()

    def output_projection(st, s):
        for d in range(NCH):
            g = (c + NCH - d) % NCH
            got(mixb.at[st, 1 - k, g], r5.at[st, g])
        if st == 0:
            @pl.when(s == 0)
            def _():
                wo_wait()

        for b in range(2):
            total = None
            for a in range(2):
                x = mixb[st, a].reshape(NCH * R, QC)
                term = jnp.dot(x, wo_l[a, b], preferred_element_type=F32)
                total = term if total is None else total + term
            osend[st, :, :, b * QC:(b + 1) * QC] = total.astype(BF).reshape(NCH, R, QC)

        for d in range(1, NCH):
            p4_copy(st, d).wait_send()
        for d in range(NCH):
            p5_copy(st, d).wait_send()

        @pl.when(y == s)
        def _():
            for g in range(NSEC):
                @pl.when(y != g)
                def _():
                    p3_copy(st, g).wait_send()

        for e in range(1, 8):
            p6_copy(st, e).start()
        ob[st, own] = osend[st, own]

    def residual(st, s):
        for e in range(1, 8):
            g = (own + 8 - e) % 8
            got(ob.at[st, g], r6.at[st, g])
        total = ob[st, 0].astype(F32)
        for g in range(1, 8):
            total = total + ob[st, g].astype(F32)
        hA[st, k, own] = (hA[st, k, own].astype(F32) + total).astype(BF)

        @pl.when(s < NSEC - 1)
        def _():
            ag_send(st)

        bout_send(st, s)
        for e in range(1, 8):
            p6_copy(st, e).wait_send()

    phases = [
        lambda st, s: project(st),
        finish_projection,
        mix,
        spread,
        lambda st, s: spread_twin(st),
        output_projection,
        residual,
        ag_forward,
        ag_wait,
    ]
    n = len(phases)

    def section_step(s, carry):
        for i in range(n):
            phases[i](0, s)
            for st in range(1, NS):
                if i >= SKEW:
                    phases[i - SKEW](st, s)
                else:
                    @pl.when(s > 0)
                    def _():
                        phases[n + i - SKEW](st, s - 1)
        return carry

    lax.fori_loop(0, NSEC, section_step, 0)
    for i in range(SKEW):
        for st in range(1, NS):
            phases[n + i - SKEW](st, NSEC - 1)

    for st in range(NS):
        bout_sent(st, NSEC - 1)
        for d in range(NCH):
            g = (c + d) % NCH
            mine = (y == c // 2) & (c == g) & (t == 2 * (c % 2) + t // 2)

            @pl.when(jnp.logical_not(mine))
            def _():
                got(obuf.at[g, pl.ds(STREAMS[st][0], R), :], ro.at[st, g])
    for d in range(1, NSEC):
        g = (y + NSEC - d) % NSEC
        got(pbuf.at[g], pr.at[g])
        pool_copy(d).wait_send()
    for g in range(NCH):
        bout[:, g * QC:(g + 1) * QC] = obuf[g]
    for g in range(NSEC):
        pool[g] = pbuf[g]


def local(block_input, norm_gain, w_query, w_kv, w_out, kv_cache, page_table, prefix_len, page_owner):
    length = prefix_len[0]
    gain = norm_gain.astype(F32).reshape(NSEC * NCH, WIDTH // (NSEC * NCH))

    pages = PREFIX // PAGE
    ids = jnp.arange(pages, dtype=jnp.int32)
    logical = jnp.sum(jnp.where(page_table[0][None, :] == ids[:, None], ids[None, :], 0), axis=1)
    place = logical[:, None] * PAGE + jnp.arange(PAGE, dtype=jnp.int32)[None, :]
    bias = jnp.where(place < length, 0.0, -1e30).astype(F32).reshape(NCHUNK, CH)

    lane = jnp.arange(HD)
    inverse = 500000.0 ** (-((lane % (HD // 2)).astype(F32) * 2.0 / HD))
    angles = (length + jnp.arange(NEW)).astype(F32)[:, None] * inverse[None, :]
    sine = jnp.where(lane[None, :] < HD // 2, -1.0, 1.0) * jnp.sin(angles)
    table = jnp.stack([jnp.cos(angles), sine])

    owners = page_owner[0, :, 0]
    q = jnp.arange(NEW // PAGE)
    earlier = (owners[:, None] == owners[None, :]) & (q[None, :] < q[:, None])
    slots = owners * 2 + jnp.sum(earlier.astype(jnp.int32), axis=1)
    sel = (slots[None, :] == jnp.arange(2 * NSEC)[:, None]).astype(F32)

    vm = pl.BlockSpec(memory_space=pltpu.VMEM)
    hbm = pl.BlockSpec(memory_space=pl.ANY)
    dma = pltpu.SemaphoreType.DMA
    V = pltpu.VMEM
    bout, pool = pl.pallas_call(
        kernel,
        out_shape=(
            jax.ShapeDtypeStruct((NEW, WIDTH // NTP), BF),
            jax.ShapeDtypeStruct((NSEC, 2 * PAGE, 512), BF),
        ),
        in_specs=[vm, hbm, hbm, hbm, vm, hbm, vm, vm, pl.BlockSpec(memory_space=pltpu.SMEM)],
        out_specs=(vm, vm),
        scratch_shapes=[
            V((PREFIX, 512), BF),
            V((NSEC, 256, PC), BF),
            V((2, 2, 256, 256), BF),
            V((NS, 2, NCH, R, 512), BF),
            V((NS, NCH, R, PC), BF),
            V((NS, NCH, R, PC), BF),
            V((NS, NCH, 8, 128), F32),
            V((NS, NCH, 8, 128), F32),
            V((NS, R, PC), BF),
            V((NS, NSEC, R, PC), BF),
            V((NEW, 512), BF),
            V((NCHUNK, 4 * R, CH), F32),
            V((NS, NSEC, R, QC), BF),
            V((NS, 2, NCH, R, QC), BF),
            V((NS, NCH, R, 512), BF),
            V((NS, NCH, R, 512), BF),
            V((NSEC, 2 * PAGE, 512), BF),
            V((NCH, NEW, QC), BF),
            V((NSEC, 2 * PAGE, 512), BF),
            dma(()),
            dma((NS, NCH)), dma((NS, NCH)),
            dma((NS, 3)), dma((NS, 3)),
            dma((NSEC,)), dma((NSEC,)),
            dma((NSEC,)), dma((NSEC,)),
            dma((NSEC,)), dma((2, 2)),
            dma((NS, NCH)), dma((NS, NCH)),
            dma((NS, NCH)), dma((NS, NCH)),
            dma((NS,)), dma((NS, NSEC)),
            dma((NS, NSEC)), dma((NS,)),
            dma((NS, NCH)), dma((NS, NCH)),
            dma((NS, NCH)), dma((NS, NCH)),
            dma((NS, 8)), dma((NS, 8)),
            dma((NS, 8)), dma((NS, 8)),
            dma((NS, 8)), dma((NS, 8)),
            dma((NS, 2)), dma((NS, NCH)),
            dma((NSEC,)), dma((NSEC,)),
        ],
        compiler_params=pltpu.CompilerParams(
            collective_id=0, has_side_effects=True, vmem_limit_bytes=48 * 1024 * 1024
        ),
    )(block_input[0], w_query, w_kv, w_out, gain, kv_cache.reshape(PREFIX, 512), bias, table, sel)
    return bout[None, None], pool.reshape(1, 1, 2 * NSEC, PAGE, 512)


def solution(mesh):
    in_specs = (
        P("chain", None, "tp"),
        P(),
        P(("section", "chain"), "tp"),
        P(("section", "chain"), "tp"),
        P("tp", ("section", "chain")),
        P("section", "chain", None, None, "tp"),
        P("chain", None),
        P("chain"),
        P("chain", "section", None),
    )
    out_specs = (P("section", "chain", None, "tp"), P("section", "chain", None, None, "tp"))
    return jax.shard_map(local, mesh=mesh, in_specs=in_specs, out_specs=out_specs, check_vma=False)
```

```python
import math

import jax
import jax.numpy as jnp
from jax import lax
from jax.experimental import pallas as pl
from jax.experimental.pallas import tpu as pltpu
from jax.sharding import PartitionSpec as P

HD = 128
PAGE = 16
PREFIX = 4096
NEW = 64
WIDTH = 8192
NSEC = 4
NCH = 8
NTP = 4
QC = 256
PC = 384
CH = 512
NCHUNK = PREFIX // CH
STREAMS = ((0, 32), (32, 32))
NS = len(STREAMS)
R = STREAMS[0][1]
MESH = pl.DeviceIdType.MESH
BF = jnp.bfloat16
F32 = jnp.float32


def kernel(
    hin, wq, wkv, wo, gain_in, cache, pages_in, cos_in, sin_in, length, owner,
    bout, pool,
    gain, pages, cosv, sinv, bias, cachev, wq_l, wo_l, hA, part1, rbuf, ssend, srecv, sbuf2, qbuf, kvnew, S, msend, mixb, osend, ob, placed, obuf, pbuf,
    insem, csem, h0s, h0r, h2s, h2r, wqs, wqr, wks, wkr, wos, wor,
    s1, r1, ss_s, ss_r, s2, r2, s3, r3, s4, r4, s5, r5, s6, r6, s7, r7, s7f, r7f, so, ro, ps, pr,
):
    y = lax.axis_index("section")
    c = lax.axis_index("chain")
    t = lax.axis_index("tp")
    u = t // 2
    k = t % 2
    own = 2 * y + u
    twin = (y, c, 2 * u + 1 - k)

    def remote(src, dst, ssem, rsem, dev):
        return pltpu.make_async_remote_copy(
            src_ref=src, dst_ref=dst, send_sem=ssem, recv_sem=rsem, device_id=dev, device_id_type=MESH
        )

    def got(dst, rsem):
        pltpu.make_async_copy(dst, dst, rsem).wait()

    inputs = ((gain_in, gain), (pages_in, pages), (cos_in, cosv), (sin_in, sinv))
    for i, (src, dst) in enumerate(inputs):
        pltpu.make_async_copy(src, dst, insem.at[i]).start()
    cache_copy = pltpu.make_async_copy(cache, cachev, csem)
    cache_copy.start()
    across = 2 * (1 - u) + k
    across_twin = 2 * (1 - u) + 1 - k

    barrier = pltpu.get_barrier_semaphore()
    for d in range(1, NCH):
        pl.semaphore_signal(barrier, inc=1, device_id=(y, (c + d) % NCH, t), device_id_type=MESH)
        pl.semaphore_signal(barrier, inc=1, device_id=(y, (c + d) % NCH, across), device_id_type=MESH)
    for dy in range(NSEC):
        for dt in range(NTP):
            if dy or dt:
                pl.semaphore_signal(
                    barrier, inc=1, device_id=((y + dy) % NSEC, c, (t + dt) % NTP), device_id_type=MESH
                )
    for g in range(NCH):
        mine = (y == c // 2) & (c == g) & (t == 2 * (c % 2) + t // 2)

        @pl.when(jnp.logical_not(mine))
        def _():
            pl.semaphore_signal(
                barrier, inc=1, device_id=(c // 2, g, 2 * (c % 2) + t // 2), device_id_type=MESH
            )

    own_dest = (c == own) & (k == u)

    for i, (src, dst) in enumerate(inputs):
        pltpu.make_async_copy(src, dst, insem.at[i]).wait()
    n_pages = PREFIX // PAGE
    logical = lax.broadcasted_iota(jnp.int32, (8, n_pages), 1)
    live = jnp.clip(length[0] - logical * PAGE, 0, PAGE).astype(F32).astype(BF)
    physical = lax.broadcasted_iota(jnp.int32, (n_pages, n_pages), 0)
    named = jnp.where(pages[...] == physical, 1.0, 0.0).astype(BF)
    rows_live = lax.dot_general(live, named, (((1,), (1,)), ((), ())), preferred_element_type=F32)
    chunk_pages = CH // PAGE
    first = lax.broadcasted_iota(jnp.int32, (NCHUNK, n_pages), 0) * chunk_pages
    page = lax.broadcasted_iota(jnp.int32, (NCHUNK, n_pages), 1)
    held = jnp.where((page >= first) & (page < first + chunk_pages), rows_live, 0.0).astype(BF)
    key = lax.broadcasted_iota(jnp.int32, (n_pages, CH), 1)
    page_in = lax.rem(lax.broadcasted_iota(jnp.int32, (n_pages, CH), 0), chunk_pages)
    start = page_in * PAGE
    spread_to = jnp.where((key >= start) & (key < start + PAGE), 1.0, 0.0).astype(BF)
    count = jnp.dot(held, spread_to, preferred_element_type=F32)
    row_in = lax.rem(lax.broadcasted_iota(jnp.int32, (NCHUNK, CH), 1), PAGE).astype(F32)
    bias[...] = jnp.where(row_in + 0.5 < count, 0.0, -1e30)

    pl.semaphore_wait(barrier, 2 * (NCH - 1) + NSEC * NTP - 1 + 8 - own_dest.astype(jnp.int32))

    def wq_copy(d):
        peer = (y + d) % NSEC
        src = wq.at[:, pl.ds(pl.multiple_of(peer * QC, QC), QC)]
        dst = wq_l.at[y, :, pl.ds(0, QC)]
        return lambda: remote(src, dst, wqs.at[d], wqr.at[y], (peer, c, t)), src, dst

    def wkv_copy(d):
        peer = (y + d) % NSEC
        src = wkv.at[:, pl.ds(pl.multiple_of(peer * HD, HD), HD)]
        dst = wq_l.at[y, :, pl.ds(QC, HD)]
        return lambda: remote(src, dst, wks.at[d], wkr.at[y], (peer, c, t)), src, dst

    def wo_copy(d):
        peer = (y + d) % NSEC
        src = wo.at[pl.ds(pl.multiple_of(peer * QC, QC), QC), :]
        return lambda: remote(src, wo_l.at[k, y % 2], wos.at[d], wor.at[k, y % 2], (peer, c, 2 * u + y // 2)), src

    def first_hop(st, d, far):
        peer = (c + d) % NCH
        src = hin.at[pl.ds(STREAMS[st][0], R), pl.ds(pl.multiple_of(peer * QC, QC), QC)]
        dst = hA.at[st, t // 2, c, :, pl.ds(pl.multiple_of((t % 2) * QC, QC), QC)]
        dev = (y, peer, across if far else t)
        return lambda: remote(src, dst, h0s.at[st, far, d], h0r.at[st, far, c], dev), src, dst

    def columns(st, tt):
        return hA.at[st, tt // 2, :, :, pl.ds(pl.multiple_of((tt % 2) * QC, QC), QC)]

    def second_hop(st, far):
        piece = columns(st, across if far else t)
        return remote(piece, piece, h2s.at[st, far], h2r.at[st, far], twin)

    def first_sends(st):
        _, src, dst = first_hop(st, 0, 0)
        pltpu.make_async_copy(src, dst, h0r.at[st, 0, c]).start()
        first_hop(st, 0, 1)[0]().start()
        for d in range(1, NCH):
            first_hop(st, d, 0)[0]().start()
            first_hop(st, d, 1)[0]().start()

    def second_sends(st):
        for far in range(2):
            tt = across if far else t
            for d in range(NCH):
                g = (c + NCH - d) % NCH
                got(hA.at[st, tt // 2, g, :, pl.ds(pl.multiple_of((tt % 2) * QC, QC), QC)], h0r.at[st, far, g])
            second_hop(st, far).start()

    first_sends(0)
    for d in range(1, NSEC):
        wq_copy(d)[0]().start()
        wkv_copy(d)[0]().start()
    _, src, dst = wq_copy(0)
    pltpu.make_async_copy(src, dst, wqr.at[y]).start()
    _, src, dst = wkv_copy(0)
    pltpu.make_async_copy(src, dst, wkr.at[y]).start()
    for st in range(1, NS):
        first_sends(st)
    for d in range(NSEC):
        if d:
            wo_copy(d)[0]().start()
        else:
            @pl.when(k == y // 2)
            def _():
                pltpu.make_async_copy(wo_copy(0)[1], wo_l.at[k, y % 2], wor.at[k, y % 2]).start()

            @pl.when(k != y // 2)
            def _():
                wo_copy(0)[0]().start()

    second_sends(0)
    for d in range(NSEC):
        g = (y + NSEC - d) % NSEC
        got(wq_l.at[g, :, pl.ds(0, QC)], wqr.at[g])
        got(wq_l.at[g, :, pl.ds(QC, HD)], wkr.at[g])
        row = gain[pl.ds(g * NCH + c, 1), :]
        column = jnp.transpose(jnp.broadcast_to(row, (128, QC)))
        for a in range(PC // 128):
            part = wq_l[g, :, a * 128:(a + 1) * 128].astype(F32) * column
            wq_l[g, :, a * 128:(a + 1) * 128] = part.astype(BF)
    for st in range(1, NS):
        second_sends(st)

    def first_wait(st):
        got(columns(st, 2 * u + 1 - k), h2r.at[st, 0])
        got(columns(st, across_twin), h2r.at[st, 1])

    def prologue_sent():
        for d in range(1, NSEC):
            wq_copy(d)[0]().wait_send()
            wkv_copy(d)[0]().wait_send()
        for st in range(NS):
            first_hop(st, 0, 1)[0]().wait_send()
            for d in range(1, NCH):
                first_hop(st, d, 0)[0]().wait_send()
                first_hop(st, d, 1)[0]().wait_send()
            for far in range(2):
                second_hop(st, far).wait_send()
        cache_copy.wait()

    def ag_copy(st, e):
        g = (own + e) % 8
        piece = hA.at[st, k, own]
        return remote(piece, piece, s7.at[st, e], r7.at[st, own], (g // 2, c, 2 * (g % 2) + k))

    def twin_copy(st, e):
        g = (own + 8 - e) % 8
        piece = hA.at[st, k, g]
        return remote(piece, piece, s7f.at[st, e], r7f.at[st, g], twin)

    def ag_send(st):
        for e in range(1, 8):
            ag_copy(st, e).start()
        twin_copy(st, 0).start()

    def ag_forward(st, s):
        @pl.when(s < NSEC - 1)
        def _():
            for e in range(1, 8):
                g = (own + 8 - e) % 8
                got(hA.at[st, k, g], r7.at[st, g])
                twin_copy(st, e).start()

    def ag_wait(st, s):
        @pl.when(s == 0)
        def _():
            first_wait(st)

        @pl.when(s > 0)
        def _():
            for e in range(8):
                g = (own + 8 - e) % 8
                got(hA.at[st, 1 - k, g], r7f.at[st, g])

    def ag_sent(st):
        for e in range(1, 8):
            ag_copy(st, e).wait_send()
        for e in range(8):
            twin_copy(st, e).wait_send()

    def p1_copy(st, d):
        peer = (c + d) % NCH
        return remote(part1.at[st, peer], rbuf.at[st, c], s1.at[st, d], r1.at[st, c], (y, peer, t))

    def ss_copy(st, d):
        peer = (c + d) % NCH
        return remote(ssend.at[st, peer], srecv.at[st, c], ss_s.at[st, d], ss_r.at[st, c], (y, peer, t))

    def project(st, s):
        ag_wait(st, s)
        total = None
        for half in range(2):
            x = hA[st, half].reshape(NCH * R, 512)
            w = wq_l[pl.ds(2 * half, 2)].reshape(512, PC)
            term = jnp.dot(x, w, preferred_element_type=F32)
            total = term if total is None else total + term
        part1[st] = total.astype(BF).reshape(NCH, R, PC)
        for d in range(1, NCH):
            p1_copy(st, d).start()
        ones = jnp.ones((8, 128), BF)
        for g in range(NCH):
            acc = None
            for half in range(2):
                wide = hA[st, half, g].astype(F32)
                square = wide * wide
                for a in range(4):
                    piece = square[:, a * 128:(a + 1) * 128]
                    acc = piece if acc is None else acc + piece
            high = acc.astype(BF)
            low = (acc - high.astype(F32)).astype(BF)
            dims = (((1,), (1,)), ((), ()))
            row = lax.dot_general(ones, high, dims, preferred_element_type=F32)
            row = row + lax.dot_general(ones, low, dims, preferred_element_type=F32)
            ssend[st, g] = jnp.concatenate([row, jnp.zeros((8, 128 - R), F32)], axis=1)
        for d in range(1, NCH):
            ss_copy(st, d).start()
        rbuf[st, c] = part1[st, c]
        srecv[st, c] = ssend[st, c]

    def p2_copy(st, s):
        return remote(sbuf2.at[st], qbuf.at[st, y], s2.at[st], r2.at[st, y], (s, c, t))

    def finish_projection(st, s):
        r0 = STREAMS[st][0]
        for d in range(1, NCH):
            g = (c + NCH - d) % NCH
            got(rbuf.at[st, g], r1.at[st, g])
            got(srecv.at[st, g], ss_r.at[st, g])
        total = rbuf[st, 0].astype(F32)
        squares = srecv[st, 0]
        for g in range(1, NCH):
            total = total + rbuf[st, g].astype(F32)
            squares = squares + srecv[st, g]
        inv = lax.rsqrt(squares * (1.0 / WIDTH) + 1e-05)[0:1, :R]
        eye = lax.broadcasted_iota(jnp.int32, (R, R), 0) == lax.broadcasted_iota(jnp.int32, (R, R), 1)
        scale = jnp.sum(jnp.where(eye, inv, 0.0), axis=1, keepdims=True)
        total = total * scale
        cs = cosv[r0:r0 + R, :]
        sn = sinv[r0:r0 + R, :]
        to_score = math.log2(math.e) / math.sqrt(HD)

        def rope(v):
            return v * cs + pltpu.roll(v, 64, 1) * sn

        q0 = rope(total[:, 0:128]) * to_score
        q1 = rope(total[:, 128:256]) * to_score
        kv = total[:, 256:384]
        even = (y % 2 == 0).astype(F32)
        kv = rope(kv) * even + kv * (1.0 - even)
        sbuf2[st] = jnp.concatenate([q0, q1, kv], axis=1).astype(BF)

        @pl.when(y == s)
        def _():
            qbuf[st, y] = sbuf2[st]

        @pl.when(y != s)
        def _():
            p2_copy(st, s).start()

        for d in range(1, NCH):
            p1_copy(st, d).wait_send()
            ss_copy(st, d).wait_send()

        @pl.when(s > 0)
        def _():
            ag_sent(st)
            bout_send(st, s - 1)

        if st == 0:
            @pl.when(s == 0)
            def _():
                prologue_sent()

    def p3_copy(st, peer):
        return remote(msend.at[st, peer], mixb.at[st, k, c], s3.at[st, peer], r3.at[st], (peer, c, t))

    def pool_copy(d):
        peer = (y + d) % NSEC
        return remote(placed.at[peer], pbuf.at[y], ps.at[d], pr.at[y], (peer, c, t))

    def attend(st):
        r0 = STREAMS[st][0]
        seen = r0 + R
        dims = (((1,), (1,)), ((), ()))
        for j in range(2):
            for g in (2 * j, 2 * j + 1):
                @pl.when(y != g)
                def _():
                    got(qbuf.at[st, g], r2.at[st, g])

                kvnew[r0:r0 + R, g * 128:(g + 1) * 128] = qbuf[st, g, :, QC:PC]
            q = jnp.concatenate(
                [qbuf[st, 2 * j + hh // 2, :, (hh % 2) * 128:(hh % 2 + 1) * 128] for hh in range(4)], axis=0
            )
            kcol = j * 256
            vcol = j * 256 + 128
            sf = lax.dot_general(q, kvnew[0:seen, kcol:kcol + 128], dims, preferred_element_type=F32)
            row = lax.broadcasted_iota(jnp.int32, (4, R, seen), 1).reshape(4 * R, seen) + r0
            col = lax.broadcasted_iota(jnp.int32, (4 * R, seen), 1)
            sf = jnp.where(col <= row, sf, -1e30)
            peak = jnp.full((4 * R, 128), -1e30, F32)
            for i in range(NCHUNK):
                keys = cachev[i * CH:(i + 1) * CH, kcol:kcol + 128]
                sc = lax.dot_general(q, keys, dims, preferred_element_type=F32) + bias[i:i + 1, :]
                S[i] = sc
                for a in range(CH // 128):
                    peak = jnp.maximum(peak, sc[:, a * 128:(a + 1) * 128])
            top = jnp.maximum(jnp.max(peak, axis=1, keepdims=True), jnp.max(sf, axis=1, keepdims=True))
            pf = jnp.exp2(sf - top)
            acc = jnp.dot(pf.astype(BF), kvnew[0:seen, vcol:vcol + 128], preferred_element_type=F32)
            den = jnp.zeros((4 * R, 128), F32)
            for i in range(NCHUNK):
                p = jnp.exp2(S[i] - top)
                for a in range(CH // 128):
                    den = den + p[:, a * 128:(a + 1) * 128]
                values = cachev[i * CH:(i + 1) * CH, vcol:vcol + 128]
                acc = acc + jnp.dot(p.astype(BF), values, preferred_element_type=F32)
            den = jnp.sum(den, axis=1, keepdims=True) + jnp.sum(pf, axis=1, keepdims=True)
            mixed = (acc / den).astype(BF)
            for hh in range(4):
                msend[st, 2 * j + hh // 2, :, (hh % 2) * 128:(hh % 2 + 1) * 128] = mixed[hh * R:(hh + 1) * R]
            for g in (2 * j, 2 * j + 1):
                @pl.when(y != g)
                def _():
                    p3_copy(st, g).start()

                @pl.when(y == g)
                def _():
                    mixb[st, k, c] = msend[st, g]

    def place_pages():
        for slot in range(2 * NSEC):
            acc = None
            for q in range(NEW // PAGE):
                rank = jnp.int32(0)
                for before in range(q):
                    rank = rank + jnp.where(owner[before] == owner[q], 1, 0)
                factor = jnp.where(owner[q] * 2 + rank == slot, 1.0, 0.0)
                term = kvnew[q * PAGE:(q + 1) * PAGE, :].astype(F32) * factor
                acc = term if acc is None else acc + term
            placed[slot // 2, (slot % 2) * PAGE:(slot % 2 + 1) * PAGE, :] = acc.astype(BF)
        for d in range(1, NSEC):
            pool_copy(d).start()
        pbuf[y] = placed[y]

    def mix(st, s):
        @pl.when(y == s)
        def _():
            attend(st)

        @pl.when(y != s)
        def _():
            p2_copy(st, s).wait_send()

    def p4_copy(st, d):
        peer = (c + d) % NCH
        piece = mixb.at[st, k, c]
        return remote(piece, piece, s4.at[st, d], r4.at[st, c], (y, peer, t))

    def p5_copy(st, d):
        g = (c + NCH - d) % NCH
        piece = mixb.at[st, k, g]
        return remote(piece, piece, s5.at[st, d], r5.at[st, g], twin)

    def spread(st, s):
        @pl.when(y != s)
        def _():
            got(mixb.at[st, k, c], r3.at[st])

        for d in range(1, NCH):
            p4_copy(st, d).start()
        p5_copy(st, 0).start()
        if st == NS - 1:
            @pl.when(y == s)
            def _():
                place_pages()

    def spread_twin(st, s):
        for d in range(1, NCH):
            g = (c + NCH - d) % NCH
            got(mixb.at[st, k, g], r4.at[st, g])
            p5_copy(st, d).start()

    def p6_copy(st, e):
        g = (own + e) % 8
        return remote(osend.at[st, g], ob.at[st, own], s6.at[st, e], r6.at[st, own], (g // 2, c, 2 * (g % 2) + k))

    def bout_copy(st, s, a):
        src = hA.at[st, k, own, :, pl.ds(a * QC, QC)]
        dst = obuf.at[c, pl.ds(STREAMS[st][0], R), :]
        return lambda: remote(src, dst, so.at[st, a], ro.at[st, c], (s, own, 2 * k + a)), src, dst

    def bout_mine(s, a):
        return (y == s) & (c == own) & (t == 2 * k + a)

    def bout_send(st, s):
        for a in range(2):
            @pl.when(bout_mine(s, a))
            def _():
                _, src, dst = bout_copy(st, s, a)
                pltpu.make_async_copy(src, dst, so.at[st, a]).start()

            @pl.when(jnp.logical_not(bout_mine(s, a)))
            def _():
                bout_copy(st, s, a)[0]().start()

    def bout_sent(st, s):
        for a in range(2):
            @pl.when(bout_mine(s, a))
            def _():
                got(bout_copy(st, s, a)[2], so.at[st, a])

            @pl.when(jnp.logical_not(bout_mine(s, a)))
            def _():
                bout_copy(st, s, a)[0]().wait_send()

    def wo_wait():
        for a in range(2):
            for b in range(2):
                got(wo_l.at[a, b], wor.at[a, b])
        for d in range(NSEC):
            if d:
                wo_copy(d)[0]().wait_send()
            else:
                @pl.when(k != y // 2)
                def _():
                    wo_copy(0)[0]().wait_send()

    def output_projection(st, s):
        for d in range(NCH):
            g = (c + NCH - d) % NCH
            got(mixb.at[st, 1 - k, g], r5.at[st, g])
        if st == 0:
            @pl.when(s == 0)
            def _():
                wo_wait()

        for b in range(2):
            total = None
            for a in range(2):
                x = mixb[st, a].reshape(NCH * R, QC)
                term = jnp.dot(x, wo_l[a, b], preferred_element_type=F32)
                total = term if total is None else total + term
            osend[st, :, :, b * QC:(b + 1) * QC] = total.astype(BF).reshape(NCH, R, QC)

        for e in range(1, 8):
            p6_copy(st, e).start()
        ob[st, own] = osend[st, own]
        for d in range(1, NCH):
            p4_copy(st, d).wait_send()
        for d in range(NCH):
            p5_copy(st, d).wait_send()

        @pl.when(y == s)
        def _():
            for g in range(NSEC):
                @pl.when(y != g)
                def _():
                    p3_copy(st, g).wait_send()

        @pl.when(s > 0)
        def _():
            bout_sent(st, s - 1)

    def residual(st, s):
        for e in range(1, 8):
            g = (own + 8 - e) % 8
            got(ob.at[st, g], r6.at[st, g])
        total = ob[st, 0].astype(F32)
        for g in range(1, 8):
            total = total + ob[st, g].astype(F32)
        hA[st, k, own] = (hA[st, k, own].astype(F32) + total).astype(BF)

        @pl.when(s < NSEC - 1)
        def _():
            ag_send(st)

        @pl.when(s == NSEC - 1)
        def _():
            bout_send(st, s)

        for e in range(1, 8):
            p6_copy(st, e).wait_send()

    def attend_and_spread(st, s):
        mix(st, s)
        spread(st, s)

    def section_step(s, carry):
        for phase in (
            project, finish_projection, attend_and_spread, spread_twin, output_projection, residual, ag_forward
        ):
            for st in range(NS):
                phase(st, s)
        return carry

    lax.fori_loop(0, NSEC, section_step, 0)

    for st in range(NS):
        bout_sent(st, NSEC - 1)
        for d in range(NCH):
            g = (c + d) % NCH
            mine = (y == c // 2) & (c == g) & (t == 2 * (c % 2) + t // 2)

            @pl.when(jnp.logical_not(mine))
            def _():
                got(obuf.at[g, pl.ds(STREAMS[st][0], R), :], ro.at[st, g])
    for d in range(1, NSEC):
        g = (y + NSEC - d) % NSEC
        got(pbuf.at[g], pr.at[g])
        pool_copy(d).wait_send()
    for g in range(NCH):
        bout[:, g * QC:(g + 1) * QC] = obuf[g]
    for g in range(NSEC):
        pool[g] = pbuf[g]


def local(block_input, norm_gain, w_query, w_kv, w_out, kv_cache, page_table, prefix_len, page_owner):
    length = prefix_len[0]
    gain = norm_gain.astype(F32).reshape(NSEC * NCH, WIDTH // (NSEC * NCH))

    lane = jnp.arange(HD)
    inverse = 500000.0 ** (-((lane % (HD // 2)).astype(F32) * 2.0 / HD))
    angles = (length + jnp.arange(NEW)).astype(F32)[:, None] * inverse[None, :]
    sine = jnp.where(lane[None, :] < HD // 2, -1.0, 1.0) * jnp.sin(angles)
    vm = pl.BlockSpec(memory_space=pltpu.VMEM)
    hbm = pl.BlockSpec(memory_space=pltpu.HBM)
    dma = pltpu.SemaphoreType.DMA
    V = pltpu.VMEM
    bout, pool = pl.pallas_call(
        kernel,
        out_shape=(
            jax.ShapeDtypeStruct((NEW, WIDTH // NTP), BF),
            jax.ShapeDtypeStruct((NSEC, 2 * PAGE, 512), BF),
        ),
        in_specs=[hbm] * 9 + [pl.BlockSpec(memory_space=pltpu.SMEM)] * 2,
        out_specs=(vm, vm),
        scratch_shapes=[
            V((NSEC * NCH, QC), F32),
            V((1, PREFIX // PAGE), jnp.int32),
            V((NEW, HD), F32),
            V((NEW, HD), F32),
            V((NCHUNK, CH), F32),
            V((PREFIX, 512), BF),
            V((NSEC, 256, PC), BF),
            V((2, 2, 256, 256), BF),
            V((NS, 2, NCH, R, 512), BF),
            V((NS, NCH, R, PC), BF),
            V((NS, NCH, R, PC), BF),
            V((NS, NCH, 8, 128), F32),
            V((NS, NCH, 8, 128), F32),
            V((NS, R, PC), BF),
            V((NS, NSEC, R, PC), BF),
            V((NEW, 512), BF),
            V((NCHUNK, 4 * R, CH), F32),
            V((NS, NSEC, R, QC), BF),
            V((NS, 2, NCH, R, QC), BF),
            V((NS, NCH, R, 512), BF),
            V((NS, NCH, R, 512), BF),
            V((NSEC, 2 * PAGE, 512), BF),
            V((NCH, NEW, QC), BF),
            V((NSEC, 2 * PAGE, 512), BF),
            dma((4,)), dma(()),
            dma((NS, 2, NCH)), dma((NS, 2, NCH)),
            dma((NS, 2)), dma((NS, 2)),
            dma((NSEC,)), dma((NSEC,)),
            dma((NSEC,)), dma((NSEC,)),
            dma((NSEC,)), dma((2, 2)),
            dma((NS, NCH)), dma((NS, NCH)),
            dma((NS, NCH)), dma((NS, NCH)),
            dma((NS,)), dma((NS, NSEC)),
            dma((NS, NSEC)), dma((NS,)),
            dma((NS, NCH)), dma((NS, NCH)),
            dma((NS, NCH)), dma((NS, NCH)),
            dma((NS, 8)), dma((NS, 8)),
            dma((NS, 8)), dma((NS, 8)),
            dma((NS, 8)), dma((NS, 8)),
            dma((NS, 2)), dma((NS, NCH)),
            dma((NSEC,)), dma((NSEC,)),
        ],
        compiler_params=pltpu.CompilerParams(
            collective_id=0, has_side_effects=True, vmem_limit_bytes=56 * 1024 * 1024
        ),
    )(
        block_input[0], w_query, w_kv, w_out, gain, kv_cache.reshape(PREFIX, 512), page_table,
        jnp.cos(angles), sine, prefix_len, page_owner[0, :, 0],
    )
    return bout[None, None], pool.reshape(1, 1, 2 * NSEC, PAGE, 512)


def solution(mesh):
    in_specs = (
        P("chain", None, "tp"),
        P(),
        P(("section", "chain"), "tp"),
        P(("section", "chain"), "tp"),
        P("tp", ("section", "chain")),
        P("section", "chain", None, None, "tp"),
        P("chain", None),
        P("chain"),
        P("chain", "section", None),
    )
    out_specs = (P("section", "chain", None, "tp"), P("section", "chain", None, None, "tp"))
    return jax.shard_map(local, mesh=mesh, in_specs=in_specs, out_specs=out_specs, check_vma=False)
```

```python
import math

import jax
import jax.numpy as jnp
import numpy as np
from jax import lax
from jax.experimental import pallas as pl
from jax.experimental.pallas import tpu as pltpu
from jax.sharding import PartitionSpec as P

HD = 128
PAGE = 16
PREFIX = 4096
NEW = 64
WIDTH = 8192
NSEC = 4
NCH = 8
NTP = 4
QC = 256
PC = 384
CH = 512
NCHUNK = PREFIX // CH
STREAMS = ((0, 32), (32, 32))
NS = len(STREAMS)
R = STREAMS[0][1]
MESH = pl.DeviceIdType.MESH
BF = jnp.bfloat16
F32 = jnp.float32


def kernel(
    hin, wq, wkv, wo, gain_in, cache, pages_in, inverse_in, owner_in, length,
    bout, pool,
    owner, gain_raw, gain, pages, inverse, cosv, sinv, bias, cachev, wq_l, wo_l, hA, part1, rbuf, ssend, srecv, sbuf2, qbuf, kvnew, S, msend, mixb, osend, ob, placed, obuf, pbuf,
    insem, csem, h0s, h0r, h2s, h2r, wqs, wqr, wks, wkr, wos, wor,
    s1, r1, ss_s, ss_r, s2, r2, s3, r3, s4, r4, s5, r5, s6, r6, s7, r7, s7f, r7f, so, ro, ps, pr,
):
    y = lax.axis_index("section")
    c = lax.axis_index("chain")
    t = lax.axis_index("tp")
    u = t // 2
    k = t % 2
    own = 2 * y + u
    twin = (y, c, 2 * u + 1 - k)

    def remote(src, dst, ssem, rsem, dev):
        return pltpu.make_async_remote_copy(
            src_ref=src, dst_ref=dst, send_sem=ssem, recv_sem=rsem, device_id=dev, device_id_type=MESH
        )

    def got(dst, rsem):
        pltpu.make_async_copy(dst, dst, rsem).wait()

    inputs = ((gain_in, gain_raw), (pages_in, pages), (inverse_in, inverse), (owner_in, owner))
    for i, (src, dst) in enumerate(inputs):
        pltpu.make_async_copy(src, dst, insem.at[i]).start()
    cache_copy = pltpu.make_async_copy(cache, cachev, csem)
    cache_copy.start()
    across = 2 * (1 - u) + k
    across_twin = 2 * (1 - u) + 1 - k

    barrier = pltpu.get_barrier_semaphore()
    for d in range(1, NCH):
        pl.semaphore_signal(barrier, inc=1, device_id=(y, (c + d) % NCH, t), device_id_type=MESH)
        pl.semaphore_signal(barrier, inc=1, device_id=(y, (c + d) % NCH, across), device_id_type=MESH)
    for dy in range(NSEC):
        for dt in range(NTP):
            if dy or dt:
                pl.semaphore_signal(
                    barrier, inc=1, device_id=((y + dy) % NSEC, c, (t + dt) % NTP), device_id_type=MESH
                )
    for g in range(NCH):
        mine = (y == c // 2) & (c == g) & (t == 2 * (c % 2) + t // 2)

        @pl.when(jnp.logical_not(mine))
        def _():
            pl.semaphore_signal(
                barrier, inc=1, device_id=(c // 2, g, 2 * (c % 2) + t // 2), device_id_type=MESH
            )

    own_dest = (c == own) & (k == u)

    pl.semaphore_wait(barrier, 2 * (NCH - 1) + NSEC * NTP - 1 + 8 - own_dest.astype(jnp.int32))

    def wq_copy(d):
        peer = (y + d) % NSEC
        src = wq.at[:, pl.ds(pl.multiple_of(peer * QC, QC), QC)]
        dst = wq_l.at[y, :, pl.ds(0, QC)]
        return lambda: remote(src, dst, wqs.at[d], wqr.at[y], (peer, c, t)), src, dst

    def wkv_copy(d):
        peer = (y + d) % NSEC
        src = wkv.at[:, pl.ds(pl.multiple_of(peer * HD, HD), HD)]
        dst = wq_l.at[y, :, pl.ds(QC, HD)]
        return lambda: remote(src, dst, wks.at[d], wkr.at[y], (peer, c, t)), src, dst

    def wo_copy(d):
        peer = (y + d) % NSEC
        src = wo.at[pl.ds(pl.multiple_of(peer * QC, QC), QC), :]
        return lambda: remote(src, wo_l.at[k, y % 2], wos.at[d], wor.at[k, y % 2], (peer, c, 2 * u + y // 2)), src

    def first_hop(st, d, far):
        peer = (c + d) % NCH
        src = hin.at[pl.ds(STREAMS[st][0], R), pl.ds(pl.multiple_of(peer * QC, QC), QC)]
        dst = hA.at[st, t // 2, c, :, pl.ds(pl.multiple_of((t % 2) * QC, QC), QC)]
        dev = (y, peer, across if far else t)
        return lambda: remote(src, dst, h0s.at[st, far, d], h0r.at[st, far, c], dev), src, dst

    def columns(st, tt):
        return hA.at[st, tt // 2, :, :, pl.ds(pl.multiple_of((tt % 2) * QC, QC), QC)]

    def second_hop(st, far):
        piece = columns(st, across if far else t)
        return remote(piece, piece, h2s.at[st, far], h2r.at[st, far], twin)

    def first_sends(st):
        _, src, dst = first_hop(st, 0, 0)
        pltpu.make_async_copy(src, dst, h0r.at[st, 0, c]).start()
        first_hop(st, 0, 1)[0]().start()
        for d in range(1, NCH):
            first_hop(st, d, 0)[0]().start()
            first_hop(st, d, 1)[0]().start()

    def second_sends(st):
        for far in range(2):
            tt = across if far else t
            for d in range(NCH):
                g = (c + NCH - d) % NCH
                got(hA.at[st, tt // 2, g, :, pl.ds(pl.multiple_of((tt % 2) * QC, QC), QC)], h0r.at[st, far, g])
            second_hop(st, far).start()

    first_sends(0)
    for d in range(1, NSEC):
        wq_copy(d)[0]().start()
        wkv_copy(d)[0]().start()
    _, src, dst = wq_copy(0)
    pltpu.make_async_copy(src, dst, wqr.at[y]).start()
    _, src, dst = wkv_copy(0)
    pltpu.make_async_copy(src, dst, wkr.at[y]).start()
    for st in range(1, NS):
        first_sends(st)
    for d in range(NSEC):
        if d:
            wo_copy(d)[0]().start()
        else:
            @pl.when(k == y // 2)
            def _():
                pltpu.make_async_copy(wo_copy(0)[1], wo_l.at[k, y % 2], wor.at[k, y % 2]).start()

            @pl.when(k != y // 2)
            def _():
                wo_copy(0)[0]().start()

    for i, (src, dst) in enumerate(inputs):
        pltpu.make_async_copy(src, dst, insem.at[i]).wait()
    gain[...] = gain_raw[...].astype(F32)
    row_pos = length[0] + lax.broadcasted_iota(jnp.int32, (NEW, HD), 0)
    angles = row_pos.astype(F32) * inverse[...]
    lane = lax.broadcasted_iota(jnp.int32, (NEW, HD), 1)
    cosv[...] = jnp.cos(angles)
    sinv[...] = jnp.where(lane < HD // 2, -1.0, 1.0) * jnp.sin(angles)
    n_pages = PREFIX // PAGE
    logical = lax.broadcasted_iota(jnp.int32, (8, n_pages), 1)
    live = jnp.clip(length[0] - logical * PAGE, 0, PAGE).astype(F32).astype(BF)
    physical = lax.broadcasted_iota(jnp.int32, (n_pages, n_pages), 0)
    named = jnp.where(pages[...] == physical, 1.0, 0.0).astype(BF)
    rows_live = lax.dot_general(live, named, (((1,), (1,)), ((), ())), preferred_element_type=F32)
    chunk_pages = CH // PAGE
    first = lax.broadcasted_iota(jnp.int32, (NCHUNK, n_pages), 0) * chunk_pages
    page = lax.broadcasted_iota(jnp.int32, (NCHUNK, n_pages), 1)
    held = jnp.where((page >= first) & (page < first + chunk_pages), rows_live, 0.0).astype(BF)
    key = lax.broadcasted_iota(jnp.int32, (n_pages, CH), 1)
    page_in = lax.rem(lax.broadcasted_iota(jnp.int32, (n_pages, CH), 0), chunk_pages)
    start = page_in * PAGE
    spread_to = jnp.where((key >= start) & (key < start + PAGE), 1.0, 0.0).astype(BF)
    count = jnp.dot(held, spread_to, preferred_element_type=F32)
    row_in = lax.rem(lax.broadcasted_iota(jnp.int32, (NCHUNK, CH), 1), PAGE).astype(F32)
    bias[...] = jnp.where(row_in + 0.5 < count, 0.0, -1e30)

    second_sends(0)
    for d in range(NSEC):
        g = (y + NSEC - d) % NSEC
        got(wq_l.at[g, :, pl.ds(0, QC)], wqr.at[g])
        got(wq_l.at[g, :, pl.ds(QC, HD)], wkr.at[g])
        halves = [gain[pl.ds((g * NCH + c) * 2 + a, 1), :] for a in range(2)]
        row = jnp.concatenate(halves, axis=1)
        column = jnp.transpose(jnp.broadcast_to(row, (128, QC)))
        for a in range(PC // 128):
            part = wq_l[g, :, a * 128:(a + 1) * 128].astype(F32) * column
            wq_l[g, :, a * 128:(a + 1) * 128] = part.astype(BF)
    for st in range(1, NS):
        second_sends(st)

    def first_wait(st):
        got(columns(st, 2 * u + 1 - k), h2r.at[st, 0])
        got(columns(st, across_twin), h2r.at[st, 1])

    def prologue_sent():
        for d in range(1, NSEC):
            wq_copy(d)[0]().wait_send()
            wkv_copy(d)[0]().wait_send()
        for st in range(NS):
            first_hop(st, 0, 1)[0]().wait_send()
            for d in range(1, NCH):
                first_hop(st, d, 0)[0]().wait_send()
                first_hop(st, d, 1)[0]().wait_send()
            for far in range(2):
                second_hop(st, far).wait_send()
        cache_copy.wait()

    def ag_copy(st, e):
        g = (own + e) % 8
        piece = hA.at[st, k, own]
        return remote(piece, piece, s7.at[st, e], r7.at[st, own], (g // 2, c, 2 * (g % 2) + k))

    def twin_copy(st, e):
        g = (own + 8 - e) % 8
        piece = hA.at[st, k, g]
        return remote(piece, piece, s7f.at[st, e], r7f.at[st, g], twin)

    def ag_send(st):
        for e in range(1, 8):
            ag_copy(st, e).start()
        twin_copy(st, 0).start()

    def ag_forward(st, s):
        @pl.when(s < NSEC - 1)
        def _():
            for e in range(1, 8):
                g = (own + 8 - e) % 8
                got(hA.at[st, k, g], r7.at[st, g])
                twin_copy(st, e).start()

    def ag_wait(st, s):
        @pl.when(s == 0)
        def _():
            first_wait(st)

        @pl.when(s > 0)
        def _():
            for e in range(8):
                g = (own + 8 - e) % 8
                got(hA.at[st, 1 - k, g], r7f.at[st, g])

    def ag_sent(st):
        for e in range(1, 8):
            ag_copy(st, e).wait_send()
        for e in range(8):
            twin_copy(st, e).wait_send()

    def p1_copy(st, d):
        peer = (c + d) % NCH
        return remote(part1.at[st, peer], rbuf.at[st, c], s1.at[st, d], r1.at[st, c], (y, peer, t))

    def ss_copy(st, d):
        peer = (c + d) % NCH
        return remote(ssend.at[st, peer], srecv.at[st, c], ss_s.at[st, d], ss_r.at[st, c], (y, peer, t))

    def project(st, s):
        ag_wait(st, s)
        total = None
        for half in range(2):
            x = hA[st, half].reshape(NCH * R, 512)
            w = wq_l[pl.ds(2 * half, 2)].reshape(512, PC)
            term = jnp.dot(x, w, preferred_element_type=F32)
            total = term if total is None else total + term
        part1[st] = total.astype(BF).reshape(NCH, R, PC)
        for d in range(1, NCH):
            p1_copy(st, d).start()
        ones = jnp.ones((8, 128), BF)
        for g in range(NCH):
            acc = None
            for half in range(2):
                wide = hA[st, half, g].astype(F32)
                square = wide * wide
                for a in range(4):
                    piece = square[:, a * 128:(a + 1) * 128]
                    acc = piece if acc is None else acc + piece
            high = acc.astype(BF)
            low = (acc - high.astype(F32)).astype(BF)
            dims = (((1,), (1,)), ((), ()))
            row = lax.dot_general(ones, high, dims, preferred_element_type=F32)
            row = row + lax.dot_general(ones, low, dims, preferred_element_type=F32)
            ssend[st, g] = jnp.concatenate([row, jnp.zeros((8, 128 - R), F32)], axis=1)
        for d in range(1, NCH):
            ss_copy(st, d).start()
        rbuf[st, c] = part1[st, c]
        srecv[st, c] = ssend[st, c]

    def p2_copy(st, s):
        return remote(sbuf2.at[st], qbuf.at[st, y], s2.at[st], r2.at[st, y], (s, c, t))

    def finish_projection(st, s):
        r0 = STREAMS[st][0]
        for d in range(1, NCH):
            g = (c + NCH - d) % NCH
            got(rbuf.at[st, g], r1.at[st, g])
            got(srecv.at[st, g], ss_r.at[st, g])
        total = rbuf[st, 0].astype(F32)
        squares = srecv[st, 0]
        for g in range(1, NCH):
            total = total + rbuf[st, g].astype(F32)
            squares = squares + srecv[st, g]
        inv = lax.rsqrt(squares * (1.0 / WIDTH) + 1e-05)[0:1, :R]
        eye = lax.broadcasted_iota(jnp.int32, (R, R), 0) == lax.broadcasted_iota(jnp.int32, (R, R), 1)
        scale = jnp.sum(jnp.where(eye, inv, 0.0), axis=1, keepdims=True)
        total = total * scale
        cs = cosv[r0:r0 + R, :]
        sn = sinv[r0:r0 + R, :]
        to_score = math.log2(math.e) / math.sqrt(HD)

        def rope(v):
            return v * cs + pltpu.roll(v, 64, 1) * sn

        q0 = rope(total[:, 0:128]) * to_score
        q1 = rope(total[:, 128:256]) * to_score
        kv = total[:, 256:384]
        even = (y % 2 == 0).astype(F32)
        kv = rope(kv) * even + kv * (1.0 - even)
        sbuf2[st] = jnp.concatenate([q0, q1, kv], axis=1).astype(BF)

        @pl.when(y == s)
        def _():
            qbuf[st, y] = sbuf2[st]

        @pl.when(y != s)
        def _():
            p2_copy(st, s).start()

        for d in range(1, NCH):
            p1_copy(st, d).wait_send()
            ss_copy(st, d).wait_send()

        @pl.when(s > 0)
        def _():
            ag_sent(st)
            bout_send(st, s - 1)

        if st == 0:
            @pl.when(s == 0)
            def _():
                prologue_sent()

    def p3_copy(st, peer):
        return remote(msend.at[st, peer], mixb.at[st, k, c], s3.at[st, peer], r3.at[st], (peer, c, t))

    def pool_copy(d):
        peer = (y + d) % NSEC
        return remote(placed.at[peer], pbuf.at[y], ps.at[d], pr.at[y], (peer, c, t))

    def attend(st):
        r0 = STREAMS[st][0]
        seen = r0 + R
        dims = (((1,), (1,)), ((), ()))
        for j in range(2):
            for g in (2 * j, 2 * j + 1):
                @pl.when(y != g)
                def _():
                    got(qbuf.at[st, g], r2.at[st, g])

                kvnew[r0:r0 + R, g * 128:(g + 1) * 128] = qbuf[st, g, :, QC:PC]
            q = jnp.concatenate(
                [qbuf[st, 2 * j + hh // 2, :, (hh % 2) * 128:(hh % 2 + 1) * 128] for hh in range(4)], axis=0
            )
            kcol = j * 256
            vcol = j * 256 + 128
            sf = lax.dot_general(q, kvnew[0:seen, kcol:kcol + 128], dims, preferred_element_type=F32)
            row = lax.broadcasted_iota(jnp.int32, (4, R, seen), 1).reshape(4 * R, seen) + r0
            col = lax.broadcasted_iota(jnp.int32, (4 * R, seen), 1)
            sf = jnp.where(col <= row, sf, -1e30)
            peak = jnp.full((4 * R, 128), -1e30, F32)
            for i in range(NCHUNK):
                keys = cachev[i * CH:(i + 1) * CH, kcol:kcol + 128]
                sc = lax.dot_general(q, keys, dims, preferred_element_type=F32) + bias[i:i + 1, :]
                S[i] = sc
                for a in range(CH // 128):
                    peak = jnp.maximum(peak, sc[:, a * 128:(a + 1) * 128])
            top = jnp.maximum(jnp.max(peak, axis=1, keepdims=True), jnp.max(sf, axis=1, keepdims=True))
            pf = jnp.exp2(sf - top)
            acc = jnp.dot(pf.astype(BF), kvnew[0:seen, vcol:vcol + 128], preferred_element_type=F32)
            den = jnp.zeros((4 * R, 128), F32)
            for i in range(NCHUNK):
                p = jnp.exp2(S[i] - top)
                for a in range(CH // 128):
                    den = den + p[:, a * 128:(a + 1) * 128]
                values = cachev[i * CH:(i + 1) * CH, vcol:vcol + 128]
                acc = acc + jnp.dot(p.astype(BF), values, preferred_element_type=F32)
            den = jnp.sum(den, axis=1, keepdims=True) + jnp.sum(pf, axis=1, keepdims=True)
            mixed = (acc / den).astype(BF)
            for hh in range(4):
                msend[st, 2 * j + hh // 2, :, (hh % 2) * 128:(hh % 2 + 1) * 128] = mixed[hh * R:(hh + 1) * R]
            for g in (2 * j, 2 * j + 1):
                @pl.when(y != g)
                def _():
                    p3_copy(st, g).start()

                @pl.when(y == g)
                def _():
                    mixb[st, k, c] = msend[st, g]

    def place_pages():
        for slot in range(2 * NSEC):
            acc = None
            for q in range(NEW // PAGE):
                rank = jnp.int32(0)
                for before in range(q):
                    rank = rank + jnp.where(owner[before] == owner[q], 1, 0)
                factor = jnp.where(owner[q] * 2 + rank == slot, 1.0, 0.0)
                term = kvnew[q * PAGE:(q + 1) * PAGE, :].astype(F32) * factor
                acc = term if acc is None else acc + term
            placed[slot // 2, (slot % 2) * PAGE:(slot % 2 + 1) * PAGE, :] = acc.astype(BF)
        for d in range(1, NSEC):
            pool_copy(d).start()
        pbuf[y] = placed[y]

    def mix(st, s):
        @pl.when(y == s)
        def _():
            attend(st)

        @pl.when(y != s)
        def _():
            p2_copy(st, s).wait_send()

    def p4_copy(st, d):
        peer = (c + d) % NCH
        piece = mixb.at[st, k, c]
        return remote(piece, piece, s4.at[st, d], r4.at[st, c], (y, peer, t))

    def p5_copy(st, d):
        g = (c + NCH - d) % NCH
        piece = mixb.at[st, k, g]
        return remote(piece, piece, s5.at[st, d], r5.at[st, g], twin)

    def spread(st, s):
        @pl.when(y != s)
        def _():
            got(mixb.at[st, k, c], r3.at[st])

        for d in range(1, NCH):
            p4_copy(st, d).start()
        p5_copy(st, 0).start()
        if st == NS - 1:
            @pl.when(y == s)
            def _():
                place_pages()

    def spread_twin(st, s):
        for d in range(1, NCH):
            g = (c + NCH - d) % NCH
            got(mixb.at[st, k, g], r4.at[st, g])
            p5_copy(st, d).start()

    def p6_copy(st, e):
        g = (own + e) % 8
        return remote(osend.at[st, g], ob.at[st, own], s6.at[st, e], r6.at[st, own], (g // 2, c, 2 * (g % 2) + k))

    def bout_copy(st, s, a):
        src = hA.at[st, k, own, :, pl.ds(a * QC, QC)]
        dst = obuf.at[c, pl.ds(STREAMS[st][0], R), :]
        return lambda: remote(src, dst, so.at[st, a], ro.at[st, c], (s, own, 2 * k + a)), src, dst

    def bout_mine(s, a):
        return (y == s) & (c == own) & (t == 2 * k + a)

    def bout_send(st, s):
        for a in range(2):
            @pl.when(bout_mine(s, a))
            def _():
                _, src, dst = bout_copy(st, s, a)
                pltpu.make_async_copy(src, dst, so.at[st, a]).start()

            @pl.when(jnp.logical_not(bout_mine(s, a)))
            def _():
                bout_copy(st, s, a)[0]().start()

    def bout_sent(st, s):
        for a in range(2):
            @pl.when(bout_mine(s, a))
            def _():
                got(bout_copy(st, s, a)[2], so.at[st, a])

            @pl.when(jnp.logical_not(bout_mine(s, a)))
            def _():
                bout_copy(st, s, a)[0]().wait_send()

    def wo_wait():
        for a in range(2):
            for b in range(2):
                got(wo_l.at[a, b], wor.at[a, b])
        for d in range(NSEC):
            if d:
                wo_copy(d)[0]().wait_send()
            else:
                @pl.when(k != y // 2)
                def _():
                    wo_copy(0)[0]().wait_send()

    def output_projection(st, s):
        for d in range(NCH):
            g = (c + NCH - d) % NCH
            got(mixb.at[st, 1 - k, g], r5.at[st, g])
        if st == 0:
            @pl.when(s == 0)
            def _():
                wo_wait()

        for b in range(2):
            total = None
            for a in range(2):
                x = mixb[st, a].reshape(NCH * R, QC)
                term = jnp.dot(x, wo_l[a, b], preferred_element_type=F32)
                total = term if total is None else total + term
            osend[st, :, :, b * QC:(b + 1) * QC] = total.astype(BF).reshape(NCH, R, QC)

        for e in range(1, 8):
            p6_copy(st, e).start()
        ob[st, own] = osend[st, own]
        for d in range(1, NCH):
            p4_copy(st, d).wait_send()
        for d in range(NCH):
            p5_copy(st, d).wait_send()

        @pl.when(y == s)
        def _():
            for g in range(NSEC):
                @pl.when(y != g)
                def _():
                    p3_copy(st, g).wait_send()

        @pl.when(s > 0)
        def _():
            bout_sent(st, s - 1)

    def residual(st, s):
        for e in range(1, 8):
            g = (own + 8 - e) % 8
            got(ob.at[st, g], r6.at[st, g])
        total = ob[st, 0].astype(F32)
        for g in range(1, 8):
            total = total + ob[st, g].astype(F32)
        hA[st, k, own] = (hA[st, k, own].astype(F32) + total).astype(BF)

        @pl.when(s < NSEC - 1)
        def _():
            ag_send(st)

        @pl.when(s == NSEC - 1)
        def _():
            bout_send(st, s)

        for e in range(1, 8):
            p6_copy(st, e).wait_send()

    def attend_and_spread(st, s):
        mix(st, s)
        spread(st, s)

    def section_step(s, carry):
        for phase in (
            project, finish_projection, attend_and_spread, spread_twin, output_projection, residual, ag_forward
        ):
            for st in range(NS):
                phase(st, s)
        return carry

    lax.fori_loop(0, NSEC, section_step, 0)

    for st in range(NS):
        bout_sent(st, NSEC - 1)
        for d in range(NCH):
            g = (c + d) % NCH
            mine = (y == c // 2) & (c == g) & (t == 2 * (c % 2) + t // 2)

            @pl.when(jnp.logical_not(mine))
            def _():
                got(obuf.at[g, pl.ds(STREAMS[st][0], R), :], ro.at[st, g])
    for d in range(1, NSEC):
        g = (y + NSEC - d) % NSEC
        got(pbuf.at[g], pr.at[g])
        pool_copy(d).wait_send()
    for g in range(NCH):
        bout[:, g * QC:(g + 1) * QC] = obuf[g]
    for g in range(NSEC):
        pool[g] = pbuf[g]


def local(block_input, norm_gain, w_query, w_kv, w_out, kv_cache, page_table, prefix_len, page_owner):
    lane = np.arange(HD, dtype=np.float64)[None, :] % (HD // 2)
    inverse = jnp.asarray((500000.0 ** (-(lane * 2.0 / HD))).astype(np.float32))

    vm = pl.BlockSpec(memory_space=pltpu.VMEM)
    hbm = pl.BlockSpec(memory_space=pltpu.HBM)
    dma = pltpu.SemaphoreType.DMA
    V = pltpu.VMEM
    bout, pool = pl.pallas_call(
        kernel,
        out_shape=(
            jax.ShapeDtypeStruct((NEW, WIDTH // NTP), BF),
            jax.ShapeDtypeStruct((NSEC, 2 * PAGE, 512), BF),
        ),
        in_specs=[hbm] * 9 + [pl.BlockSpec(memory_space=pltpu.SMEM)],
        out_specs=(vm, vm),
        scratch_shapes=[
            pltpu.SMEM((NEW // PAGE,), jnp.int32),
            V((WIDTH // 128, 128), BF),
            V((WIDTH // 128, 128), F32),
            V((1, PREFIX // PAGE), jnp.int32),
            V((1, HD), F32),
            V((NEW, HD), F32),
            V((NEW, HD), F32),
            V((NCHUNK, CH), F32),
            V((PREFIX, 512), BF),
            V((NSEC, 256, PC), BF),
            V((2, 2, 256, 256), BF),
            V((NS, 2, NCH, R, 512), BF),
            V((NS, NCH, R, PC), BF),
            V((NS, NCH, R, PC), BF),
            V((NS, NCH, 8, 128), F32),
            V((NS, NCH, 8, 128), F32),
            V((NS, R, PC), BF),
            V((NS, NSEC, R, PC), BF),
            V((NEW, 512), BF),
            V((NCHUNK, 4 * R, CH), F32),
            V((NS, NSEC, R, QC), BF),
            V((NS, 2, NCH, R, QC), BF),
            V((NS, NCH, R, 512), BF),
            V((NS, NCH, R, 512), BF),
            V((NSEC, 2 * PAGE, 512), BF),
            V((NCH, NEW, QC), BF),
            V((NSEC, 2 * PAGE, 512), BF),
            dma((4,)), dma(()),
            dma((NS, 2, NCH)), dma((NS, 2, NCH)),
            dma((NS, 2)), dma((NS, 2)),
            dma((NSEC,)), dma((NSEC,)),
            dma((NSEC,)), dma((NSEC,)),
            dma((NSEC,)), dma((2, 2)),
            dma((NS, NCH)), dma((NS, NCH)),
            dma((NS, NCH)), dma((NS, NCH)),
            dma((NS,)), dma((NS, NSEC)),
            dma((NS, NSEC)), dma((NS,)),
            dma((NS, NCH)), dma((NS, NCH)),
            dma((NS, NCH)), dma((NS, NCH)),
            dma((NS, 8)), dma((NS, 8)),
            dma((NS, 8)), dma((NS, 8)),
            dma((NS, 8)), dma((NS, 8)),
            dma((NS, 2)), dma((NS, NCH)),
            dma((NSEC,)), dma((NSEC,)),
        ],
        compiler_params=pltpu.CompilerParams(
            collective_id=0, has_side_effects=True, vmem_limit_bytes=32 * 1024 * 1024
        ),
    )(
        *[
            pltpu.with_memory_space_constraint(v, pltpu.HBM)
            for v in (
                block_input[0], w_query, w_kv, w_out, norm_gain.reshape(WIDTH // 128, 128),
                kv_cache.reshape(PREFIX, 512), page_table, inverse, page_owner[0, :, 0],
            )
        ],
        prefix_len,
    )
    return bout[None, None], pool.reshape(1, 1, 2 * NSEC, PAGE, 512)


def solution(mesh):
    in_specs = (
        P("chain", None, "tp"),
        P(),
        P(("section", "chain"), "tp"),
        P(("section", "chain"), "tp"),
        P("tp", ("section", "chain")),
        P("section", "chain", None, None, "tp"),
        P("chain", None),
        P("chain"),
        P("chain", "section", None),
    )
    out_specs = (P("section", "chain", None, "tp"), P("section", "chain", None, None, "tp"))
    return jax.shard_map(local, mesh=mesh, in_specs=in_specs, out_specs=out_specs, check_vma=False)
```

```python
import math

import jax
import jax.numpy as jnp
import numpy as np
from jax import lax
from jax.experimental import pallas as pl
from jax.experimental.pallas import tpu as pltpu
from jax.sharding import PartitionSpec as P

HD = 128
PAGE = 16
PREFIX = 4096
NEW = 64
WIDTH = 8192
NSEC = 4
NCH = 8
NTP = 4
QC = 256
PC = 384
CH = 512
NCHUNK = PREFIX // CH
STREAMS = ((0, 32), (32, 32))
NS = len(STREAMS)
R = STREAMS[0][1]
MESH = pl.DeviceIdType.MESH
BF = jnp.bfloat16
F32 = jnp.float32


NEAR_CHAIN = ((0, 0), (2, 1), (2, 0), (1, 1), (3, 1), (1, 0), (3, 0), (0, 1))
NEAR_SECTION = ((0, 0), (2, 1), (1, 1), (3, 1), (2, 0), (0, 1), (1, 0), (3, 0))


def there(i, d, steps):
    return (i // 2 + steps[d][0]) % 4 * 2 + (i % 2 + steps[d][1]) % 2


def back(i, d, steps):
    return (i // 2 + 4 - steps[d][0]) % 4 * 2 + (i % 2 + steps[d][1]) % 2


def kernel(
    hin, wq, wkv, wo, gain_in, cache, pages_in, inverse_in, owner_in, length,
    bout, pool,
    owner, gain_raw, gain, pages, inverse, cosv, sinv, bias, cachev, wq_l, wo_l, hA, part1, rbuf, ssend, srecv, sbuf2, qbuf, kvnew, S, msend, mixb, osend, ob, placed, obuf, pbuf,
    insem, csem, h0s, h0r, h2s, h2r, wqs, wqr, wks, wkr, wos, wor,
    s1, r1, ss_s, ss_r, s2, r2, s3, r3, s4, r4, s5, r5, s6, r6, s7, r7, s7f, r7f, so, ro, ps, pr,
):
    y = lax.axis_index("section")
    c = lax.axis_index("chain")
    t = lax.axis_index("tp")
    u = t // 2
    k = t % 2
    own = 2 * y + u
    twin = (y, c, 2 * u + 1 - k)

    def remote(src, dst, ssem, rsem, dev):
        return pltpu.make_async_remote_copy(
            src_ref=src, dst_ref=dst, send_sem=ssem, recv_sem=rsem, device_id=dev, device_id_type=MESH
        )

    def got(dst, rsem):
        pltpu.make_async_copy(dst, dst, rsem).wait()

    inputs = ((gain_in, gain_raw), (pages_in, pages), (inverse_in, inverse), (owner_in, owner))
    for i, (src, dst) in enumerate(inputs):
        pltpu.make_async_copy(src, dst, insem.at[i]).start()
    cache_copy = pltpu.make_async_copy(cache, cachev, csem)
    cache_copy.start()
    across = 2 * (1 - u) + k
    across_twin = 2 * (1 - u) + 1 - k

    barrier = pltpu.get_barrier_semaphore()
    for d in range(1, NCH):
        pl.semaphore_signal(barrier, inc=1, device_id=(y, there(c, d, NEAR_CHAIN), t), device_id_type=MESH)
        pl.semaphore_signal(barrier, inc=1, device_id=(y, there(c, d, NEAR_CHAIN), across), device_id_type=MESH)
    for dy in range(NSEC):
        for dt in range(NTP):
            if dy or dt:
                pl.semaphore_signal(
                    barrier, inc=1, device_id=((y + dy) % NSEC, c, (t + dt) % NTP), device_id_type=MESH
                )
    for g in range(NCH):
        mine = (y == c // 2) & (c == g) & (t == 2 * (c % 2) + t // 2)

        @pl.when(jnp.logical_not(mine))
        def _():
            pl.semaphore_signal(
                barrier, inc=1, device_id=(c // 2, g, 2 * (c % 2) + t // 2), device_id_type=MESH
            )

    own_dest = (c == own) & (k == u)

    pl.semaphore_wait(barrier, 2 * (NCH - 1) + NSEC * NTP - 1 + 8 - own_dest.astype(jnp.int32))

    def wq_copy(d):
        peer = (y + d) % NSEC
        src = wq.at[:, pl.ds(pl.multiple_of(peer * QC, QC), QC)]
        dst = wq_l.at[y, :, pl.ds(0, QC)]
        return lambda: remote(src, dst, wqs.at[d], wqr.at[y], (peer, c, t)), src, dst

    def wkv_copy(d):
        peer = (y + d) % NSEC
        src = wkv.at[:, pl.ds(pl.multiple_of(peer * HD, HD), HD)]
        dst = wq_l.at[y, :, pl.ds(QC, HD)]
        return lambda: remote(src, dst, wks.at[d], wkr.at[y], (peer, c, t)), src, dst

    def wo_copy(d):
        peer = (y + d) % NSEC
        src = wo.at[pl.ds(pl.multiple_of(peer * QC, QC), QC), :]
        return lambda: remote(src, wo_l.at[k, y % 2], wos.at[d], wor.at[k, y % 2], (peer, c, 2 * u + y // 2)), src

    def first_hop(st, d, far):
        peer = there(c, d, NEAR_CHAIN)
        src = hin.at[pl.ds(STREAMS[st][0], R), pl.ds(pl.multiple_of(peer * QC, QC), QC)]
        dst = hA.at[st, t // 2, c, :, pl.ds(pl.multiple_of((t % 2) * QC, QC), QC)]
        dev = (y, peer, across if far else t)
        return lambda: remote(src, dst, h0s.at[st, far, d], h0r.at[st, far, c], dev), src, dst

    def columns(st, tt):
        return hA.at[st, tt // 2, :, :, pl.ds(pl.multiple_of((tt % 2) * QC, QC), QC)]

    def second_hop(st, far):
        piece = columns(st, across if far else t)
        return remote(piece, piece, h2s.at[st, far], h2r.at[st, far], twin)

    def first_sends(st):
        _, src, dst = first_hop(st, 0, 0)
        pltpu.make_async_copy(src, dst, h0r.at[st, 0, c]).start()
        first_hop(st, 0, 1)[0]().start()
        for d in range(1, NCH):
            first_hop(st, d, 0)[0]().start()
            first_hop(st, d, 1)[0]().start()

    def second_sends(st):
        for far in range(2):
            tt = across if far else t
            for d in range(NCH):
                g = back(c, d, NEAR_CHAIN)
                got(hA.at[st, tt // 2, g, :, pl.ds(pl.multiple_of((tt % 2) * QC, QC), QC)], h0r.at[st, far, g])
            second_hop(st, far).start()

    first_sends(0)
    for d in range(1, NSEC):
        wq_copy(d)[0]().start()
        wkv_copy(d)[0]().start()
    _, src, dst = wq_copy(0)
    pltpu.make_async_copy(src, dst, wqr.at[y]).start()
    _, src, dst = wkv_copy(0)
    pltpu.make_async_copy(src, dst, wkr.at[y]).start()
    for st in range(1, NS):
        first_sends(st)
    for d in range(NSEC):
        if d:
            wo_copy(d)[0]().start()
        else:
            @pl.when(k == y // 2)
            def _():
                pltpu.make_async_copy(wo_copy(0)[1], wo_l.at[k, y % 2], wor.at[k, y % 2]).start()

            @pl.when(k != y // 2)
            def _():
                wo_copy(0)[0]().start()

    for i, (src, dst) in enumerate(inputs):
        pltpu.make_async_copy(src, dst, insem.at[i]).wait()
    gain[...] = gain_raw[...].astype(F32)
    row_pos = length[0] + lax.broadcasted_iota(jnp.int32, (NEW, HD), 0)
    angles = row_pos.astype(F32) * inverse[...]
    lane = lax.broadcasted_iota(jnp.int32, (NEW, HD), 1)
    cosv[...] = jnp.cos(angles)
    sinv[...] = jnp.where(lane < HD // 2, -1.0, 1.0) * jnp.sin(angles)
    n_pages = PREFIX // PAGE
    logical = lax.broadcasted_iota(jnp.int32, (8, n_pages), 1)
    live = jnp.clip(length[0] - logical * PAGE, 0, PAGE).astype(F32).astype(BF)
    physical = lax.broadcasted_iota(jnp.int32, (n_pages, n_pages), 0)
    named = jnp.where(pages[...] == physical, 1.0, 0.0).astype(BF)
    rows_live = lax.dot_general(live, named, (((1,), (1,)), ((), ())), preferred_element_type=F32)
    chunk_pages = CH // PAGE
    first = lax.broadcasted_iota(jnp.int32, (NCHUNK, n_pages), 0) * chunk_pages
    page = lax.broadcasted_iota(jnp.int32, (NCHUNK, n_pages), 1)
    held = jnp.where((page >= first) & (page < first + chunk_pages), rows_live, 0.0).astype(BF)
    key = lax.broadcasted_iota(jnp.int32, (n_pages, CH), 1)
    page_in = lax.rem(lax.broadcasted_iota(jnp.int32, (n_pages, CH), 0), chunk_pages)
    start = page_in * PAGE
    spread_to = jnp.where((key >= start) & (key < start + PAGE), 1.0, 0.0).astype(BF)
    count = jnp.dot(held, spread_to, preferred_element_type=F32)
    row_in = lax.rem(lax.broadcasted_iota(jnp.int32, (NCHUNK, CH), 1), PAGE).astype(F32)
    bias[...] = jnp.where(row_in + 0.5 < count, 0.0, -1e30)

    second_sends(0)
    for d in range(NSEC):
        g = (y + NSEC - d) % NSEC
        got(wq_l.at[g, :, pl.ds(0, QC)], wqr.at[g])
        got(wq_l.at[g, :, pl.ds(QC, HD)], wkr.at[g])
        halves = [gain[pl.ds((g * NCH + c) * 2 + a, 1), :] for a in range(2)]
        row = jnp.concatenate(halves, axis=1)
        column = jnp.transpose(jnp.broadcast_to(row, (128, QC)))
        for a in range(PC // 128):
            part = wq_l[g, :, a * 128:(a + 1) * 128].astype(F32) * column
            wq_l[g, :, a * 128:(a + 1) * 128] = part.astype(BF)
    for st in range(1, NS):
        second_sends(st)

    def first_wait(st):
        got(columns(st, 2 * u + 1 - k), h2r.at[st, 0])
        got(columns(st, across_twin), h2r.at[st, 1])

    def prologue_sent():
        for d in range(1, NSEC):
            wq_copy(d)[0]().wait_send()
            wkv_copy(d)[0]().wait_send()
        for st in range(NS):
            first_hop(st, 0, 1)[0]().wait_send()
            for d in range(1, NCH):
                first_hop(st, d, 0)[0]().wait_send()
                first_hop(st, d, 1)[0]().wait_send()
            for far in range(2):
                second_hop(st, far).wait_send()
        cache_copy.wait()

    def ag_copy(st, e):
        g = there(own, e, NEAR_SECTION)
        piece = hA.at[st, k, own]
        return remote(piece, piece, s7.at[st, e], r7.at[st, own], (g // 2, c, 2 * (g % 2) + k))

    def twin_copy(st, e):
        g = back(own, e, NEAR_SECTION)
        piece = hA.at[st, k, g]
        return remote(piece, piece, s7f.at[st, e], r7f.at[st, g], twin)

    def ag_send(st):
        for e in range(1, 8):
            ag_copy(st, e).start()
        twin_copy(st, 0).start()

    def ag_wait(st, s):
        @pl.when(s == 0)
        def _():
            first_wait(st)

        @pl.when(s > 0)
        def _():
            for e in range(1, 8):
                g = back(own, e, NEAR_SECTION)
                got(hA.at[st, k, g], r7.at[st, g])
                twin_copy(st, e).start()
            for e in range(8):
                g = back(own, e, NEAR_SECTION)
                got(hA.at[st, 1 - k, g], r7f.at[st, g])

    def ag_sent(st):
        for e in range(1, 8):
            ag_copy(st, e).wait_send()
        for e in range(8):
            twin_copy(st, e).wait_send()

    def p1_copy(st, d):
        peer = there(c, d, NEAR_CHAIN)
        return remote(part1.at[st, peer], rbuf.at[st, c], s1.at[st, d], r1.at[st, c], (y, peer, t))

    def ss_copy(st, d):
        peer = there(c, d, NEAR_CHAIN)
        return remote(ssend.at[st, peer], srecv.at[st, c], ss_s.at[st, d], ss_r.at[st, c], (y, peer, t))

    def project(st, s):
        ag_wait(st, s)
        total = None
        for half in range(2):
            x = hA[st, half].reshape(NCH * R, 512)
            w = wq_l[pl.ds(2 * half, 2)].reshape(512, PC)
            term = jnp.dot(x, w, preferred_element_type=F32)
            total = term if total is None else total + term
        part1[st] = total.astype(BF).reshape(NCH, R, PC)
        for d in range(1, NCH):
            p1_copy(st, d).start()
        ones = jnp.ones((8, 128), BF)
        for g in range(NCH):
            acc = None
            for half in range(2):
                wide = hA[st, half, g].astype(F32)
                square = wide * wide
                for a in range(4):
                    piece = square[:, a * 128:(a + 1) * 128]
                    acc = piece if acc is None else acc + piece
            high = acc.astype(BF)
            low = (acc - high.astype(F32)).astype(BF)
            dims = (((1,), (1,)), ((), ()))
            row = lax.dot_general(ones, high, dims, preferred_element_type=F32)
            row = row + lax.dot_general(ones, low, dims, preferred_element_type=F32)
            ssend[st, g] = jnp.concatenate([row, jnp.zeros((8, 128 - R), F32)], axis=1)
        for d in range(1, NCH):
            ss_copy(st, d).start()
        rbuf[st, c] = part1[st, c]
        srecv[st, c] = ssend[st, c]

    def p2_copy(st, s):
        return remote(sbuf2.at[st], qbuf.at[st, y], s2.at[st], r2.at[st, y], (s, c, t))

    def finish_projection(st, s):
        r0 = STREAMS[st][0]
        for d in range(1, NCH):
            g = back(c, d, NEAR_CHAIN)
            got(rbuf.at[st, g], r1.at[st, g])
            got(srecv.at[st, g], ss_r.at[st, g])
        total = rbuf[st, 0].astype(F32)
        squares = srecv[st, 0]
        for g in range(1, NCH):
            total = total + rbuf[st, g].astype(F32)
            squares = squares + srecv[st, g]
        inv = lax.rsqrt(squares * (1.0 / WIDTH) + 1e-05)[0:1, :R]
        eye = lax.broadcasted_iota(jnp.int32, (R, R), 0) == lax.broadcasted_iota(jnp.int32, (R, R), 1)
        scale = jnp.sum(jnp.where(eye, inv, 0.0), axis=1, keepdims=True)
        total = total * scale
        cs = cosv[r0:r0 + R, :]
        sn = sinv[r0:r0 + R, :]
        to_score = math.log2(math.e) / math.sqrt(HD)

        def rope(v):
            return v * cs + pltpu.roll(v, 64, 1) * sn

        q0 = rope(total[:, 0:128]) * to_score
        q1 = rope(total[:, 128:256]) * to_score
        kv = total[:, 256:384]
        even = (y % 2 == 0).astype(F32)
        kv = rope(kv) * even + kv * (1.0 - even)
        sbuf2[st] = jnp.concatenate([q0, q1, kv], axis=1).astype(BF)

        @pl.when(y == s)
        def _():
            qbuf[st, y] = sbuf2[st]

        @pl.when(y != s)
        def _():
            p2_copy(st, s).start()

        for d in range(1, NCH):
            p1_copy(st, d).wait_send()
            ss_copy(st, d).wait_send()

        @pl.when(s > 0)
        def _():
            ag_sent(st)
            bout_send(st, s - 1)

        if st == 0:
            @pl.when(s == 0)
            def _():
                prologue_sent()

    def p3_copy(st, peer):
        return remote(msend.at[st, peer], mixb.at[st, k, c], s3.at[st, peer], r3.at[st], (peer, c, t))

    def pool_copy(d):
        peer = (y + d) % NSEC
        return remote(placed.at[peer], pbuf.at[y], ps.at[d], pr.at[y], (peer, c, t))

    def attend(st):
        r0 = STREAMS[st][0]
        seen = r0 + R
        dims = (((1,), (1,)), ((), ()))
        for j in range(2):
            for g in (2 * j, 2 * j + 1):
                @pl.when(y != g)
                def _():
                    got(qbuf.at[st, g], r2.at[st, g])

                kvnew[r0:r0 + R, g * 128:(g + 1) * 128] = qbuf[st, g, :, QC:PC]
            q = jnp.concatenate(
                [qbuf[st, 2 * j + hh // 2, :, (hh % 2) * 128:(hh % 2 + 1) * 128] for hh in range(4)], axis=0
            )
            kcol = j * 256
            vcol = j * 256 + 128
            sf = lax.dot_general(q, kvnew[0:seen, kcol:kcol + 128], dims, preferred_element_type=F32)
            row = lax.broadcasted_iota(jnp.int32, (4, R, seen), 1).reshape(4 * R, seen) + r0
            col = lax.broadcasted_iota(jnp.int32, (4 * R, seen), 1)
            sf = jnp.where(col <= row, sf, -1e30)
            peak = jnp.full((4 * R, 128), -1e30, F32)
            for i in range(NCHUNK):
                keys = cachev[i * CH:(i + 1) * CH, kcol:kcol + 128]
                sc = lax.dot_general(q, keys, dims, preferred_element_type=F32) + bias[i:i + 1, :]
                S[i] = sc
                for a in range(CH // 128):
                    peak = jnp.maximum(peak, sc[:, a * 128:(a + 1) * 128])
            top = jnp.maximum(jnp.max(peak, axis=1, keepdims=True), jnp.max(sf, axis=1, keepdims=True))
            pf = jnp.exp2(sf - top)
            acc = jnp.dot(pf.astype(BF), kvnew[0:seen, vcol:vcol + 128], preferred_element_type=F32)
            den = jnp.zeros((4 * R, 128), F32)
            for i in range(NCHUNK):
                p = jnp.exp2(S[i] - top)
                for a in range(CH // 128):
                    den = den + p[:, a * 128:(a + 1) * 128]
                values = cachev[i * CH:(i + 1) * CH, vcol:vcol + 128]
                acc = acc + jnp.dot(p.astype(BF), values, preferred_element_type=F32)
            den = jnp.sum(den, axis=1, keepdims=True) + jnp.sum(pf, axis=1, keepdims=True)
            mixed = (acc / den).astype(BF)
            for hh in range(4):
                msend[st, 2 * j + hh // 2, :, (hh % 2) * 128:(hh % 2 + 1) * 128] = mixed[hh * R:(hh + 1) * R]
            for g in (2 * j, 2 * j + 1):
                @pl.when(y != g)
                def _():
                    p3_copy(st, g).start()

                @pl.when(y == g)
                def _():
                    mixb[st, k, c] = msend[st, g]

    def place_pages():
        for slot in range(2 * NSEC):
            acc = None
            for q in range(NEW // PAGE):
                rank = jnp.int32(0)
                for before in range(q):
                    rank = rank + jnp.where(owner[before] == owner[q], 1, 0)
                factor = jnp.where(owner[q] * 2 + rank == slot, 1.0, 0.0)
                term = kvnew[q * PAGE:(q + 1) * PAGE, :].astype(F32) * factor
                acc = term if acc is None else acc + term
            placed[slot // 2, (slot % 2) * PAGE:(slot % 2 + 1) * PAGE, :] = acc.astype(BF)
        for d in range(1, NSEC):
            pool_copy(d).start()
        pbuf[y] = placed[y]

    def mix(st, s):
        @pl.when(y == s)
        def _():
            attend(st)

        @pl.when(y != s)
        def _():
            p2_copy(st, s).wait_send()

    def p4_copy(st, d):
        peer = there(c, d, NEAR_CHAIN)
        piece = mixb.at[st, k, c]
        return remote(piece, piece, s4.at[st, d], r4.at[st, c], (y, peer, t))

    def p5_copy(st, d):
        g = back(c, d, NEAR_CHAIN)
        piece = mixb.at[st, k, g]
        return remote(piece, piece, s5.at[st, d], r5.at[st, g], twin)

    def spread(st, s):
        @pl.when(y != s)
        def _():
            got(mixb.at[st, k, c], r3.at[st])

        for d in range(1, NCH):
            p4_copy(st, d).start()
        p5_copy(st, 0).start()
        if st == NS - 1:
            @pl.when(y == s)
            def _():
                place_pages()

    def spread_twin(st, s):
        for d in range(1, NCH):
            g = back(c, d, NEAR_CHAIN)
            got(mixb.at[st, k, g], r4.at[st, g])
            p5_copy(st, d).start()

    def p6_copy(st, e):
        g = there(own, e, NEAR_SECTION)
        return remote(osend.at[st, g], ob.at[st, own], s6.at[st, e], r6.at[st, own], (g // 2, c, 2 * (g % 2) + k))

    def bout_copy(st, s, a):
        src = hA.at[st, k, own, :, pl.ds(a * QC, QC)]
        dst = obuf.at[c, pl.ds(STREAMS[st][0], R), :]
        return lambda: remote(src, dst, so.at[st, a], ro.at[st, c], (s, own, 2 * k + a)), src, dst

    def bout_mine(s, a):
        return (y == s) & (c == own) & (t == 2 * k + a)

    def bout_send(st, s):
        for a in range(2):
            @pl.when(bout_mine(s, a))
            def _():
                _, src, dst = bout_copy(st, s, a)
                pltpu.make_async_copy(src, dst, so.at[st, a]).start()

            @pl.when(jnp.logical_not(bout_mine(s, a)))
            def _():
                bout_copy(st, s, a)[0]().start()

    def bout_sent(st, s):
        for a in range(2):
            @pl.when(bout_mine(s, a))
            def _():
                got(bout_copy(st, s, a)[2], so.at[st, a])

            @pl.when(jnp.logical_not(bout_mine(s, a)))
            def _():
                bout_copy(st, s, a)[0]().wait_send()

    def wo_wait():
        for a in range(2):
            for b in range(2):
                got(wo_l.at[a, b], wor.at[a, b])
        for d in range(NSEC):
            if d:
                wo_copy(d)[0]().wait_send()
            else:
                @pl.when(k != y // 2)
                def _():
                    wo_copy(0)[0]().wait_send()

    def output_projection(st, s):
        for d in range(NCH):
            g = back(c, d, NEAR_CHAIN)
            got(mixb.at[st, 1 - k, g], r5.at[st, g])
        if st == 0:
            @pl.when(s == 0)
            def _():
                wo_wait()

        for b in range(2):
            total = None
            for a in range(2):
                x = mixb[st, a].reshape(NCH * R, QC)
                term = jnp.dot(x, wo_l[a, b], preferred_element_type=F32)
                total = term if total is None else total + term
            osend[st, :, :, b * QC:(b + 1) * QC] = total.astype(BF).reshape(NCH, R, QC)

        for e in range(1, 8):
            p6_copy(st, e).start()
        ob[st, own] = osend[st, own]
        for d in range(1, NCH):
            p4_copy(st, d).wait_send()
        for d in range(NCH):
            p5_copy(st, d).wait_send()

        @pl.when(y == s)
        def _():
            for g in range(NSEC):
                @pl.when(y != g)
                def _():
                    p3_copy(st, g).wait_send()

        @pl.when(s > 0)
        def _():
            bout_sent(st, s - 1)

    def residual(st, s):
        for e in range(1, 8):
            g = back(own, e, NEAR_SECTION)
            got(ob.at[st, g], r6.at[st, g])
        total = ob[st, 0].astype(F32)
        for g in range(1, 8):
            total = total + ob[st, g].astype(F32)
        hA[st, k, own] = (hA[st, k, own].astype(F32) + total).astype(BF)

        @pl.when(s < NSEC - 1)
        def _():
            ag_send(st)

        @pl.when(s == NSEC - 1)
        def _():
            bout_send(st, s)

        for e in range(1, 8):
            p6_copy(st, e).wait_send()

    def attend_and_spread(st, s):
        mix(st, s)
        spread(st, s)

    def twin_and_output(st, s):
        spread_twin(st, s)
        output_projection(st, s)

    def section_step(s, carry):
        for phase in (project, finish_projection, attend_and_spread, twin_and_output, residual):
            for st in range(NS):
                phase(st, s)
        return carry

    lax.fori_loop(0, NSEC, section_step, 0)

    for st in range(NS):
        bout_sent(st, NSEC - 1)
        for d in range(NCH):
            g = there(c, d, NEAR_CHAIN)
            mine = (y == c // 2) & (c == g) & (t == 2 * (c % 2) + t // 2)

            @pl.when(jnp.logical_not(mine))
            def _():
                got(obuf.at[g, pl.ds(STREAMS[st][0], R), :], ro.at[st, g])
    for d in range(1, NSEC):
        g = (y + NSEC - d) % NSEC
        got(pbuf.at[g], pr.at[g])
        pool_copy(d).wait_send()
    for g in range(NCH):
        bout[:, g * QC:(g + 1) * QC] = obuf[g]
    for g in range(NSEC):
        pool[g] = pbuf[g]


def local(block_input, norm_gain, w_query, w_kv, w_out, kv_cache, page_table, prefix_len, page_owner):
    lane = np.arange(HD, dtype=np.float64)[None, :] % (HD // 2)
    inverse = jnp.asarray((500000.0 ** (-(lane * 2.0 / HD))).astype(np.float32))

    vm = pl.BlockSpec(memory_space=pltpu.VMEM)
    hbm = pl.BlockSpec(memory_space=pltpu.HBM)
    dma = pltpu.SemaphoreType.DMA
    V = pltpu.VMEM
    bout, pool = pl.pallas_call(
        kernel,
        out_shape=(
            jax.ShapeDtypeStruct((NEW, WIDTH // NTP), BF),
            jax.ShapeDtypeStruct((NSEC, 2 * PAGE, 512), BF),
        ),
        in_specs=[hbm] * 9 + [pl.BlockSpec(memory_space=pltpu.SMEM)],
        out_specs=(vm, vm),
        scratch_shapes=[
            pltpu.SMEM((NEW // PAGE,), jnp.int32),
            V((WIDTH // 128, 128), BF),
            V((WIDTH // 128, 128), F32),
            V((1, PREFIX // PAGE), jnp.int32),
            V((1, HD), F32),
            V((NEW, HD), F32),
            V((NEW, HD), F32),
            V((NCHUNK, CH), F32),
            V((PREFIX, 512), BF),
            V((NSEC, 256, PC), BF),
            V((2, 2, 256, 256), BF),
            V((NS, 2, NCH, R, 512), BF),
            V((NS, NCH, R, PC), BF),
            V((NS, NCH, R, PC), BF),
            V((NS, NCH, 8, 128), F32),
            V((NS, NCH, 8, 128), F32),
            V((NS, R, PC), BF),
            V((NS, NSEC, R, PC), BF),
            V((NEW, 512), BF),
            V((NCHUNK, 4 * R, CH), F32),
            V((NS, NSEC, R, QC), BF),
            V((NS, 2, NCH, R, QC), BF),
            V((NS, NCH, R, 512), BF),
            V((NS, NCH, R, 512), BF),
            V((NSEC, 2 * PAGE, 512), BF),
            V((NCH, NEW, QC), BF),
            V((NSEC, 2 * PAGE, 512), BF),
            dma((4,)), dma(()),
            dma((NS, 2, NCH)), dma((NS, 2, NCH)),
            dma((NS, 2)), dma((NS, 2)),
            dma((NSEC,)), dma((NSEC,)),
            dma((NSEC,)), dma((NSEC,)),
            dma((NSEC,)), dma((2, 2)),
            dma((NS, NCH)), dma((NS, NCH)),
            dma((NS, NCH)), dma((NS, NCH)),
            dma((NS,)), dma((NS, NSEC)),
            dma((NS, NSEC)), dma((NS,)),
            dma((NS, NCH)), dma((NS, NCH)),
            dma((NS, NCH)), dma((NS, NCH)),
            dma((NS, 8)), dma((NS, 8)),
            dma((NS, 8)), dma((NS, 8)),
            dma((NS, 8)), dma((NS, 8)),
            dma((NS, 2)), dma((NS, NCH)),
            dma((NSEC,)), dma((NSEC,)),
        ],
        compiler_params=pltpu.CompilerParams(
            collective_id=0, has_side_effects=True, vmem_limit_bytes=32 * 1024 * 1024
        ),
    )(
        *[
            pltpu.with_memory_space_constraint(v, pltpu.HBM)
            for v in (
                block_input[0], w_query, w_kv, w_out, norm_gain.reshape(WIDTH // 128, 128),
                kv_cache.reshape(PREFIX, 512), page_table, inverse, page_owner[0, :, 0],
            )
        ],
        prefix_len,
    )
    return bout[None, None], pool.reshape(1, 1, 2 * NSEC, PAGE, 512)


def solution(mesh):
    in_specs = (
        P("chain", None, "tp"),
        P(),
        P(("section", "chain"), "tp"),
        P(("section", "chain"), "tp"),
        P("tp", ("section", "chain")),
        P("section", "chain", None, None, "tp"),
        P("chain", None),
        P("chain"),
        P("chain", "section", None),
    )
    out_specs = (P("section", "chain", None, "tp"), P("section", "chain", None, None, "tp"))
    return jax.shard_map(local, mesh=mesh, in_specs=in_specs, out_specs=out_specs, check_vma=False)
```

```python
import math

import jax
import jax.numpy as jnp
import numpy as np
from jax import lax
from jax.experimental import pallas as pl
from jax.experimental.pallas import tpu as pltpu
from jax.sharding import PartitionSpec as P

HD = 128
PAGE = 16
PREFIX = 4096
NEW = 64
WIDTH = 8192
NSEC = 4
NCH = 8
NTP = 4
QC = 256
PC = 384
CH = 512
NCHUNK = PREFIX // CH
STREAMS = ((0, 32), (32, 32))
NS = len(STREAMS)
R = STREAMS[0][1]
MESH = pl.DeviceIdType.MESH
BF = jnp.bfloat16
F32 = jnp.float32


NEAR_CHAIN = ((0, 0), (2, 1), (2, 0), (1, 1), (3, 1), (1, 0), (3, 0), (0, 1))
NEAR_SECTION = ((0, 0), (2, 1), (2, 0), (1, 1), (3, 1), (0, 1), (1, 0), (3, 0))


def there(i, d, steps):
    return (i // 2 + steps[d][0]) % 4 * 2 + (i % 2 + steps[d][1]) % 2


def back(i, d, steps):
    return (i // 2 + 4 - steps[d][0]) % 4 * 2 + (i % 2 + steps[d][1]) % 2


def kernel(
    hin, wq, wkv, wo, gain_in, cache, pages_in, inverse_in, owner_in, length,
    bout, pool,
    owner, gain_raw, gain, pages, inverse, cosv, sinv, bias, cachev, wq_l, wo_l, hA, part1, rbuf, ssend, srecv, sbuf2, qbuf, kvnew, S, msend, mixb, osend, ob, placed, obuf, pbuf,
    insem, csem, h0s, h0r, h2s, h2r, wqs, wqr, wks, wkr, wos, wor,
    s1, r1, ss_s, ss_r, s2, r2, s3, r3, s4, r4, s5, r5, s6, r6, s7, r7, s7f, r7f, so, ro, ps, pr,
):
    y = lax.axis_index("section")
    c = lax.axis_index("chain")
    t = lax.axis_index("tp")
    u = t // 2
    k = t % 2
    own = 2 * y + u
    twin = (y, c, 2 * u + 1 - k)

    def remote(src, dst, ssem, rsem, dev):
        return pltpu.make_async_remote_copy(
            src_ref=src, dst_ref=dst, send_sem=ssem, recv_sem=rsem, device_id=dev, device_id_type=MESH
        )

    def got(dst, rsem):
        pltpu.make_async_copy(dst, dst, rsem).wait()

    inputs = ((gain_in, gain_raw), (pages_in, pages), (inverse_in, inverse), (owner_in, owner))
    for i, (src, dst) in enumerate(inputs):
        pltpu.make_async_copy(src, dst, insem.at[i]).start()
    cache_copy = pltpu.make_async_copy(cache, cachev, csem)
    cache_copy.start()
    across = 2 * (1 - u) + k
    across_twin = 2 * (1 - u) + 1 - k

    barrier = pltpu.get_barrier_semaphore()
    for d in range(1, NCH):
        pl.semaphore_signal(barrier, inc=1, device_id=(y, there(c, d, NEAR_CHAIN), t), device_id_type=MESH)
        pl.semaphore_signal(barrier, inc=1, device_id=(y, there(c, d, NEAR_CHAIN), across), device_id_type=MESH)
    for dy in range(NSEC):
        for dt in range(NTP):
            if dy or dt:
                pl.semaphore_signal(
                    barrier, inc=1, device_id=((y + dy) % NSEC, c, (t + dt) % NTP), device_id_type=MESH
                )
    for g in range(NCH):
        mine = (y == c // 2) & (c == g) & (t == 2 * (c % 2) + t // 2)

        @pl.when(jnp.logical_not(mine))
        def _():
            pl.semaphore_signal(
                barrier, inc=1, device_id=(c // 2, g, 2 * (c % 2) + t // 2), device_id_type=MESH
            )

    own_dest = (c == own) & (k == u)

    pl.semaphore_wait(barrier, 2 * (NCH - 1) + NSEC * NTP - 1 + 8 - own_dest.astype(jnp.int32))

    def wq_copy(d):
        peer = (y + d) % NSEC
        src = wq.at[:, pl.ds(pl.multiple_of(peer * QC, QC), QC)]
        dst = wq_l.at[y, :, pl.ds(0, QC)]
        return lambda: remote(src, dst, wqs.at[d], wqr.at[y], (peer, c, t)), src, dst

    def wkv_copy(d):
        peer = (y + d) % NSEC
        src = wkv.at[:, pl.ds(pl.multiple_of(peer * HD, HD), HD)]
        dst = wq_l.at[y, :, pl.ds(QC, HD)]
        return lambda: remote(src, dst, wks.at[d], wkr.at[y], (peer, c, t)), src, dst

    def wo_copy(d):
        peer = (y + d) % NSEC
        src = wo.at[pl.ds(pl.multiple_of(peer * QC, QC), QC), :]
        return lambda: remote(src, wo_l.at[k, y % 2], wos.at[d], wor.at[k, y % 2], (peer, c, 2 * u + y // 2)), src

    def first_hop(st, d, far):
        peer = there(c, d, NEAR_CHAIN)
        src = hin.at[pl.ds(STREAMS[st][0], R), pl.ds(pl.multiple_of(peer * QC, QC), QC)]
        dst = hA.at[st, t // 2, c, :, pl.ds(pl.multiple_of((t % 2) * QC, QC), QC)]
        dev = (y, peer, across if far else t)
        return lambda: remote(src, dst, h0s.at[st, far, d], h0r.at[st, far, c], dev), src, dst

    def columns(st, tt):
        return hA.at[st, tt // 2, :, :, pl.ds(pl.multiple_of((tt % 2) * QC, QC), QC)]

    def second_hop(st, far):
        piece = columns(st, across if far else t)
        return remote(piece, piece, h2s.at[st, far], h2r.at[st, far], twin)

    def first_sends(st):
        _, src, dst = first_hop(st, 0, 0)
        pltpu.make_async_copy(src, dst, h0r.at[st, 0, c]).start()
        first_hop(st, 0, 1)[0]().start()
        for d in range(1, NCH):
            first_hop(st, d, 0)[0]().start()
            first_hop(st, d, 1)[0]().start()

    def second_sends(st):
        for far in range(2):
            tt = across if far else t
            for d in range(NCH):
                g = back(c, d, NEAR_CHAIN)
                got(hA.at[st, tt // 2, g, :, pl.ds(pl.multiple_of((tt % 2) * QC, QC), QC)], h0r.at[st, far, g])
            second_hop(st, far).start()

    first_sends(0)
    for d in (2, 1, 3):
        wq_copy(d)[0]().start()
        wkv_copy(d)[0]().start()
    _, src, dst = wq_copy(0)
    pltpu.make_async_copy(src, dst, wqr.at[y]).start()
    _, src, dst = wkv_copy(0)
    pltpu.make_async_copy(src, dst, wkr.at[y]).start()
    for st in range(1, NS):
        first_sends(st)
    for d in (2, 1, 3, 0):
        if d:
            wo_copy(d)[0]().start()
        else:
            @pl.when(k == y // 2)
            def _():
                pltpu.make_async_copy(wo_copy(0)[1], wo_l.at[k, y % 2], wor.at[k, y % 2]).start()

            @pl.when(k != y // 2)
            def _():
                wo_copy(0)[0]().start()

    for i, (src, dst) in enumerate(inputs):
        pltpu.make_async_copy(src, dst, insem.at[i]).wait()
    gain[...] = gain_raw[...].astype(F32)
    row_pos = length[0] + lax.broadcasted_iota(jnp.int32, (NEW, HD), 0)
    angles = row_pos.astype(F32) * inverse[...]
    lane = lax.broadcasted_iota(jnp.int32, (NEW, HD), 1)
    cosv[...] = jnp.cos(angles)
    sinv[...] = jnp.where(lane < HD // 2, -1.0, 1.0) * jnp.sin(angles)
    n_pages = PREFIX // PAGE
    logical = lax.broadcasted_iota(jnp.int32, (8, n_pages), 1)
    live = jnp.clip(length[0] - logical * PAGE, 0, PAGE).astype(F32).astype(BF)
    physical = lax.broadcasted_iota(jnp.int32, (n_pages, n_pages), 0)
    named = jnp.where(pages[...] == physical, 1.0, 0.0).astype(BF)
    rows_live = lax.dot_general(live, named, (((1,), (1,)), ((), ())), preferred_element_type=F32)
    chunk_pages = CH // PAGE
    first = lax.broadcasted_iota(jnp.int32, (NCHUNK, n_pages), 0) * chunk_pages
    page = lax.broadcasted_iota(jnp.int32, (NCHUNK, n_pages), 1)
    held = jnp.where((page >= first) & (page < first + chunk_pages), rows_live, 0.0).astype(BF)
    key = lax.broadcasted_iota(jnp.int32, (n_pages, CH), 1)
    page_in = lax.rem(lax.broadcasted_iota(jnp.int32, (n_pages, CH), 0), chunk_pages)
    start = page_in * PAGE
    spread_to = jnp.where((key >= start) & (key < start + PAGE), 1.0, 0.0).astype(BF)
    count = jnp.dot(held, spread_to, preferred_element_type=F32)
    row_in = lax.rem(lax.broadcasted_iota(jnp.int32, (NCHUNK, CH), 1), PAGE).astype(F32)
    bias[...] = jnp.where(row_in + 0.5 < count, 0.0, -1e30)

    second_sends(0)
    for d in range(NSEC):
        g = (y + NSEC - d) % NSEC
        got(wq_l.at[g, :, pl.ds(0, QC)], wqr.at[g])
        got(wq_l.at[g, :, pl.ds(QC, HD)], wkr.at[g])
        halves = [gain[pl.ds((g * NCH + c) * 2 + a, 1), :] for a in range(2)]
        row = jnp.concatenate(halves, axis=1)
        column = jnp.transpose(jnp.broadcast_to(row, (128, QC)))
        for a in range(PC // 128):
            part = wq_l[g, :, a * 128:(a + 1) * 128].astype(F32) * column
            wq_l[g, :, a * 128:(a + 1) * 128] = part.astype(BF)
    for st in range(1, NS):
        second_sends(st)

    def first_wait(st):
        got(columns(st, 2 * u + 1 - k), h2r.at[st, 0])
        got(columns(st, across_twin), h2r.at[st, 1])

    def prologue_sent():
        for d in range(1, NSEC):
            wq_copy(d)[0]().wait_send()
            wkv_copy(d)[0]().wait_send()
        for st in range(NS):
            first_hop(st, 0, 1)[0]().wait_send()
            for d in range(1, NCH):
                first_hop(st, d, 0)[0]().wait_send()
                first_hop(st, d, 1)[0]().wait_send()
            for far in range(2):
                second_hop(st, far).wait_send()
        cache_copy.wait()

    def ag_copy(st, e):
        g = there(own, e, NEAR_SECTION)
        piece = hA.at[st, k, own]
        return remote(piece, piece, s7.at[st, e], r7.at[st, own], (g // 2, c, 2 * (g % 2) + k))

    def twin_copy(st, e):
        g = back(own, e, NEAR_SECTION)
        piece = hA.at[st, k, g]
        return remote(piece, piece, s7f.at[st, e], r7f.at[st, g], twin)

    def ag_send(st):
        for e in range(1, 8):
            ag_copy(st, e).start()
        twin_copy(st, 0).start()

    def ag_wait(st, s):
        @pl.when(s == 0)
        def _():
            first_wait(st)

        @pl.when(s > 0)
        def _():
            for e in range(1, 8):
                g = back(own, e, NEAR_SECTION)
                got(hA.at[st, k, g], r7.at[st, g])
                twin_copy(st, e).start()
            for e in range(8):
                g = back(own, e, NEAR_SECTION)
                got(hA.at[st, 1 - k, g], r7f.at[st, g])

    def ag_sent(st):
        for e in range(1, 8):
            ag_copy(st, e).wait_send()
        for e in range(8):
            twin_copy(st, e).wait_send()

    def p1_copy(st, d):
        peer = there(c, d, NEAR_CHAIN)
        return remote(part1.at[st, peer], rbuf.at[st, c], s1.at[st, d], r1.at[st, c], (y, peer, t))

    def ss_copy(st, d):
        peer = there(c, d, NEAR_CHAIN)
        return remote(ssend.at[st, peer], srecv.at[st, c], ss_s.at[st, d], ss_r.at[st, c], (y, peer, t))

    def project(st, s):
        ag_wait(st, s)
        z = c // 2
        for group in ((2,), (1, 3, 0)):
            total = None
            for half in range(2):
                x = jnp.concatenate(
                    [hA[st, half, pl.ds((z + dz) % 4 * 2, 2)].reshape(2 * R, 512) for dz in group], axis=0
                )
                w = wq_l[pl.ds(2 * half, 2)].reshape(512, PC)
                term = jnp.dot(x, w, preferred_element_type=F32)
                total = term if total is None else total + term
            for i, dz in enumerate(group):
                piece = total[i * 2 * R:(i + 1) * 2 * R].astype(BF).reshape(2, R, PC)
                part1[st, pl.ds((z + dz) % 4 * 2, 2)] = piece
            if len(group) == 1:
                for d in (1, 2):
                    p1_copy(st, d).start()
        ones = jnp.ones((8, 128), BF)
        for g in range(NCH):
            acc = None
            for half in range(2):
                wide = hA[st, half, g].astype(F32)
                square = wide * wide
                for a in range(4):
                    piece = square[:, a * 128:(a + 1) * 128]
                    acc = piece if acc is None else acc + piece
            high = acc.astype(BF)
            low = (acc - high.astype(F32)).astype(BF)
            dims = (((1,), (1,)), ((), ()))
            row = lax.dot_general(ones, high, dims, preferred_element_type=F32)
            row = row + lax.dot_general(ones, low, dims, preferred_element_type=F32)
            ssend[st, g] = jnp.concatenate([row, jnp.zeros((8, 128 - R), F32)], axis=1)
        for d in range(1, NCH):
            if d > 2:
                p1_copy(st, d).start()
            ss_copy(st, d).start()
        rbuf[st, c] = part1[st, c]
        srecv[st, c] = ssend[st, c]

    def p2_copy(st, s):
        return remote(sbuf2.at[st], qbuf.at[st, y], s2.at[st], r2.at[st, y], (s, c, t))

    def finish_projection(st, s):
        r0 = STREAMS[st][0]
        for d in range(1, NCH):
            g = back(c, d, NEAR_CHAIN)
            got(rbuf.at[st, g], r1.at[st, g])
            got(srecv.at[st, g], ss_r.at[st, g])
        total = rbuf[st, 0].astype(F32)
        squares = srecv[st, 0]
        for g in range(1, NCH):
            total = total + rbuf[st, g].astype(F32)
            squares = squares + srecv[st, g]
        inv = lax.rsqrt(squares * (1.0 / WIDTH) + 1e-05)[0:1, :R]
        eye = lax.broadcasted_iota(jnp.int32, (R, R), 0) == lax.broadcasted_iota(jnp.int32, (R, R), 1)
        scale = jnp.sum(jnp.where(eye, inv, 0.0), axis=1, keepdims=True)
        total = total * scale
        cs = cosv[r0:r0 + R, :]
        sn = sinv[r0:r0 + R, :]
        to_score = math.log2(math.e) / math.sqrt(HD)

        def rope(v):
            return v * cs + pltpu.roll(v, 64, 1) * sn

        q0 = rope(total[:, 0:128]) * to_score
        q1 = rope(total[:, 128:256]) * to_score
        kv = total[:, 256:384]
        even = (y % 2 == 0).astype(F32)
        kv = rope(kv) * even + kv * (1.0 - even)
        sbuf2[st] = jnp.concatenate([q0, q1, kv], axis=1).astype(BF)

        @pl.when(y == s)
        def _():
            qbuf[st, y] = sbuf2[st]

        @pl.when(y != s)
        def _():
            p2_copy(st, s).start()

        for d in range(1, NCH):
            p1_copy(st, d).wait_send()
            ss_copy(st, d).wait_send()

        @pl.when(s > 0)
        def _():
            ag_sent(st)
            bout_send(st, s - 1)

        if st == 0:
            @pl.when(s == 0)
            def _():
                prologue_sent()

    def p3_copy(st, peer):
        return remote(msend.at[st, peer], mixb.at[st, k, c], s3.at[st, peer], r3.at[st], (peer, c, t))

    def pool_copy(d):
        peer = (y + d) % NSEC
        return remote(placed.at[peer], pbuf.at[y], ps.at[d], pr.at[y], (peer, c, t))

    def attend(st):
        r0 = STREAMS[st][0]
        seen = r0 + R
        dims = (((1,), (1,)), ((), ()))
        for j in range(2):
            for g in (2 * j, 2 * j + 1):
                @pl.when(y != g)
                def _():
                    got(qbuf.at[st, g], r2.at[st, g])

                kvnew[r0:r0 + R, g * 128:(g + 1) * 128] = qbuf[st, g, :, QC:PC]
            q = jnp.concatenate(
                [qbuf[st, 2 * j + hh // 2, :, (hh % 2) * 128:(hh % 2 + 1) * 128] for hh in range(4)], axis=0
            )
            kcol = j * 256
            vcol = j * 256 + 128
            sf = lax.dot_general(q, kvnew[0:seen, kcol:kcol + 128], dims, preferred_element_type=F32)
            row = lax.broadcasted_iota(jnp.int32, (4, R, seen), 1).reshape(4 * R, seen) + r0
            col = lax.broadcasted_iota(jnp.int32, (4 * R, seen), 1)
            sf = jnp.where(col <= row, sf, -1e30)
            peak = jnp.full((4 * R, 128), -1e30, F32)
            for i in range(NCHUNK):
                keys = cachev[i * CH:(i + 1) * CH, kcol:kcol + 128]
                sc = lax.dot_general(q, keys, dims, preferred_element_type=F32) + bias[i:i + 1, :]
                S[i] = sc
                for a in range(CH // 128):
                    peak = jnp.maximum(peak, sc[:, a * 128:(a + 1) * 128])
            top = jnp.maximum(jnp.max(peak, axis=1, keepdims=True), jnp.max(sf, axis=1, keepdims=True))
            pf = jnp.exp2(sf - top)
            acc = jnp.dot(pf.astype(BF), kvnew[0:seen, vcol:vcol + 128], preferred_element_type=F32)
            den = jnp.zeros((4 * R, 128), F32)
            for i in range(NCHUNK):
                p = jnp.exp2(S[i] - top)
                for a in range(CH // 128):
                    den = den + p[:, a * 128:(a + 1) * 128]
                values = cachev[i * CH:(i + 1) * CH, vcol:vcol + 128]
                acc = acc + jnp.dot(p.astype(BF), values, preferred_element_type=F32)
            den = jnp.sum(den, axis=1, keepdims=True) + jnp.sum(pf, axis=1, keepdims=True)
            mixed = (acc / den).astype(BF)
            for hh in range(4):
                msend[st, 2 * j + hh // 2, :, (hh % 2) * 128:(hh % 2 + 1) * 128] = mixed[hh * R:(hh + 1) * R]
            for g in (2 * j, 2 * j + 1):
                @pl.when(y != g)
                def _():
                    p3_copy(st, g).start()

                @pl.when(y == g)
                def _():
                    mixb[st, k, c] = msend[st, g]

    def place_pages():
        for slot in range(2 * NSEC):
            acc = None
            for q in range(NEW // PAGE):
                rank = jnp.int32(0)
                for before in range(q):
                    rank = rank + jnp.where(owner[before] == owner[q], 1, 0)
                factor = jnp.where(owner[q] * 2 + rank == slot, 1.0, 0.0)
                term = kvnew[q * PAGE:(q + 1) * PAGE, :].astype(F32) * factor
                acc = term if acc is None else acc + term
            placed[slot // 2, (slot % 2) * PAGE:(slot % 2 + 1) * PAGE, :] = acc.astype(BF)
        for d in range(1, NSEC):
            pool_copy(d).start()
        pbuf[y] = placed[y]

    def mix(st, s):
        @pl.when(y == s)
        def _():
            attend(st)

        @pl.when(y != s)
        def _():
            p2_copy(st, s).wait_send()

    def p4_copy(st, d):
        peer = there(c, d, NEAR_CHAIN)
        piece = mixb.at[st, k, c]
        return remote(piece, piece, s4.at[st, d], r4.at[st, c], (y, peer, t))

    def p5_copy(st, d):
        g = back(c, d, NEAR_CHAIN)
        piece = mixb.at[st, k, g]
        return remote(piece, piece, s5.at[st, d], r5.at[st, g], twin)

    def spread(st, s):
        @pl.when(y != s)
        def _():
            got(mixb.at[st, k, c], r3.at[st])

        for d in range(1, NCH):
            p4_copy(st, d).start()
        p5_copy(st, 0).start()
        if st == NS - 1:
            @pl.when(y == s)
            def _():
                place_pages()

    def spread_twin(st, s):
        for d in range(1, NCH):
            g = back(c, d, NEAR_CHAIN)
            got(mixb.at[st, k, g], r4.at[st, g])
            p5_copy(st, d).start()

    def p6_copy(st, e):
        g = there(own, e, NEAR_SECTION)
        return remote(osend.at[st, g], ob.at[st, own], s6.at[st, e], r6.at[st, own], (g // 2, c, 2 * (g % 2) + k))

    def bout_copy(st, s, a):
        src = hA.at[st, k, own, :, pl.ds(a * QC, QC)]
        dst = obuf.at[c, pl.ds(STREAMS[st][0], R), :]
        return lambda: remote(src, dst, so.at[st, a], ro.at[st, c], (s, own, 2 * k + a)), src, dst

    def bout_mine(s, a):
        return (y == s) & (c == own) & (t == 2 * k + a)

    def bout_send(st, s):
        for a in range(2):
            @pl.when(bout_mine(s, a))
            def _():
                _, src, dst = bout_copy(st, s, a)
                pltpu.make_async_copy(src, dst, so.at[st, a]).start()

            @pl.when(jnp.logical_not(bout_mine(s, a)))
            def _():
                bout_copy(st, s, a)[0]().start()

    def bout_sent(st, s):
        for a in range(2):
            @pl.when(bout_mine(s, a))
            def _():
                got(bout_copy(st, s, a)[2], so.at[st, a])

            @pl.when(jnp.logical_not(bout_mine(s, a)))
            def _():
                bout_copy(st, s, a)[0]().wait_send()

    def wo_wait():
        for a in range(2):
            for b in range(2):
                got(wo_l.at[a, b], wor.at[a, b])
        for d in range(NSEC):
            if d:
                wo_copy(d)[0]().wait_send()
            else:
                @pl.when(k != y // 2)
                def _():
                    wo_copy(0)[0]().wait_send()

    def output_projection(st, s):
        for d in range(NCH):
            g = back(c, d, NEAR_CHAIN)
            got(mixb.at[st, 1 - k, g], r5.at[st, g])
        if st == 0:
            @pl.when(s == 0)
            def _():
                wo_wait()

        for group in ((2,), (1, 3, 0)):
            for b in range(2):
                total = None
                for a in range(2):
                    x = jnp.concatenate(
                        [mixb[st, a, pl.ds((y + dy) % 4 * 2, 2)].reshape(2 * R, QC) for dy in group], axis=0
                    )
                    term = jnp.dot(x, wo_l[a, b], preferred_element_type=F32)
                    total = term if total is None else total + term
                for i, dy in enumerate(group):
                    piece = total[i * 2 * R:(i + 1) * 2 * R].astype(BF).reshape(2, R, QC)
                    osend[st, pl.ds((y + dy) % 4 * 2, 2), :, b * QC:(b + 1) * QC] = piece
            for e in range(1, 3) if len(group) == 1 else range(3, 8):
                p6_copy(st, e).start()
        ob[st, own] = osend[st, own]
        for d in range(1, NCH):
            p4_copy(st, d).wait_send()
        for d in range(NCH):
            p5_copy(st, d).wait_send()

        @pl.when(y == s)
        def _():
            for g in range(NSEC):
                @pl.when(y != g)
                def _():
                    p3_copy(st, g).wait_send()

        @pl.when(s > 0)
        def _():
            bout_sent(st, s - 1)

    def residual(st, s):
        for e in range(1, 8):
            g = back(own, e, NEAR_SECTION)
            got(ob.at[st, g], r6.at[st, g])
        total = ob[st, 0].astype(F32)
        for g in range(1, 8):
            total = total + ob[st, g].astype(F32)
        hA[st, k, own] = (hA[st, k, own].astype(F32) + total).astype(BF)

        @pl.when(s < NSEC - 1)
        def _():
            ag_send(st)

        @pl.when(s == NSEC - 1)
        def _():
            bout_send(st, s)

        for e in range(1, 8):
            p6_copy(st, e).wait_send()

    def attend_and_spread(st, s):
        mix(st, s)
        spread(st, s)

    def twin_and_output(st, s):
        spread_twin(st, s)
        output_projection(st, s)

    def section_step(s, carry):
        for phase in (project, finish_projection, attend_and_spread, twin_and_output, residual):
            for st in range(NS):
                phase(st, s)
        return carry

    lax.fori_loop(0, NSEC, section_step, 0)

    for st in range(NS):
        bout_sent(st, NSEC - 1)
        for d in range(NCH):
            g = there(c, d, NEAR_CHAIN)
            mine = (y == c // 2) & (c == g) & (t == 2 * (c % 2) + t // 2)

            @pl.when(jnp.logical_not(mine))
            def _():
                got(obuf.at[g, pl.ds(STREAMS[st][0], R), :], ro.at[st, g])
    for d in range(1, NSEC):
        g = (y + NSEC - d) % NSEC
        got(pbuf.at[g], pr.at[g])
        pool_copy(d).wait_send()
    for g in range(NCH):
        bout[:, g * QC:(g + 1) * QC] = obuf[g]
    for g in range(NSEC):
        pool[g] = pbuf[g]


def local(block_input, norm_gain, w_query, w_kv, w_out, kv_cache, page_table, prefix_len, page_owner):
    lane = np.arange(HD, dtype=np.float64)[None, :] % (HD // 2)
    inverse = jnp.asarray((500000.0 ** (-(lane * 2.0 / HD))).astype(np.float32))

    vm = pl.BlockSpec(memory_space=pltpu.VMEM)
    hbm = pl.BlockSpec(memory_space=pltpu.HBM)
    dma = pltpu.SemaphoreType.DMA
    V = pltpu.VMEM
    bout, pool = pl.pallas_call(
        kernel,
        out_shape=(
            jax.ShapeDtypeStruct((NEW, WIDTH // NTP), BF),
            jax.ShapeDtypeStruct((NSEC, 2 * PAGE, 512), BF),
        ),
        in_specs=[hbm] * 9 + [pl.BlockSpec(memory_space=pltpu.SMEM)],
        out_specs=(vm, vm),
        scratch_shapes=[
            pltpu.SMEM((NEW // PAGE,), jnp.int32),
            V((WIDTH // 128, 128), BF),
            V((WIDTH // 128, 128), F32),
            V((1, PREFIX // PAGE), jnp.int32),
            V((1, HD), F32),
            V((NEW, HD), F32),
            V((NEW, HD), F32),
            V((NCHUNK, CH), F32),
            V((PREFIX, 512), BF),
            V((NSEC, 256, PC), BF),
            V((2, 2, 256, 256), BF),
            V((NS, 2, NCH, R, 512), BF),
            V((NS, NCH, R, PC), BF),
            V((NS, NCH, R, PC), BF),
            V((NS, NCH, 8, 128), F32),
            V((NS, NCH, 8, 128), F32),
            V((NS, R, PC), BF),
            V((NS, NSEC, R, PC), BF),
            V((NEW, 512), BF),
            V((NCHUNK, 4 * R, CH), F32),
            V((NS, NSEC, R, QC), BF),
            V((NS, 2, NCH, R, QC), BF),
            V((NS, NCH, R, 512), BF),
            V((NS, NCH, R, 512), BF),
            V((NSEC, 2 * PAGE, 512), BF),
            V((NCH, NEW, QC), BF),
            V((NSEC, 2 * PAGE, 512), BF),
            dma((4,)), dma(()),
            dma((NS, 2, NCH)), dma((NS, 2, NCH)),
            dma((NS, 2)), dma((NS, 2)),
            dma((NSEC,)), dma((NSEC,)),
            dma((NSEC,)), dma((NSEC,)),
            dma((NSEC,)), dma((2, 2)),
            dma((NS, NCH)), dma((NS, NCH)),
            dma((NS, NCH)), dma((NS, NCH)),
            dma((NS,)), dma((NS, NSEC)),
            dma((NS, NSEC)), dma((NS,)),
            dma((NS, NCH)), dma((NS, NCH)),
            dma((NS, NCH)), dma((NS, NCH)),
            dma((NS, 8)), dma((NS, 8)),
            dma((NS, 8)), dma((NS, 8)),
            dma((NS, 8)), dma((NS, 8)),
            dma((NS, 2)), dma((NS, NCH)),
            dma((NSEC,)), dma((NSEC,)),
        ],
        compiler_params=pltpu.CompilerParams(
            collective_id=0, has_side_effects=True, vmem_limit_bytes=32 * 1024 * 1024
        ),
    )(
        *[
            pltpu.with_memory_space_constraint(v, pltpu.HBM)
            for v in (
                block_input[0], w_query, w_kv, w_out, norm_gain.reshape(WIDTH // 128, 128),
                kv_cache.reshape(PREFIX, 512), page_table, inverse, page_owner[0, :, 0],
            )
        ],
        prefix_len,
    )
    return bout[None, None], pool.reshape(1, 1, 2 * NSEC, PAGE, 512)


def solution(mesh):
    in_specs = (
        P("chain", None, "tp"),
        P(),
        P(("section", "chain"), "tp"),
        P(("section", "chain"), "tp"),
        P("tp", ("section", "chain")),
        P("section", "chain", None, None, "tp"),
        P("chain", None),
        P("chain"),
        P("chain", "section", None),
    )
    out_specs = (P("section", "chain", None, "tp"), P("section", "chain", None, None, "tp"))
    return jax.shard_map(local, mesh=mesh, in_specs=in_specs, out_specs=out_specs, check_vma=False)
```

```python
import math

import jax
import jax.numpy as jnp
import numpy as np
from jax import lax
from jax.experimental import pallas as pl
from jax.experimental.pallas import tpu as pltpu
from jax.sharding import PartitionSpec as P

HD = 128
PAGE = 16
PREFIX = 4096
NEW = 64
WIDTH = 8192
NSEC = 4
NCH = 8
NTP = 4
QC = 256
PC = 384
CH = 512
NCHUNK = PREFIX // CH
STREAMS = ((0, 32), (32, 32))
NS = len(STREAMS)
R = STREAMS[0][1]
MESH = pl.DeviceIdType.MESH
BF = jnp.bfloat16
F32 = jnp.float32


NEAR_CHAIN = ((0, 0), (2, 1), (2, 0), (1, 1), (3, 1), (1, 0), (3, 0), (0, 1))
NEAR_SECTION = ((0, 0), (2, 1), (2, 0), (1, 1), (3, 1), (0, 1), (1, 0), (3, 0))


def there(i, d, steps):
    return (i // 2 + steps[d][0]) % 4 * 2 + (i % 2 + steps[d][1]) % 2


def back(i, d, steps):
    return (i // 2 + 4 - steps[d][0]) % 4 * 2 + (i % 2 + steps[d][1]) % 2


def kernel(
    hin, wq, wkv, wo, gain_in, cache, pages_in, inverse_in, owner_in, length,
    bout, pool,
    owner, gain_raw, gain, pages, inverse, cosv, sinv, bias, cachev, wq_l, wo_l, hA, part1, rbuf, ssend, srecv, sbuf2, qbuf, kvnew, S, msend, mixb, osend, ob, placed, obuf, pbuf,
    insem, csem, h0s, h0r, h2s, h2r, wqs, wqr, wks, wkr, wos, wor,
    s1, r1, ss_s, ss_r, s2, r2, s3, r3, s4, r4, s5, r5, s6, r6, s7, r7, s7f, r7f, so, ro, ps, pr,
):
    y = lax.axis_index("section")
    c = lax.axis_index("chain")
    t = lax.axis_index("tp")
    u = t // 2
    k = t % 2
    own = 2 * y + u
    twin = (y, c, 2 * u + 1 - k)

    def remote(src, dst, ssem, rsem, dev):
        return pltpu.make_async_remote_copy(
            src_ref=src, dst_ref=dst, send_sem=ssem, recv_sem=rsem, device_id=dev, device_id_type=MESH
        )

    def got(dst, rsem):
        pltpu.make_async_copy(dst, dst, rsem).wait()

    inputs = ((gain_in, gain_raw), (pages_in, pages), (inverse_in, inverse), (owner_in, owner))
    for i, (src, dst) in enumerate(inputs):
        pltpu.make_async_copy(src, dst, insem.at[i]).start()
    cache_copy = pltpu.make_async_copy(cache, cachev, csem)
    cache_copy.start()
    across = 2 * (1 - u) + k
    across_twin = 2 * (1 - u) + 1 - k

    barrier = pltpu.get_barrier_semaphore()
    for d in range(1, NCH):
        pl.semaphore_signal(barrier, inc=1, device_id=(y, there(c, d, NEAR_CHAIN), t), device_id_type=MESH)
        pl.semaphore_signal(barrier, inc=1, device_id=(y, there(c, d, NEAR_CHAIN), across), device_id_type=MESH)
    for dy in range(NSEC):
        for dt in range(NTP):
            if dy or dt:
                pl.semaphore_signal(
                    barrier, inc=1, device_id=((y + dy) % NSEC, c, (t + dt) % NTP), device_id_type=MESH
                )
    for g in range(NCH):
        mine = (y == c // 2) & (c == g) & (t == 2 * (c % 2) + t // 2)

        @pl.when(jnp.logical_not(mine))
        def _():
            pl.semaphore_signal(
                barrier, inc=1, device_id=(c // 2, g, 2 * (c % 2) + t // 2), device_id_type=MESH
            )

    own_dest = (c == own) & (k == u)

    pl.semaphore_wait(barrier, 2 * (NCH - 1) + NSEC * NTP - 1 + 8 - own_dest.astype(jnp.int32))

    def wq_copy(d):
        peer = (y + d) % NSEC
        src = wq.at[:, pl.ds(pl.multiple_of(peer * QC, QC), QC)]
        dst = wq_l.at[y, :, pl.ds(0, QC)]
        return lambda: remote(src, dst, wqs.at[d], wqr.at[y], (peer, c, t)), src, dst

    def wkv_copy(d):
        peer = (y + d) % NSEC
        src = wkv.at[:, pl.ds(pl.multiple_of(peer * HD, HD), HD)]
        dst = wq_l.at[y, :, pl.ds(QC, HD)]
        return lambda: remote(src, dst, wks.at[d], wkr.at[y], (peer, c, t)), src, dst

    def wo_copy(d):
        peer = (y + d) % NSEC
        src = wo.at[pl.ds(pl.multiple_of(peer * QC, QC), QC), :]
        return lambda: remote(src, wo_l.at[k, y % 2], wos.at[d], wor.at[k, y % 2], (peer, c, 2 * u + y // 2)), src

    def first_hop(st, d, far):
        peer = there(c, d, NEAR_CHAIN)
        src = hin.at[pl.ds(STREAMS[st][0], R), pl.ds(pl.multiple_of(peer * QC, QC), QC)]
        dst = hA.at[st, t // 2, c, :, pl.ds(pl.multiple_of((t % 2) * QC, QC), QC)]
        dev = (y, peer, across if far else t)
        return lambda: remote(src, dst, h0s.at[st, far, d], h0r.at[st, far, c], dev), src, dst

    def columns(st, tt):
        return hA.at[st, tt // 2, :, :, pl.ds(pl.multiple_of((tt % 2) * QC, QC), QC)]

    def second_hop(st, far):
        piece = columns(st, across if far else t)
        return remote(piece, piece, h2s.at[st, far], h2r.at[st, far], twin)

    def first_sends(st):
        _, src, dst = first_hop(st, 0, 0)
        pltpu.make_async_copy(src, dst, h0r.at[st, 0, c]).start()
        first_hop(st, 0, 1)[0]().start()
        for d in range(1, NCH):
            first_hop(st, d, 0)[0]().start()
            first_hop(st, d, 1)[0]().start()

    def second_sends(st):
        for far in range(2):
            tt = across if far else t
            for d in range(NCH):
                g = back(c, d, NEAR_CHAIN)
                got(hA.at[st, tt // 2, g, :, pl.ds(pl.multiple_of((tt % 2) * QC, QC), QC)], h0r.at[st, far, g])
            second_hop(st, far).start()

    first_sends(0)
    for d in (2, 1, 3):
        wq_copy(d)[0]().start()
        wkv_copy(d)[0]().start()
    _, src, dst = wq_copy(0)
    pltpu.make_async_copy(src, dst, wqr.at[y]).start()
    _, src, dst = wkv_copy(0)
    pltpu.make_async_copy(src, dst, wkr.at[y]).start()
    for st in range(1, NS):
        first_sends(st)
    for d in (2, 1, 3, 0):
        if d:
            wo_copy(d)[0]().start()
        else:
            @pl.when(k == y // 2)
            def _():
                pltpu.make_async_copy(wo_copy(0)[1], wo_l.at[k, y % 2], wor.at[k, y % 2]).start()

            @pl.when(k != y // 2)
            def _():
                wo_copy(0)[0]().start()

    for i, (src, dst) in enumerate(inputs):
        pltpu.make_async_copy(src, dst, insem.at[i]).wait()
    gain[...] = gain_raw[...].astype(F32)
    row_pos = length[0] + lax.broadcasted_iota(jnp.int32, (NEW, HD), 0)
    angles = row_pos.astype(F32) * inverse[...]
    lane = lax.broadcasted_iota(jnp.int32, (NEW, HD), 1)
    cosv[...] = jnp.cos(angles)
    sinv[...] = jnp.where(lane < HD // 2, -1.0, 1.0) * jnp.sin(angles)
    n_pages = PREFIX // PAGE
    logical = lax.broadcasted_iota(jnp.int32, (8, n_pages), 1)
    live = jnp.clip(length[0] - logical * PAGE, 0, PAGE).astype(F32).astype(BF)
    physical = lax.broadcasted_iota(jnp.int32, (n_pages, n_pages), 0)
    named = jnp.where(pages[...] == physical, 1.0, 0.0).astype(BF)
    rows_live = lax.dot_general(live, named, (((1,), (1,)), ((), ())), preferred_element_type=F32)
    chunk_pages = CH // PAGE
    first = lax.broadcasted_iota(jnp.int32, (NCHUNK, n_pages), 0) * chunk_pages
    page = lax.broadcasted_iota(jnp.int32, (NCHUNK, n_pages), 1)
    held = jnp.where((page >= first) & (page < first + chunk_pages), rows_live, 0.0).astype(BF)
    key = lax.broadcasted_iota(jnp.int32, (n_pages, CH), 1)
    page_in = lax.rem(lax.broadcasted_iota(jnp.int32, (n_pages, CH), 0), chunk_pages)
    start = page_in * PAGE
    spread_to = jnp.where((key >= start) & (key < start + PAGE), 1.0, 0.0).astype(BF)
    count = jnp.dot(held, spread_to, preferred_element_type=F32)
    row_in = lax.rem(lax.broadcasted_iota(jnp.int32, (NCHUNK, CH), 1), PAGE).astype(F32)
    bias[...] = jnp.where(row_in + 0.5 < count, 0.0, -1e30)

    for st in range(NS):
        second_sends(st)
    for d in range(NSEC):
        g = (y + NSEC - d) % NSEC
        got(wq_l.at[g, :, pl.ds(0, QC)], wqr.at[g])
        got(wq_l.at[g, :, pl.ds(QC, HD)], wkr.at[g])
        halves = [gain[pl.ds((g * NCH + c) * 2 + a, 1), :] for a in range(2)]
        row = jnp.concatenate(halves, axis=1)
        column = jnp.transpose(jnp.broadcast_to(row, (128, QC)))
        for a in range(PC // 128):
            part = wq_l[g, :, a * 128:(a + 1) * 128].astype(F32) * column
            wq_l[g, :, a * 128:(a + 1) * 128] = part.astype(BF)
    def first_wait(st):
        got(columns(st, 2 * u + 1 - k), h2r.at[st, 0])
        got(columns(st, across_twin), h2r.at[st, 1])

    def prologue_sent():
        for d in range(1, NSEC):
            wq_copy(d)[0]().wait_send()
            wkv_copy(d)[0]().wait_send()
        for st in range(NS):
            first_hop(st, 0, 1)[0]().wait_send()
            for d in range(1, NCH):
                first_hop(st, d, 0)[0]().wait_send()
                first_hop(st, d, 1)[0]().wait_send()
            for far in range(2):
                second_hop(st, far).wait_send()
        cache_copy.wait()

    def ag_copy(st, e):
        g = there(own, e, NEAR_SECTION)
        piece = hA.at[st, k, own]
        return remote(piece, piece, s7.at[st, e], r7.at[st, own], (g // 2, c, 2 * (g % 2) + k))

    def twin_copy(st, e):
        g = back(own, e, NEAR_SECTION)
        piece = hA.at[st, k, g]
        return remote(piece, piece, s7f.at[st, e], r7f.at[st, g], twin)

    def ag_send(st):
        for e in range(1, 8):
            ag_copy(st, e).start()
        twin_copy(st, 0).start()

    def ag_forward(st, s):
        @pl.when(s == 0)
        def _():
            first_wait(st)

        @pl.when(s > 0)
        def _():
            for e in range(1, 8):
                g = back(own, e, NEAR_SECTION)
                got(hA.at[st, k, g], r7.at[st, g])
                twin_copy(st, e).start()

    def ag_wait(st, s):
        @pl.when(s > 0)
        def _():
            for e in range(8):
                g = back(own, e, NEAR_SECTION)
                got(hA.at[st, 1 - k, g], r7f.at[st, g])

    def ag_sent(st):
        for e in range(1, 8):
            ag_copy(st, e).wait_send()
        for e in range(8):
            twin_copy(st, e).wait_send()

    def p1_copy(st, d):
        peer = there(c, d, NEAR_CHAIN)
        return remote(part1.at[st, peer], rbuf.at[st, c], s1.at[st, d], r1.at[st, c], (y, peer, t))

    def ss_copy(st, d):
        peer = there(c, d, NEAR_CHAIN)
        return remote(ssend.at[st, peer], srecv.at[st, c], ss_s.at[st, d], ss_r.at[st, c], (y, peer, t))

    def rows_of(ref, st, half, base, group, width):
        parts = [ref[st, half, pl.ds((base + step) % 4 * 2, 2)].reshape(2 * R, width) for step in group]
        return jnp.concatenate(parts, axis=0)

    def squares_of(st, half):
        sums = []
        for g in range(NCH):
            wide = hA[st, half, g].astype(F32)
            square = wide * wide
            sums.append(sum(square[:, a * 128:(a + 1) * 128] for a in range(1, 4)) + square[:, :128])
        return sums

    def project(st, s):
        z = c // 2
        ag_forward(st, s)
        w_own = wq_l[pl.ds(2 * k, 2)].reshape(512, PC)
        before = jnp.dot(rows_of(hA, st, k, z, (2, 1, 3, 0), 512), w_own, preferred_element_type=F32)
        own_squares = squares_of(st, k)
        ag_wait(st, s)
        w_other = wq_l[pl.ds(2 - 2 * k, 2)].reshape(512, PC)
        done = 0
        for group in ((2,), (1, 3, 0)):
            x = rows_of(hA, st, 1 - k, z, group, 512)
            total = before[done:done + x.shape[0]] + jnp.dot(x, w_other, preferred_element_type=F32)
            done += x.shape[0]
            for i, dz in enumerate(group):
                piece = total[i * 2 * R:(i + 1) * 2 * R].astype(BF).reshape(2, R, PC)
                part1[st, pl.ds((z + dz) % 4 * 2, 2)] = piece
            if len(group) == 1:
                for d in (1, 2):
                    p1_copy(st, d).start()
        ones = jnp.ones((8, 128), BF)
        for g, (mine, other) in enumerate(zip(own_squares, squares_of(st, 1 - k))):
            acc = mine + other
            high = acc.astype(BF)
            low = (acc - high.astype(F32)).astype(BF)
            dims = (((1,), (1,)), ((), ()))
            row = lax.dot_general(ones, high, dims, preferred_element_type=F32)
            row = row + lax.dot_general(ones, low, dims, preferred_element_type=F32)
            ssend[st, g] = jnp.concatenate([row, jnp.zeros((8, 128 - R), F32)], axis=1)
        for d in range(1, NCH):
            if d > 2:
                p1_copy(st, d).start()
            ss_copy(st, d).start()
        rbuf[st, c] = part1[st, c]
        srecv[st, c] = ssend[st, c]

    def p2_copy(st, s):
        return remote(sbuf2.at[st], qbuf.at[st, y], s2.at[st], r2.at[st, y], (s, c, t))

    def finish_projection(st, s):
        r0 = STREAMS[st][0]
        for d in range(1, NCH):
            g = back(c, d, NEAR_CHAIN)
            got(rbuf.at[st, g], r1.at[st, g])
            got(srecv.at[st, g], ss_r.at[st, g])
        total = rbuf[st, 0].astype(F32)
        squares = srecv[st, 0]
        for g in range(1, NCH):
            total = total + rbuf[st, g].astype(F32)
            squares = squares + srecv[st, g]
        inv = lax.rsqrt(squares * (1.0 / WIDTH) + 1e-05)[0:1, :R]
        eye = lax.broadcasted_iota(jnp.int32, (R, R), 0) == lax.broadcasted_iota(jnp.int32, (R, R), 1)
        scale = jnp.sum(jnp.where(eye, inv, 0.0), axis=1, keepdims=True)
        total = total * scale
        cs = cosv[r0:r0 + R, :]
        sn = sinv[r0:r0 + R, :]
        to_score = math.log2(math.e) / math.sqrt(HD)

        def rope(v):
            return v * cs + pltpu.roll(v, 64, 1) * sn

        q0 = rope(total[:, 0:128]) * to_score
        q1 = rope(total[:, 128:256]) * to_score
        kv = total[:, 256:384]
        even = (y % 2 == 0).astype(F32)
        kv = rope(kv) * even + kv * (1.0 - even)
        sbuf2[st] = jnp.concatenate([q0, q1, kv], axis=1).astype(BF)

        @pl.when(y == s)
        def _():
            qbuf[st, y] = sbuf2[st]

        @pl.when(y != s)
        def _():
            p2_copy(st, s).start()

        for d in range(1, NCH):
            p1_copy(st, d).wait_send()
            ss_copy(st, d).wait_send()

        @pl.when(s > 0)
        def _():
            ag_sent(st)
            bout_send(st, s - 1)

        if st == 0:
            @pl.when(s == 0)
            def _():
                prologue_sent()

    def p3_copy(st, peer):
        return remote(msend.at[st, peer], mixb.at[st, k, c], s3.at[st, peer], r3.at[st], (peer, c, t))

    def pool_copy(d):
        peer = (y + d) % NSEC
        return remote(placed.at[peer], pbuf.at[y], ps.at[d], pr.at[y], (peer, c, t))

    def attend(st):
        r0 = STREAMS[st][0]
        seen = r0 + R
        dims = (((1,), (1,)), ((), ()))
        for j in range(2):
            for g in (2 * j, 2 * j + 1):
                @pl.when(y != g)
                def _():
                    got(qbuf.at[st, g], r2.at[st, g])

                kvnew[r0:r0 + R, g * 128:(g + 1) * 128] = qbuf[st, g, :, QC:PC]
            q = jnp.concatenate(
                [qbuf[st, 2 * j + hh // 2, :, (hh % 2) * 128:(hh % 2 + 1) * 128] for hh in range(4)], axis=0
            )
            kcol = j * 256
            vcol = j * 256 + 128
            sf = lax.dot_general(q, kvnew[0:seen, kcol:kcol + 128], dims, preferred_element_type=F32)
            row = lax.broadcasted_iota(jnp.int32, (4, R, seen), 1).reshape(4 * R, seen) + r0
            col = lax.broadcasted_iota(jnp.int32, (4 * R, seen), 1)
            sf = jnp.where(col <= row, sf, -1e30)
            peak = jnp.full((4 * R, 128), -1e30, F32)
            for i in range(NCHUNK):
                keys = cachev[i * CH:(i + 1) * CH, kcol:kcol + 128]
                sc = lax.dot_general(q, keys, dims, preferred_element_type=F32) + bias[i:i + 1, :]
                S[i] = sc
                for a in range(CH // 128):
                    peak = jnp.maximum(peak, sc[:, a * 128:(a + 1) * 128])
            top = jnp.maximum(jnp.max(peak, axis=1, keepdims=True), jnp.max(sf, axis=1, keepdims=True))
            pf = jnp.exp2(sf - top)
            acc = jnp.dot(pf.astype(BF), kvnew[0:seen, vcol:vcol + 128], preferred_element_type=F32)
            den = jnp.zeros((4 * R, 128), F32)
            for i in range(NCHUNK):
                p = jnp.exp2(S[i] - top)
                for a in range(CH // 128):
                    den = den + p[:, a * 128:(a + 1) * 128]
                values = cachev[i * CH:(i + 1) * CH, vcol:vcol + 128]
                acc = acc + jnp.dot(p.astype(BF), values, preferred_element_type=F32)
            den = jnp.sum(den, axis=1, keepdims=True) + jnp.sum(pf, axis=1, keepdims=True)
            mixed = (acc / den).astype(BF)
            for hh in range(4):
                msend[st, 2 * j + hh // 2, :, (hh % 2) * 128:(hh % 2 + 1) * 128] = mixed[hh * R:(hh + 1) * R]
            for g in (2 * j, 2 * j + 1):
                @pl.when(y != g)
                def _():
                    p3_copy(st, g).start()

                @pl.when(y == g)
                def _():
                    mixb[st, k, c] = msend[st, g]

    def place_pages():
        for slot in range(2 * NSEC):
            acc = None
            for q in range(NEW // PAGE):
                rank = jnp.int32(0)
                for before in range(q):
                    rank = rank + jnp.where(owner[before] == owner[q], 1, 0)
                factor = jnp.where(owner[q] * 2 + rank == slot, 1.0, 0.0)
                term = kvnew[q * PAGE:(q + 1) * PAGE, :].astype(F32) * factor
                acc = term if acc is None else acc + term
            placed[slot // 2, (slot % 2) * PAGE:(slot % 2 + 1) * PAGE, :] = acc.astype(BF)
        for d in range(1, NSEC):
            pool_copy(d).start()
        pbuf[y] = placed[y]

    def mix(st, s):
        @pl.when(y == s)
        def _():
            attend(st)

        @pl.when(y != s)
        def _():
            p2_copy(st, s).wait_send()

    def p4_copy(st, d):
        peer = there(c, d, NEAR_CHAIN)
        piece = mixb.at[st, k, c]
        return remote(piece, piece, s4.at[st, d], r4.at[st, c], (y, peer, t))

    def p5_copy(st, d):
        g = back(c, d, NEAR_CHAIN)
        piece = mixb.at[st, k, g]
        return remote(piece, piece, s5.at[st, d], r5.at[st, g], twin)

    def spread(st, s):
        @pl.when(y != s)
        def _():
            got(mixb.at[st, k, c], r3.at[st])

        for d in range(1, NCH):
            p4_copy(st, d).start()
        p5_copy(st, 0).start()
        if st == NS - 1:
            @pl.when(y == s)
            def _():
                place_pages()

    def spread_twin(st, s):
        for d in range(1, NCH):
            g = back(c, d, NEAR_CHAIN)
            got(mixb.at[st, k, g], r4.at[st, g])
            p5_copy(st, d).start()

    def p6_copy(st, e):
        g = there(own, e, NEAR_SECTION)
        return remote(osend.at[st, g], ob.at[st, own], s6.at[st, e], r6.at[st, own], (g // 2, c, 2 * (g % 2) + k))

    def bout_copy(st, s, a):
        src = hA.at[st, k, own, :, pl.ds(a * QC, QC)]
        dst = obuf.at[c, pl.ds(STREAMS[st][0], R), :]
        return lambda: remote(src, dst, so.at[st, a], ro.at[st, c], (s, own, 2 * k + a)), src, dst

    def bout_mine(s, a):
        return (y == s) & (c == own) & (t == 2 * k + a)

    def bout_send(st, s):
        for a in range(2):
            @pl.when(bout_mine(s, a))
            def _():
                _, src, dst = bout_copy(st, s, a)
                pltpu.make_async_copy(src, dst, so.at[st, a]).start()

            @pl.when(jnp.logical_not(bout_mine(s, a)))
            def _():
                bout_copy(st, s, a)[0]().start()

    def bout_sent(st, s):
        for a in range(2):
            @pl.when(bout_mine(s, a))
            def _():
                got(bout_copy(st, s, a)[2], so.at[st, a])

            @pl.when(jnp.logical_not(bout_mine(s, a)))
            def _():
                bout_copy(st, s, a)[0]().wait_send()

    def wo_wait():
        for a in range(2):
            for b in range(2):
                got(wo_l.at[a, b], wor.at[a, b])
        for d in range(NSEC):
            if d:
                wo_copy(d)[0]().wait_send()
            else:
                @pl.when(k != y // 2)
                def _():
                    wo_copy(0)[0]().wait_send()

    def output_projection(st, s):
        if st == 0:
            @pl.when(s == 0)
            def _():
                wo_wait()

        x_own = rows_of(mixb, st, k, y, (2, 1, 3, 0), QC)
        before = [jnp.dot(x_own, wo_l[k, b], preferred_element_type=F32) for b in range(2)]
        for d in range(NCH):
            g = back(c, d, NEAR_CHAIN)
            got(mixb.at[st, 1 - k, g], r5.at[st, g])
        done = 0
        for group in ((2,), (1, 3, 0)):
            x = rows_of(mixb, st, 1 - k, y, group, QC)
            for b in range(2):
                total = before[b][done:done + x.shape[0]]
                total = total + jnp.dot(x, wo_l[1 - k, b], preferred_element_type=F32)
                for i, dy in enumerate(group):
                    piece = total[i * 2 * R:(i + 1) * 2 * R].astype(BF).reshape(2, R, QC)
                    osend[st, pl.ds((y + dy) % 4 * 2, 2), :, b * QC:(b + 1) * QC] = piece
            done += x.shape[0]
            for e in range(1, 3) if len(group) == 1 else range(3, 8):
                p6_copy(st, e).start()
        ob[st, own] = osend[st, own]
        for d in range(1, NCH):
            p4_copy(st, d).wait_send()
        for d in range(NCH):
            p5_copy(st, d).wait_send()

        @pl.when(y == s)
        def _():
            for g in range(NSEC):
                @pl.when(y != g)
                def _():
                    p3_copy(st, g).wait_send()

        @pl.when(s > 0)
        def _():
            bout_sent(st, s - 1)

    def residual(st, s):
        for e in range(1, 8):
            g = back(own, e, NEAR_SECTION)
            got(ob.at[st, g], r6.at[st, g])
        total = ob[st, 0].astype(F32)
        for g in range(1, 8):
            total = total + ob[st, g].astype(F32)
        hA[st, k, own] = (hA[st, k, own].astype(F32) + total).astype(BF)

        @pl.when(s < NSEC - 1)
        def _():
            ag_send(st)

        @pl.when(s == NSEC - 1)
        def _():
            bout_send(st, s)

        for e in range(1, 8):
            p6_copy(st, e).wait_send()

    def attend_and_spread(st, s):
        mix(st, s)
        spread(st, s)

    def twin_and_output(st, s):
        spread_twin(st, s)
        output_projection(st, s)

    def section_step(s, carry):
        for phase in (project, finish_projection, attend_and_spread, twin_and_output, residual):
            for st in range(NS):
                phase(st, s)
        return carry

    lax.fori_loop(0, NSEC, section_step, 0)

    for st in range(NS):
        bout_sent(st, NSEC - 1)
        for d in range(NCH):
            g = there(c, d, NEAR_CHAIN)
            mine = (y == c // 2) & (c == g) & (t == 2 * (c % 2) + t // 2)

            @pl.when(jnp.logical_not(mine))
            def _():
                got(obuf.at[g, pl.ds(STREAMS[st][0], R), :], ro.at[st, g])
    for d in range(1, NSEC):
        g = (y + NSEC - d) % NSEC
        got(pbuf.at[g], pr.at[g])
        pool_copy(d).wait_send()
    for g in range(NCH):
        bout[:, g * QC:(g + 1) * QC] = obuf[g]
    for g in range(NSEC):
        pool[g] = pbuf[g]


def local(block_input, norm_gain, w_query, w_kv, w_out, kv_cache, page_table, prefix_len, page_owner):
    lane = np.arange(HD, dtype=np.float64)[None, :] % (HD // 2)
    inverse = jnp.asarray((500000.0 ** (-(lane * 2.0 / HD))).astype(np.float32))

    vm = pl.BlockSpec(memory_space=pltpu.VMEM)
    hbm = pl.BlockSpec(memory_space=pltpu.HBM)
    dma = pltpu.SemaphoreType.DMA
    V = pltpu.VMEM
    bout, pool = pl.pallas_call(
        kernel,
        out_shape=(
            jax.ShapeDtypeStruct((NEW, WIDTH // NTP), BF),
            jax.ShapeDtypeStruct((NSEC, 2 * PAGE, 512), BF),
        ),
        in_specs=[hbm] * 9 + [pl.BlockSpec(memory_space=pltpu.SMEM)],
        out_specs=(vm, vm),
        scratch_shapes=[
            pltpu.SMEM((NEW // PAGE,), jnp.int32),
            V((WIDTH // 128, 128), BF),
            V((WIDTH // 128, 128), F32),
            V((1, PREFIX // PAGE), jnp.int32),
            V((1, HD), F32),
            V((NEW, HD), F32),
            V((NEW, HD), F32),
            V((NCHUNK, CH), F32),
            V((PREFIX, 512), BF),
            V((NSEC, 256, PC), BF),
            V((2, 2, 256, 256), BF),
            V((NS, 2, NCH, R, 512), BF),
            V((NS, NCH, R, PC), BF),
            V((NS, NCH, R, PC), BF),
            V((NS, NCH, 8, 128), F32),
            V((NS, NCH, 8, 128), F32),
            V((NS, R, PC), BF),
            V((NS, NSEC, R, PC), BF),
            V((NEW, 512), BF),
            V((NCHUNK, 4 * R, CH), F32),
            V((NS, NSEC, R, QC), BF),
            V((NS, 2, NCH, R, QC), BF),
            V((NS, NCH, R, 512), BF),
            V((NS, NCH, R, 512), BF),
            V((NSEC, 2 * PAGE, 512), BF),
            V((NCH, NEW, QC), BF),
            V((NSEC, 2 * PAGE, 512), BF),
            dma((4,)), dma(()),
            dma((NS, 2, NCH)), dma((NS, 2, NCH)),
            dma((NS, 2)), dma((NS, 2)),
            dma((NSEC,)), dma((NSEC,)),
            dma((NSEC,)), dma((NSEC,)),
            dma((NSEC,)), dma((2, 2)),
            dma((NS, NCH)), dma((NS, NCH)),
            dma((NS, NCH)), dma((NS, NCH)),
            dma((NS,)), dma((NS, NSEC)),
            dma((NS, NSEC)), dma((NS,)),
            dma((NS, NCH)), dma((NS, NCH)),
            dma((NS, NCH)), dma((NS, NCH)),
            dma((NS, 8)), dma((NS, 8)),
            dma((NS, 8)), dma((NS, 8)),
            dma((NS, 8)), dma((NS, 8)),
            dma((NS, 2)), dma((NS, NCH)),
            dma((NSEC,)), dma((NSEC,)),
        ],
        compiler_params=pltpu.CompilerParams(
            collective_id=0, has_side_effects=True, vmem_limit_bytes=32 * 1024 * 1024
        ),
    )(
        *[
            pltpu.with_memory_space_constraint(v, pltpu.HBM)
            for v in (
                block_input[0], w_query, w_kv, w_out, norm_gain.reshape(WIDTH // 128, 128),
                kv_cache.reshape(PREFIX, 512), page_table, inverse, page_owner[0, :, 0],
            )
        ],
        prefix_len,
    )
    return bout[None, None], pool.reshape(1, 1, 2 * NSEC, PAGE, 512)


def solution(mesh):
    in_specs = (
        P("chain", None, "tp"),
        P(),
        P(("section", "chain"), "tp"),
        P(("section", "chain"), "tp"),
        P("tp", ("section", "chain")),
        P("section", "chain", None, None, "tp"),
        P("chain", None),
        P("chain"),
        P("chain", "section", None),
    )
    out_specs = (P("section", "chain", None, "tp"), P("section", "chain", None, None, "tp"))
    return jax.shard_map(local, mesh=mesh, in_specs=in_specs, out_specs=out_specs, check_vma=False)
```
